32 devices in a mesh: dp: 4 (over y, x), seq: 8 (over z, core).
Axes of the slice: x: 2, y: 2, z: 4, core: 2. Of those that a mesh axis runs over, the one named last changes fastest.
Arguments:
- tokens: bfloat16 [8, 1024, 768], P('dp', 'seq'), may hold values from -6 to 6
- query_weight: float32 [768, 768], P(('dp', 'seq')), may hold values from -0.21875 to 0.21875
- query_bias: float32 [768], P(('dp', 'seq')), may hold values from -3 to 3
- key_weight: float32 [768, 768], P(('dp', 'seq')), may hold values from -0.21875 to 0.21875
- value_weight: float32 [768, 768], P(('dp', 'seq')), may hold values from -0.21875 to 0.21875
- value_bias: float32 [768], P(('dp', 'seq')), may hold values from -3 to 3
- out_weight: float32 [768, 768], P(('dp', 'seq')), may hold values from -0.875 to 0.875
- out_bias: float32 [768], P(('dp', 'seq')), may hold values from -3 to 3
- first_gain: float32 [768], P(('dp', 'seq')), may hold values from 0.5 to 1.5
- attention_norm_shift: float32 [768], P(('dp', 'seq')), may hold values from -3 to 3
- expand_weight: float32 [768, 3072], P(('dp', 'seq')), may hold values from -0.21875 to 0.21875
- expand_bias: float32 [3072], P(('dp', 'seq')), may hold values from -3 to 3
- reduce_weight: float32 [3072, 768], P(('dp', 'seq')), may hold values from -0.109375 to 0.109375
- reduce_bias: float32 [768], P(('dp', 'seq')), may hold values from -3 to 3
- second_gain: float32 [768], P(('dp', 'seq')), may hold values from 0.5 to 1.5
- second_shift: float32 [768], P(('dp', 'seq')), may hold values from -3 to 3
- lengths: int32 [8, 64], P('dp'), may hold values from 0 to 896, as said below
- cotangent: bfloat16 [8, 1024, 768], P('dp', 'seq'), may hold values from -6 to 6
Outputs:
- activations: bfloat16 [8, 1024, 768], P('dp', 'seq')
- tokens_gradient: float32 [8, 1024, 768], P('dp', 'seq')
- query_weight_gradient: float32 [768, 768], P(('dp', 'seq'))
- query_bias_gradient: float32 [768], P(('dp', 'seq'))
- key_weight_gradient: float32 [768, 768], P(('dp', 'seq'))
- value_weight_gradient: float32 [768, 768], P(('dp', 'seq'))
- value_bias_gradient: float32 [768], P(('dp', 'seq'))
- out_weight_gradient: float32 [768, 768], P(('dp', 'seq'))
- output_bias_gradient: float32 [768], P(('dp', 'seq'))
- first_gain_gradient: float32 [768], P(('dp', 'seq'))
- first_shift_gradient: float32 [768], P(('dp', 'seq'))
- expand_weight_gradient: float32 [768, 3072], P(('dp', 'seq'))
- expand_bias_gradient: float32 [3072], P(('dp', 'seq'))
- reduce_weight_gradient: float32 [3072, 768], P(('dp', 'seq'))
- reduce_bias_gradient: float32 [768], P(('dp', 'seq'))
- second_gain_gradient: float32 [768], P(('dp', 'seq'))
- second_shift_gradient: float32 [768], P(('dp', 'seq'))
The draws below stay inside these ranges and needn't reach their ends.
Inputs may be any that keep to these rules, and one draw needn't show every extreme that they name: The 64 lengths of a stream sum to 1024; unused slots are 0. In each group of 2 streams that share an index of dp, one stream has an item of exactly 896 rows that starts within the first 128 rows and ends within the last 128 rows.
All inputs are finite; a program needn't handle non-finite values.
Results may differ from the reference program's by a relative error of at most 0.018.
Values may be sent and summed in bfloat16 or wider, within the bound.
No kernel may reach another device: no remote copies, remote signals or barrier semaphores. Data moves between devices by JAX's collectives and lax.ppermute only.
A program may use at most 192 MiB of HBM per device.

```python
import jax
import jax.numpy as jnp
from jax import lax

D = 768
HEADS = 12
HD = 64
FF = 3072
ROWS_DEV = 128
STREAMS_DEV = 2
STREAMS = 8
SEQ_LEN = 1024
ITEMS = 64


def draw_lengths(key, part):
    key_short, key_long, key_pick, key_head = jax.random.split(key, 4)
    longest = min(256, SEQ_LEN - ROWS_DEV)
    short = jax.random.randint(key_short, (STREAMS, ITEMS), 1, 33)
    short = jnp.minimum(short, longest)
    long_flag = jax.random.randint(key_long, (STREAMS, ITEMS), 0, 16) == 0
    raw = jnp.where(long_flag, longest, short).astype(jnp.int32)
    ends = jnp.minimum(jnp.cumsum(raw, axis=1), SEQ_LEN)
    ends = ends.at[:, ITEMS - 1].set(SEQ_LEN)
    starts = jnp.concatenate([jnp.zeros((STREAMS, 1), jnp.int32), ends[:, :ITEMS - 1]], axis=1)
    bucketed = ends - starts
    head = jax.random.randint(key_head, (STREAMS, 1), 1, ROWS_DEV)
    tail = ROWS_DEV - head
    middle = jnp.full((STREAMS, 1), SEQ_LEN - ROWS_DEV, jnp.int32)
    slots = jnp.arange(ITEMS, dtype=jnp.int32)[None, :]
    spanning = jnp.where(slots == 0, head, jnp.where(slots == 1, middle, jnp.where(slots == 2, tail, 0)))
    streams_all = jnp.arange(STREAMS, dtype=jnp.int32)
    picks = jax.random.randint(key_pick, (STREAMS // STREAMS_DEV,), 0, STREAMS_DEV)
    chosen = streams_all % STREAMS_DEV == picks[streams_all // STREAMS_DEV]
    return jnp.where(chosen[:, None], spanning, bucketed).astype(jnp.int32)


def steps_of(rng, dims, cuts, low, top_value):
    factor_of = 1.0
    for position, blocks in cuts:
        draws = jax.random.uniform(jax.random.fold_in(jax.random.fold_in(rng, 6), position), (blocks,), jnp.float32, low / len(cuts), top_value / len(cuts))
        factor_of = factor_of * jnp.repeat(jnp.exp(draws), dims[position] // blocks).reshape((-1,) + (1,) * (len(dims) - 1 - position))
    return factor_of


def normal_values(own_key, extent, scale, limit, shards=(), held_as=jnp.bfloat16):
    loudness = steps_of(own_key, extent, shards, -0.22, 0.18) if shards else 1.0
    array = jax.random.normal(own_key, extent, jnp.float32) * scale * loudness
    return jnp.minimum(jnp.maximum(array, -limit), limit).astype(held_as)


def setup_inputs(seed: int = 0) -> dict:
    splits = jax.random.split(jax.random.key(seed), 19)
    tokens = normal_values(splits[0], (STREAMS, SEQ_LEN, D), 1.0, 6.0, ((0, 4), (1, 8)))
    query_weight = normal_values(splits[1], (D, D), D ** -0.5, 0.21875, ((0, 32),), jnp.float32)
    query_bias = normal_values(splits[2], (D,), 0.5, 3.0, ((0, 32),), jnp.float32)
    key_weight = normal_values(splits[3], (D, D), D ** -0.5, 0.21875, ((0, 32),), jnp.float32)
    value_weight = normal_values(splits[4], (D, D), D ** -0.5, 0.21875, ((0, 32),), jnp.float32)
    value_bias = normal_values(splits[5], (D,), 0.5, 3.0, ((0, 32),), jnp.float32)
    out_weight = normal_values(splits[6], (D, D), (D // 16) ** -0.5, 0.875, ((0, 32),), jnp.float32)
    out_bias = normal_values(splits[7], (D,), 0.5, 3.0, ((0, 32),), jnp.float32)
    first_gain = jnp.clip(1.0 + 0.1 * jax.random.normal(splits[8], (D,), jnp.float32), 0.5, 1.5)
    attention_norm_shift = normal_values(splits[9], (D,), 0.5, 3.0, ((0, 32),), jnp.float32)
    expand_weight = normal_values(splits[10], (D, FF), D ** -0.5, 0.21875, ((0, 32),), jnp.float32)
    expand_bias = normal_values(splits[11], (FF,), 0.5, 3.0, ((0, 32),), jnp.float32)
    reduce_weight = normal_values(splits[12], (FF, D), FF ** -0.5, 0.109375, ((0, 32),), jnp.float32)
    reduce_bias = normal_values(splits[13], (D,), 0.5, 3.0, ((0, 32),), jnp.float32)
    second_gain = jnp.clip(1.0 + 0.1 * jax.random.normal(splits[14], (D,), jnp.float32), 0.5, 1.5)
    second_shift = normal_values(splits[15], (D,), 0.5, 3.0, ((0, 32),), jnp.float32)
    lengths = draw_lengths(jax.random.fold_in(splits[18], 71), 0)
    cotangent = normal_values(splits[17], (STREAMS, SEQ_LEN, D), 1.0, 6.0, ((0, 4), (1, 8)))
    return {"tokens": tokens, "query_weight": query_weight, "query_bias": query_bias, "key_weight": key_weight, "value_weight": value_weight, "value_bias": value_bias, "out_weight": out_weight, "out_bias": out_bias, "first_gain": first_gain, "attention_norm_shift": attention_norm_shift, "expand_weight": expand_weight, "expand_bias": expand_bias, "reduce_weight": reduce_weight, "reduce_bias": reduce_bias, "second_gain": second_gain, "second_shift": second_shift, "lengths": lengths, "cotangent": cotangent}


FULL_PRECISION = lax.Precision.HIGHEST
NEGATIVE = -1e+30
EPSILON = 1e-12

@jax.custom_vjp
def low(v):
    return lax.optimization_barrier(v.astype(jnp.bfloat16)).astype(jnp.float32)

@jax.custom_vjp
def low_back(v):
    return v

def low_keep(v):
    return (low(v), None)

def low_pass(kept, grad):
    return (grad,)

def back_keep(v):
    return (v, None)

def back_low(kept, grad):
    return (low(grad),)
low.defvjp(low_keep, low_pass)
low_back.defvjp(back_keep, back_low)

def layer_norm(value_rows, gain, shift):
    centre = lax.optimization_barrier(jnp.mean(value_rows, axis=-1, keepdims=True))
    centred = value_rows - centre
    spread = lax.optimization_barrier(jnp.mean(centred * centred, axis=-1, keepdims=True))
    return centred * lax.rsqrt(spread + EPSILON) * gain + shift

def project(value_rows, weight_matrix):
    return jnp.einsum('ouf,ft->out', value_rows, weight_matrix, precision=FULL_PRECISION)

def item_ids(lengths_row):
    ends = jnp.cumsum(lengths_row)
    places = jnp.arange(SEQ_LEN, dtype=jnp.int32)
    return lax.optimization_barrier(jnp.sum((ends[None, :] <= places[:, None]).astype(jnp.int32), axis=1))

def attend_stream(inputs):
    queries, keys, value_rows, identity = inputs
    width = 512 if SEQ_LEN % 512 == 0 else SEQ_LEN
    blocks = SEQ_LEN // width

    def one_block(pieces):
        query_block, block_ids = pieces
        scores = jnp.einsum('qhe,khe->hqk', query_block, keys, precision=FULL_PRECISION)
        scores = low_back(scores)
        matching = block_ids[:, None] == identity[None, :]
        scores = jnp.where(matching[None], scores, NEGATIVE)
        highest = lax.optimization_barrier(jnp.max(scores, axis=-1, keepdims=True))
        weights = jnp.exp(scores - highest)
        probs = low(weights / lax.optimization_barrier(jnp.sum(weights, axis=-1, keepdims=True)))
        return jnp.einsum('hqk,khe->qhe', probs, value_rows, precision=FULL_PRECISION)
    mixed = lax.map(jax.checkpoint(one_block), (queries.reshape(blocks, width, HEADS, HD), identity.reshape(blocks, width)))
    return mixed.reshape(SEQ_LEN, HEADS, HD)

def forward(rows, params, lengths):
    query_weight, query_bias, key_weight, value_weight, value_bias, out_weight, out_bias, first_gain, attention_norm_shift, expand_weight, expand_bias, reduce_weight, reduce_bias, second_gain, second_shift = [low(entry) for entry in params]
    queries = low_back(low((project(rows, query_weight) + query_bias) * 0.125))
    keys = low_back(low(project(rows, key_weight)))
    value_rows = low_back(low(project(rows, value_weight) + value_bias))
    stacked_shape = (STREAMS, SEQ_LEN, HEADS, HD)
    identity = jax.vmap(item_ids)(lengths)
    mixed = lax.map(attend_stream, (queries.reshape(stacked_shape), keys.reshape(stacked_shape), value_rows.reshape(stacked_shape), identity))
    attended = low_back(low(mixed.reshape(STREAMS, SEQ_LEN, D)))
    branch = low_back(project(attended, out_weight) + out_bias)
    first = layer_norm(rows + branch, first_gain, attention_norm_shift)
    expanded = low_back(project(low(first), expand_weight) + expand_bias)
    hidden = low(jax.nn.gelu(expanded, approximate=False))
    second = low_back(project(hidden, reduce_weight) + reduce_bias)
    return layer_norm(first + second, second_gain, second_shift)

def reference(tokens, query_weight, query_bias, key_weight, value_weight, value_bias, out_weight, out_bias, first_gain, attention_norm_shift, expand_weight, expand_bias, reduce_weight, reduce_bias, second_gain, second_shift, lengths, cotangent):
    params = (query_weight, query_bias, key_weight, value_weight, value_bias, out_weight, out_bias, first_gain, attention_norm_shift, expand_weight, expand_bias, reduce_weight, reduce_bias, second_gain, second_shift)
    rows = tokens.astype(jnp.float32)

    def wrapped(inner_rows, inner_params):
        return forward(inner_rows, inner_params, lengths)
    layer_result, pullback = jax.vjp(wrapped, rows, params)
    rows_grad, grads = pullback(cotangent.astype(jnp.float32))
    return (layer_result.astype(jnp.bfloat16), rows_grad, grads[0], grads[1], grads[2], grads[3], grads[4], grads[5], grads[6], grads[7], grads[8], grads[9], grads[10], grads[11], grads[12], grads[13], grads[14])
```

```python
import functools

import jax
import jax.numpy as jnp
from jax import lax
from jax.experimental import pallas as pl
from jax.experimental.pallas import tpu as pltpu
from jax.sharding import PartitionSpec as P

D = 768
HEADS = 12
HD = 64
FF = 3072
PAIR = 2 * HD
PAIRS = HEADS // 2
NEGATIVE = -1e30
EPSILON = 1e-12
BF = jnp.bfloat16
F32 = jnp.float32
VMEM_LIMIT = 56 * 1024 * 1024


def nn(left, right):
    return lax.dot_general(left, right, (((1,), (0,)), ((), ())), preferred_element_type=F32)


def nt(left, right):
    return lax.dot_general(left, right, (((1,), (1,)), ((), ())), preferred_element_type=F32)


def tn(left, right):
    return lax.dot_general(left, right, (((0,), (0,)), ((), ())), preferred_element_type=F32)


def stacked_heads(pair_rows):
    lanes = lax.broadcasted_iota(jnp.int32, pair_rows.shape, 1)
    zero = jnp.zeros_like(pair_rows)
    return jnp.concatenate(
        [jnp.where(lanes < HD, pair_rows, zero), jnp.where(lanes < HD, zero, pair_rows)], axis=0
    )


def unstacked_heads(stacked):
    rows = stacked.shape[0] // 2
    lanes = lax.broadcasted_iota(jnp.int32, (rows, PAIR), 1)
    return jnp.where(lanes < HD, stacked[:rows], stacked[rows:])


def forward_kernel(qid_ref, kid_ref, q_ref, k_ref, v_ref, out_ref, lse_ref):
    queries = stacked_heads(q_ref[0])
    rows = q_ref.shape[1]
    bias = jnp.where(qid_ref[0][:, :1] == kid_ref[0][:1, :], 0.0, NEGATIVE)
    scores = nt(queries, k_ref[0])
    scores = jnp.concatenate([scores[:rows] + bias, scores[rows:] + bias], axis=0)
    highest = jnp.max(scores, axis=-1, keepdims=True)
    weights = jnp.exp(scores - highest)
    total = jnp.sum(weights, axis=-1, keepdims=True)
    probs = (weights * (1.0 / total)).astype(BF)
    out_ref[0] = unstacked_heads(nn(probs, v_ref[0])).astype(BF)
    lse_ref[0, 0] = jnp.broadcast_to(highest + jnp.log(total), lse_ref.shape[2:])


def backward_kernel(
    qid_ref, kid_ref, q_ref, k_ref, v_ref, lse_ref, up_ref, dq_ref, dk_ref, dv_ref
):
    queries = stacked_heads(q_ref[0])
    upward = stacked_heads(up_ref[0])
    rows = q_ref.shape[1]
    bias = jnp.where(qid_ref[0][:, :1] == kid_ref[0][:1, :], 0.0, NEGATIVE)
    lse = lse_ref[0, 0][:, :1]
    scores = nt(queries, k_ref[0])
    scores = jnp.concatenate([scores[:rows] + bias, scores[rows:] + bias], axis=0)
    probs = jnp.exp(scores - lse)
    dprobs = nt(upward, v_ref[0])
    correction = jnp.sum(probs * dprobs, axis=-1, keepdims=True)
    dscores = (probs * (dprobs - correction)).astype(BF)
    dq_ref[0] = (unstacked_heads(nn(dscores, k_ref[0])).astype(BF).astype(F32) * 0.125).astype(BF)
    dk_ref[0] = tn(dscores, queries).astype(BF)
    dv_ref[0] = tn(probs.astype(BF), upward).astype(BF)


def attention_specs(rows, keys):
    return dict(
        qid=pl.BlockSpec((1, rows, 128), lambda s, p: (s, 0, 0)),
        kid=pl.BlockSpec((1, 8, keys), lambda s, p: (s, 0, 0)),
        row=pl.BlockSpec((1, rows, PAIR), lambda s, p: (s, 0, p)),
        key=pl.BlockSpec((1, keys, PAIR), lambda s, p: (s, 0, p)),
        lse=pl.BlockSpec((1, 1, 2 * rows, 128), lambda s, p: (s, p, 0, 0)),
    )


def attend(query_ids, key_ids, queries, keys, values):
    streams, rows, _ = queries.shape
    count = keys.shape[1]
    specs = attention_specs(rows, count)
    macs = streams * HEADS * rows * count * HD
    return pl.pallas_call(
        forward_kernel,
        grid=(streams, PAIRS),
        in_specs=[specs["qid"], specs["kid"], specs["row"], specs["key"], specs["key"]],
        out_specs=[specs["row"], specs["lse"]],
        out_shape=[
            jax.ShapeDtypeStruct((streams, rows, D), BF),
            jax.ShapeDtypeStruct((streams, PAIRS, 2 * rows, 128), F32),
        ],
        compiler_params=pltpu.CompilerParams(vmem_limit_bytes=VMEM_LIMIT),
        cost_estimate=pl.CostEstimate(
            flops=8 * macs, bytes_accessed=4 * streams * count * D, transcendentals=macs // HD
        ),
        name="attend",
    )(query_ids, key_ids, queries, keys, values)


def attend_back(query_ids, key_ids, queries, keys, values, lse, upward):
    streams, rows, _ = queries.shape
    count = keys.shape[1]
    specs = attention_specs(rows, count)
    macs = streams * HEADS * rows * count * HD
    return pl.pallas_call(
        backward_kernel,
        grid=(streams, PAIRS),
        in_specs=[
            specs["qid"],
            specs["kid"],
            specs["row"],
            specs["key"],
            specs["key"],
            specs["lse"],
            specs["row"],
        ],
        out_specs=[specs["row"], specs["key"], specs["key"]],
        out_shape=[
            jax.ShapeDtypeStruct((streams, rows, D), BF),
            jax.ShapeDtypeStruct((streams, count, D), BF),
            jax.ShapeDtypeStruct((streams, count, D), BF),
        ],
        compiler_params=pltpu.CompilerParams(vmem_limit_bytes=VMEM_LIMIT),
        cost_estimate=pl.CostEstimate(
            flops=20 * macs, bytes_accessed=8 * streams * count * D, transcendentals=macs // HD
        ),
        name="attend_back",
    )(query_ids, key_ids, queries, keys, values, lse, upward)


def norm_rows(value_rows):
    centre = jnp.mean(value_rows, axis=-1, keepdims=True)
    centred = value_rows - centre
    inverse = lax.rsqrt(jnp.mean(centred * centred, axis=-1, keepdims=True) + EPSILON)
    return (centred * inverse, inverse)


def norm_back(upward, normed, inverse):
    mean_up = jnp.mean(upward, axis=-1, keepdims=True)
    mean_cross = jnp.mean(upward * normed, axis=-1, keepdims=True)
    return inverse * (upward - mean_up - normed * mean_cross)


def column_sum(value_rows):
    return jnp.sum(value_rows.astype(F32), axis=0)


def item_ids(lengths, first_row, count):
    items = lengths.shape[1]
    slot = jnp.arange(items, dtype=jnp.int32)
    ends = jnp.sum(jnp.where(slot[:, None] <= slot[None, :], lengths[:, :, None], 0), axis=1)
    places = first_row + jnp.arange(count, dtype=jnp.int32)
    return jnp.sum((ends[:, None, :] <= places[None, :, None]).astype(jnp.int32), axis=2)


def body(
    tokens,
    query_weight,
    query_bias,
    key_weight,
    value_weight,
    value_bias,
    out_weight,
    out_bias,
    first_gain,
    attention_norm_shift,
    expand_weight,
    expand_bias,
    reduce_weight,
    reduce_bias,
    second_gain,
    second_shift,
    lengths,
    cotangent,
    *,
    devices,
):
    axes = ("dp", "seq")
    streams, row_count, _ = tokens.shape
    block = D // devices
    wide = FF // devices

    smalls = (
        query_bias,
        value_bias,
        out_bias,
        first_gain,
        attention_norm_shift,
        reduce_bias,
        second_gain,
        second_shift,
        expand_bias,
    )
    small = jnp.concatenate(smalls)
    small_size = small.shape[0]
    small = jnp.pad(small, (0, 8 * D - small_size)).reshape(8, D)
    early = jnp.concatenate([query_weight, key_weight, value_weight, small], axis=0).astype(BF)
    late = jnp.concatenate(
        [out_weight, reduce_weight] + [expand_weight[:, c * D : (c + 1) * D] for c in range(4)], axis=0
    ).astype(BF)

    all_tokens = lax.all_gather(tokens, "seq", axis=1, tiled=True)
    early = lax.all_gather(early, axes, axis=0)
    late = lax.all_gather(late, axes, axis=0)

    def rows_of(gathered, start, count):
        return gathered[:, start : start + count].reshape(devices * count, D)

    query_weight = rows_of(early, 0, block)
    key_weight = rows_of(early, block, block)
    value_weight = rows_of(early, 2 * block, block)
    small = early[:, 3 * block :].reshape(devices, 8 * D)[:, :small_size].astype(F32)

    def vector(index):
        return small[:, index * block : (index + 1) * block].reshape(1, D)

    query_bias, value_bias, out_bias, first_gain, attention_norm_shift, reduce_bias, second_gain, second_shift = (
        vector(i) for i in range(8)
    )
    expand_bias = small[:, 8 * block :].reshape(1, FF)
    out_weight = rows_of(late, 0, block)
    reduce_weight = rows_of(late, block, wide)
    expand_weight = (
        late[:, block + wide :].reshape(devices, 4, block, D).transpose(0, 2, 1, 3).reshape(D, FF)
    )

    stream_rows = all_tokens.shape[1]
    rows = streams * row_count
    flat_tokens = tokens.reshape(rows, D)
    flat_all = all_tokens.reshape(streams * stream_rows, D)
    key_ids = item_ids(lengths, 0, stream_rows)
    query_ids = item_ids(lengths, lax.axis_index("seq") * row_count, row_count)
    key_ids = jnp.broadcast_to(key_ids[:, None, :], (streams, 8, stream_rows))
    query_ids = jnp.broadcast_to(query_ids[:, :, None], (streams, row_count, 128))

    queries = ((nn(flat_tokens, query_weight) + query_bias) * 0.125).astype(BF)
    queries = queries.reshape(streams, row_count, D)
    keys = nn(flat_all, key_weight).astype(BF).reshape(streams, stream_rows, D)
    values = (nn(flat_all, value_weight) + value_bias).astype(BF).reshape(streams, stream_rows, D)
    attended, lse = attend(query_ids, key_ids, queries, keys, values)
    attended = attended.reshape(rows, D)

    branch = nn(attended, out_weight) + out_bias
    normed_one, inverse_one = norm_rows(flat_tokens.astype(F32) + branch)
    first = normed_one * first_gain + attention_norm_shift
    first_low = first.astype(BF)
    expanded = nn(first_low, expand_weight) + expand_bias
    hidden, gelu_pull = jax.vjp(lambda inner: jax.nn.gelu(inner, approximate=False), expanded)
    hidden = hidden.astype(BF)
    reduced = nn(hidden, reduce_weight) + reduce_bias
    normed_two, inverse_two = norm_rows(first + reduced)
    activations = (normed_two * second_gain + second_shift).astype(BF)

    upward = cotangent.reshape(rows, D).astype(F32)
    second_gain_grad = jnp.sum(upward * normed_two, axis=0)
    second_shift_grad = jnp.sum(upward, axis=0)
    residual_two_back = norm_back(upward * second_gain, normed_two, inverse_two)
    reduced_back = residual_two_back.astype(BF)
    reduce_weight_grad = tn(hidden, reduced_back).astype(BF)
    reduce_bias_grad = column_sum(reduced_back)
    expanded_back = gelu_pull(nt(reduced_back, reduce_weight))[0].astype(BF)
    expand_weight_grad = tn(first_low, expanded_back).astype(BF)
    expand_bias_grad = column_sum(expanded_back)
    wide_grads = jnp.concatenate(
        [reduce_weight_grad.reshape(devices, wide, D)]
        + [expand_weight_grad[:, c * D : (c + 1) * D].reshape(devices, block, D) for c in range(4)],
        axis=1,
    )
    wide_grads = lax.psum_scatter(wide_grads, axes, scatter_dimension=0).astype(F32)

    first_back = nt(expanded_back, expand_weight) + residual_two_back
    first_gain_grad = jnp.sum(first_back * normed_one, axis=0)
    first_shift_grad = jnp.sum(first_back, axis=0)
    residual_one_back = norm_back(first_back * first_gain, normed_one, inverse_one)
    branch_back = residual_one_back.astype(BF)
    out_weight_grad = tn(attended, branch_back).astype(BF)
    out_bias_grad = column_sum(branch_back)
    attended_back = nt(branch_back, out_weight).astype(BF).reshape(streams, row_count, D)

    query_back, key_back, value_back = attend_back(
        query_ids, key_ids, queries, keys, values, lse, attended_back
    )
    query_back = query_back.reshape(rows, D)
    key_back = key_back.reshape(streams * stream_rows, D)
    value_back = value_back.reshape(streams * stream_rows, D)
    tokens_part = (nt(key_back, key_weight) + nt(value_back, value_weight)).astype(BF)
    tokens_part = lax.psum_scatter(
        tokens_part.reshape(streams, stream_rows, D), "seq", scatter_dimension=1, tiled=True
    )
    tokens_gradient = (
        residual_one_back + nt(query_back, query_weight) + tokens_part.reshape(rows, D).astype(F32)
    ).reshape(streams, row_count, D)
    query_weight_grad = tn(flat_tokens, query_back).astype(BF)
    key_weight_grad = tn(flat_all, key_back).astype(BF)
    value_weight_grad = tn(flat_all, value_back).astype(BF)
    small_grads = [
        column_sum(query_back),
        column_sum(value_back),
        out_bias_grad,
        first_gain_grad,
        first_shift_grad,
        reduce_bias_grad,
        second_gain_grad,
        second_shift_grad,
        expand_bias_grad,
    ]
    small_grads = jnp.concatenate([g.reshape(devices, -1) for g in small_grads], axis=1).astype(BF)
    small_grads = jnp.pad(small_grads, ((0, 0), (0, 8 * D - small_size))).reshape(devices, 8, D)
    narrow_grads = jnp.concatenate(
        [
            g.reshape(devices, block, D)
            for g in (query_weight_grad, key_weight_grad, value_weight_grad, out_weight_grad)
        ]
        + [small_grads],
        axis=1,
    )
    narrow_grads = lax.psum_scatter(narrow_grads, axes, scatter_dimension=0).astype(F32)
    small = narrow_grads[4 * block :].reshape(8 * D)

    def piece(index):
        return small[index * block : (index + 1) * block]

    return (
        activations.reshape(streams, row_count, D),
        tokens_gradient,
        narrow_grads[:block],
        piece(0),
        narrow_grads[block : 2 * block],
        narrow_grads[2 * block : 3 * block],
        piece(1),
        narrow_grads[3 * block : 4 * block],
        piece(2),
        piece(3),
        piece(4),
        wide_grads[wide:].reshape(4, block, D).transpose(1, 0, 2).reshape(block, FF),
        small[8 * block : 8 * block + wide],
        wide_grads[:wide],
        piece(5),
        piece(6),
        piece(7),
    )


def solution(mesh):
    sharded = ("dp", "seq")
    matrix = P(sharded, None)
    vector = P(sharded)
    token = P("dp", "seq", None)
    params = (
        matrix,
        vector,
        matrix,
        matrix,
        vector,
        matrix,
        vector,
        vector,
        vector,
        matrix,
        vector,
        matrix,
        vector,
        vector,
        vector,
    )
    return jax.shard_map(
        functools.partial(body, devices=mesh.shape["dp"] * mesh.shape["seq"]),
        mesh=mesh,
        in_specs=(token,) + params + (P("dp", None), token),
        out_specs=(token, token) + params,
        check_vma=False,
    )
```

```python
import functools

import jax
import jax.numpy as jnp
from jax import lax
from jax.experimental.layout import Layout, with_layout_constraint
from jax.experimental import pallas as pl
from jax.experimental.pallas import tpu as pltpu
from jax.sharding import PartitionSpec as P

D = 768
HEADS = 12
HD = 64
FF = 3072
HALF = D // 2
UNITS = FF // 2
PAIR = 2 * HD
PAIRS = HALF // PAIR
NEGATIVE = -1e30
EPSILON = 1e-12
BF = jnp.bfloat16
F32 = jnp.float32
VMEM_LIMIT = 56 * 1024 * 1024


def nn(left, right):
    return lax.dot_general(left, right, (((1,), (0,)), ((), ())), preferred_element_type=F32)


def nt(left, right):
    return lax.dot_general(left, right, (((1,), (1,)), ((), ())), preferred_element_type=F32)


def tn(left, right):
    return lax.dot_general(left, right, (((0,), (0,)), ((), ())), preferred_element_type=F32)


def local_copies(place, sources, shapes, plan, name, late=()):
    def kernel(place_ref, *refs):
        ins = refs[: len(sources)]
        outs = refs[len(sources) + len(late) :]
        dp = place_ref[0]
        z = place_ref[1]
        for source, source_index, target, target_index in plan:
            outs[target][target_index(dp, z)] = ins[source][source_index(dp, z)]

    moved = 2 * sum(functools.reduce(lambda a, b: a * b, s) for s in shapes)
    return pl.pallas_call(
        kernel,
        in_specs=[pl.BlockSpec(memory_space=pltpu.SMEM)]
        + [pl.BlockSpec(memory_space=pltpu.VMEM)] * len(sources)
        + [pl.BlockSpec(memory_space=pl.ANY)] * len(late),
        out_specs=[pl.BlockSpec(memory_space=pltpu.VMEM)] * len(shapes),
        out_shape=[jax.ShapeDtypeStruct(shape, BF) for shape in shapes],
        compiler_params=pltpu.CompilerParams(vmem_limit_bytes=VMEM_LIMIT),
        cost_estimate=pl.CostEstimate(flops=0, bytes_accessed=2 * moved, transcendentals=0),
        name=name,
    )(place, *sources, *late)


def first_columns(place, weights, vectors):
    block = weights[0].shape[0]
    lanes = len(weights) * HALF + 128

    def kernel(place_ref, *refs):
        ins, (mine_ref, theirs_ref, square_ref) = refs[: len(weights) + len(vectors)], refs[-3:]
        core = place_ref[2]
        square_ref[...] = jnp.zeros_like(square_ref)
        row = 0
        for ref in ins[len(weights) :]:
            for part in range(ref.shape[0] // block):
                square_ref[row : row + 1, 0:block] = ref[part * block : (part + 1) * block].reshape(1, block)
                row += 1
        columns = square_ref[...].T[:block].astype(BF)
        for out, side in ((mine_ref, core), (theirs_ref, 1 - core)):
            for i in range(len(weights)):
                picked = ins[i][:, pl.ds(pl.multiple_of(side * HALF, 128), HALF)]
                out[:, i * HALF : (i + 1) * HALF] = picked.astype(BF)
            out[:, len(weights) * HALF :] = columns

    shape = jax.ShapeDtypeStruct((block, lanes), BF)
    return pl.pallas_call(
        kernel,
        in_specs=[pl.BlockSpec(memory_space=pltpu.SMEM)]
        + [pl.BlockSpec(memory_space=pltpu.VMEM)] * (len(weights) + len(vectors)),
        out_specs=[pl.BlockSpec(memory_space=pltpu.VMEM)] * 2,
        out_shape=[shape, shape],
        scratch_shapes=[pltpu.VMEM((128, 128), F32)],
        name="first_columns",
    )(place, *weights, *vectors)


def at_lanes(start, count):
    return pl.ds(start, count)


def core_swap(value, seq):
    return lax.ppermute(value, "seq", [(i, i ^ 1) for i in range(seq)])


def z_move(value, step, seq):
    return lax.ppermute(value, "seq", [(i, i ^ (2 * step)) for i in range(seq)])


def dp_move(value, step, dps):
    return lax.ppermute(value, "dp", [(i, i ^ step) for i in range(dps)])


def gather_chips(value, dps, seq):
    along = jnp.stack([value] + [z_move(value, j, seq) for j in range(1, seq // 2)])
    return [along] + [dp_move(along, k, dps) for k in range(1, dps)]


def along_dp(packs, dps):
    return [packs[0]] + [dp_move(packs[k], k, dps) for k in range(1, dps)]


def add_along_z(came, seq):
    def total(j):
        return functools.reduce(jnp.add, [c[j].astype(F32) for c in came])

    moved = [z_move(total(j).astype(BF), j, seq) for j in range(1, seq // 2)]
    return functools.reduce(jnp.add, [m.astype(F32) for m in moved], total(0))


def stacked_heads(pair_rows):
    lanes = lax.broadcasted_iota(jnp.int32, pair_rows.shape, 1)
    zero = jnp.zeros_like(pair_rows)
    return jnp.concatenate(
        [jnp.where(lanes < HD, pair_rows, zero), jnp.where(lanes < HD, zero, pair_rows)], axis=0
    )


def unstacked_heads(stacked):
    rows = stacked.shape[0] // 2
    lanes = lax.broadcasted_iota(jnp.int32, (rows, PAIR), 1)
    return jnp.where(lanes < HD, stacked[:rows], stacked[rows:])


def masked_scores(queries, keys, query_ids, key_ids):
    rows = query_ids.shape[0]
    bias = jnp.where(query_ids == key_ids, 0.0, NEGATIVE)
    scores = nt(queries, keys)
    return jnp.concatenate([scores[:rows] + bias, scores[rows:] + bias], axis=0)


def forward_kernel(qid_ref, kid_ref, q_ref, k_ref, v_ref, out_ref, lse_ref):
    keys = k_ref[0]
    values = v_ref[0]
    rows = q_ref.shape[1] // 2
    for side in range(2):
        span = slice(side * rows, (side + 1) * rows)
        queries = stacked_heads(q_ref[0, span])
        scores = masked_scores(queries, keys, qid_ref[0, span][:, :1], kid_ref[0][:1, :])
        highest = jnp.max(scores, axis=-1, keepdims=True)
        weights = jnp.exp(scores - highest)
        total = jnp.sum(weights, axis=-1, keepdims=True)
        probs = (weights * (1.0 / total)).astype(BF)
        out_ref[0, span] = unstacked_heads(nn(probs, values)).astype(BF)
        lse_ref[0, 0, side] = jnp.broadcast_to(highest + jnp.log(total), lse_ref.shape[3:])


def backward_kernel(
    qid_ref, kid_ref, q_ref, k_ref, v_ref, lse_ref, up_ref, dq_ref, dk_ref, dv_ref
):
    keys = k_ref[0]
    values = v_ref[0]
    rows = q_ref.shape[1] // 2
    key_sum, value_sum = 0.0, 0.0
    for side in range(2):
        span = slice(side * rows, (side + 1) * rows)
        queries = stacked_heads(q_ref[0, span])
        upward = stacked_heads(up_ref[0, span])
        scores = masked_scores(queries, keys, qid_ref[0, span][:, :1], kid_ref[0][:1, :])
        probs = jnp.exp(scores - lse_ref[0, 0, side][:, :1])
        dprobs = nt(upward, values)
        correction = jnp.sum(probs * dprobs, axis=-1, keepdims=True)
        dscores = (probs * (dprobs - correction)).astype(BF)
        back = unstacked_heads(nn(dscores, keys)).astype(BF).astype(F32)
        dq_ref[0, span] = (back * 0.125).astype(BF)
        key_sum += tn(dscores, queries)
        value_sum += tn(probs.astype(BF), upward)
    dk_ref[0] = key_sum.astype(BF)
    dv_ref[0] = value_sum.astype(BF)


def attention_specs(rows, count):
    return dict(
        qid=pl.BlockSpec((1, rows, 128), lambda s, p: (s, 0, 0)),
        kid=pl.BlockSpec((1, 8, count), lambda s, p: (s, 0, 0)),
        row=pl.BlockSpec((1, rows, PAIR), lambda s, p: (s, 0, p)),
        key=pl.BlockSpec((1, count, PAIR), lambda s, p: (s, 0, p)),
        value=pl.BlockSpec((1, count, PAIR), lambda s, p: (s, 0, PAIRS + p)),
        lse=pl.BlockSpec((1, 1, 2, rows, 128), lambda s, p: (s, p, 0, 0, 0)),
    )


def attend(query_ids, key_ids, queries, key_values):
    streams, rows, _ = queries.shape
    count = key_values.shape[1]
    specs = attention_specs(rows, count)
    macs = streams * 2 * PAIRS * rows * count * HD
    return pl.pallas_call(
        forward_kernel,
        grid=(streams, PAIRS),
        in_specs=[specs["qid"], specs["kid"], specs["row"], specs["key"], specs["value"]],
        out_specs=[specs["row"], specs["lse"]],
        out_shape=[
            jax.ShapeDtypeStruct((streams, rows, HALF), BF),
            jax.ShapeDtypeStruct((streams, PAIRS, 2, rows, 128), F32),
        ],
        compiler_params=pltpu.CompilerParams(vmem_limit_bytes=VMEM_LIMIT),
        cost_estimate=pl.CostEstimate(
            flops=8 * macs, bytes_accessed=2 * key_values.size, transcendentals=macs // HD
        ),
        name="attend",
    )(query_ids, key_ids, queries, key_values, key_values)


def attend_back(query_ids, key_ids, queries, key_values, lse, upward):
    streams, rows, _ = queries.shape
    count = key_values.shape[1]
    specs = attention_specs(rows, count)
    macs = streams * 2 * PAIRS * rows * count * HD
    key_shape = jax.ShapeDtypeStruct((streams, count, HALF), BF)
    return pl.pallas_call(
        backward_kernel,
        grid=(streams, PAIRS),
        in_specs=[
            specs["qid"],
            specs["kid"],
            specs["row"],
            specs["key"],
            specs["value"],
            specs["lse"],
            specs["row"],
        ],
        out_specs=[specs["row"], specs["key"], specs["key"]],
        out_shape=[jax.ShapeDtypeStruct((streams, rows, HALF), BF), key_shape, key_shape],
        compiler_params=pltpu.CompilerParams(vmem_limit_bytes=VMEM_LIMIT),
        cost_estimate=pl.CostEstimate(
            flops=20 * macs, bytes_accessed=4 * key_values.size, transcendentals=macs // HD
        ),
        name="attend_back",
    )(query_ids, key_ids, queries, key_values, key_values, lse, upward)


def norm_rows(value_rows):
    centre = jnp.mean(value_rows, axis=-1, keepdims=True)
    centred = value_rows - centre
    inverse = lax.rsqrt(jnp.mean(centred * centred, axis=-1, keepdims=True) + EPSILON)
    return (centred * inverse, inverse)


def norm_back(upward, normed, inverse):
    mean_up = jnp.mean(upward, axis=-1, keepdims=True)
    mean_cross = jnp.mean(upward * normed, axis=-1, keepdims=True)
    return inverse * (upward - mean_up - normed * mean_cross)


def column_sum(value_rows):
    return jnp.sum(value_rows.astype(F32), axis=0)


def item_ids(lengths, places):
    items = lengths.shape[1]
    slot = jnp.arange(items, dtype=jnp.int32)
    ends = jnp.sum(jnp.where(slot[:, None] <= slot[None, :], lengths[:, :, None], 0), axis=1)
    return jnp.sum((ends[:, None, :] <= places[None, :, None]).astype(jnp.int32), axis=2)


def body(
    tokens,
    query_weight,
    query_bias,
    key_weight,
    value_weight,
    value_bias,
    out_weight,
    out_bias,
    first_gain,
    attention_norm_shift,
    expand_weight,
    expand_bias,
    reduce_weight,
    reduce_bias,
    second_gain,
    second_shift,
    lengths,
    cotangent,
    *,
    dps,
    seq,
):
    streams, row_count, _ = tokens.shape
    zs = seq // 2
    chips = dps * zs
    block = D // (2 * chips)
    both = 2 * block
    wide = FF // (2 * chips)
    chip_rows = 2 * row_count
    rows = streams * chip_rows
    dp = lax.axis_index("dp")
    z = lax.axis_index("seq") // 2
    core = lax.axis_index("seq") % 2
    place = jnp.stack([dp, z, core]).astype(jnp.int32)
    swap = functools.partial(core_swap, seq=seq)

    def row_major(value):
        return with_layout_constraint(value, Layout(major_to_minor=tuple(range(value.ndim))))

    def in_core_order(mine, other, axis):
        return jnp.where(
            core == 0,
            jnp.concatenate([mine, other], axis=axis),
            jnp.concatenate([other, mine], axis=axis),
        )

    all_tokens = row_major(lax.all_gather(tokens, "seq", axis=1, tiled=True))
    reduce_weight = lax.all_gather(reduce_weight.astype(BF), ("dp", "seq"), axis=0)
    mine, theirs = first_columns(
        place,
        (query_weight, key_weight, value_weight),
        (
            query_bias,
            value_bias,
            out_bias,
            first_gain,
            attention_norm_shift,
            reduce_bias,
            second_gain,
            second_shift,
            expand_bias,
        ),
    )
    early = gather_chips(in_core_order(mine[None], swap(theirs)[None], 0), dps, seq)

    out_weight = out_weight.astype(BF)
    units = expand_weight.astype(BF).reshape(block, chips, 2, wide)

    def columns_for(side):
        unit = lax.dynamic_index_in_dim(units, side, 2, keepdims=False).reshape(block, UNITS)
        return jnp.concatenate(
            [lax.dynamic_slice_in_dim(out_weight, side * HALF, HALF, 1), unit], axis=1
        )

    late = in_core_order(columns_for(core)[None], swap(columns_for(1 - core))[None], 0)
    late = gather_chips(late, dps, seq)
    cotangent = in_core_order(cotangent, swap(cotangent), 1)

    def gather_plan(parts):
        return [
            (
                k,
                lambda dp, z, j=j, first=first, count=count: (
                    j,
                    slice(None),
                    slice(None),
                    at_lanes(first, count),
                ),
                target,
                lambda dp, z, j=j, k=k: (dp ^ k, z ^ j),
            )
            for k in range(dps)
            for j in range(zs)
            for first, count, target in parts
        ]

    qkv_weight, small = local_copies(
        place,
        early,
        [(dps, zs, 2, block, 3 * HALF), (dps, zs, 2, block, 128)],
        gather_plan([(0, 3 * HALF, 0), (3 * HALF, 128, 1)]),
        "place_early",
    )
    qkv_weight = qkv_weight.reshape(D, 3 * HALF)
    small = small.astype(F32).reshape(D, 128)[:, :12].T
    (
        query_bias,
        value_bias,
        out_bias,
        first_gain,
        attention_norm_shift,
        reduce_bias,
        second_gain,
        second_shift,
    ) = (small[i : i + 1] for i in range(8))
    expand_bias = small[8:12].reshape(4, chips, 2, block)
    expand_bias = lax.dynamic_index_in_dim(expand_bias, core, 2, keepdims=False)
    expand_bias = expand_bias.transpose(1, 0, 2).reshape(1, UNITS)

    def half_of(vector):
        return lax.dynamic_slice_in_dim(vector, core * HALF, HALF, 1)

    chip_tokens = lax.dynamic_slice_in_dim(all_tokens, z * chip_rows, chip_rows, 1).reshape(rows, D)
    flat_all = all_tokens.reshape(-1, D)
    ids = item_ids(lengths, jnp.arange(all_tokens.shape[1], dtype=jnp.int32))
    key_ids = jnp.broadcast_to(ids[:, None, :], (streams, 8, ids.shape[1]))
    query_ids = lax.dynamic_slice_in_dim(ids, z * chip_rows, chip_rows, 1)
    query_ids = jnp.broadcast_to(query_ids[..., None], (streams, chip_rows, 128))

    queries = ((nn(chip_tokens, qkv_weight[:, :HALF]) + half_of(query_bias)) * 0.125).astype(BF)
    queries = row_major(queries.reshape(streams, chip_rows, HALF))
    key_value_bias = jnp.concatenate([jnp.zeros((1, HALF), F32), half_of(value_bias)], axis=1)
    key_values = (nn(flat_all, qkv_weight[:, HALF:]) + key_value_bias).astype(BF)
    key_values = row_major(key_values.reshape(streams, -1, D))
    attended, lse = attend(query_ids, key_ids, queries, key_values)
    attended = in_core_order(attended, swap(attended), 2).reshape(rows, D)

    out_half, expand_weight = local_copies(
        place,
        late,
        [(dps, zs, 2, block, HALF), (dps, zs, 2, block, UNITS)],
        gather_plan([(0, HALF, 0), (HALF, UNITS, 1)]),
        "place_late",
    )
    out_half = out_half.reshape(D, HALF)
    out_weight = in_core_order(out_half, swap(out_half), 1)
    out_rows = lax.dynamic_slice_in_dim(out_weight, core * HALF, HALF, 0)
    expand_weight = expand_weight.reshape(D, UNITS)
    reduce_weight = lax.dynamic_index_in_dim(
        reduce_weight.reshape(chips, 2, wide, D), core, 1, keepdims=False
    ).reshape(UNITS, D)

    def own(value):
        value = value.reshape(streams, chip_rows, -1)
        return lax.dynamic_slice_in_dim(value, core * row_count, row_count, 1)

    branch = nn(attended, out_weight) + out_bias
    normed_one, inverse_one = norm_rows(chip_tokens.astype(F32) + branch)
    first = normed_one * first_gain + attention_norm_shift
    first_low = first.astype(BF)
    expanded = nn(first_low, expand_weight) + expand_bias
    hidden, gelu_pull = jax.vjp(lambda inner: jax.nn.gelu(inner, approximate=False), expanded)
    hidden = hidden.astype(BF)
    partial = nn(hidden, reduce_weight)
    reduced = partial + swap(partial) + reduce_bias
    normed_two, inverse_two = norm_rows(first + reduced)
    activations = own((normed_two * second_gain + second_shift).astype(BF))

    upward = cotangent.reshape(rows, D).astype(F32)
    second_gain_grad = jnp.sum(upward * normed_two, axis=0)
    second_shift_grad = jnp.sum(upward, axis=0)
    residual_two_back = norm_back(upward * second_gain, normed_two, inverse_two)
    reduced_back = residual_two_back.astype(BF)
    reduce_weight_grad = tn(hidden, reduced_back).astype(BF)
    reduce_bias_grad = column_sum(reduced_back)
    expanded_back = gelu_pull(nt(reduced_back, reduce_weight))[0].astype(BF)
    expand_weight_grad = tn(first_low, expanded_back).astype(BF)
    expand_bias_grad = column_sum(expanded_back)

    def scatter_plan(parts, lanes):
        shapes = [(zs, both, lanes)] * dps
        plan = [
            (
                source,
                lambda dp, z, j=j, k=k, index=index: index(dp ^ k, z ^ j),
                k,
                lambda dp, z, j=j, first=first, count=count: (j, slice(None), at_lanes(first, count)),
            )
            for k in list(range(1, dps)) + [0]
            for j in range(zs)
            for source, index, first, count in parts
        ]
        return shapes, plan

    wide_packs = local_copies(
        place,
        [
            reduce_weight_grad.reshape(dps, zs, 2, both, D),
            expand_weight_grad.reshape(dps, zs, both, UNITS),
        ],
        *scatter_plan(
            [
                (0, lambda d, zz: (d, zz, 0), 0, D),
                (0, lambda d, zz: (d, zz, 1), D, D),
                (1, lambda d, zz: (d, zz), 2 * D, UNITS),
            ],
            2 * D + UNITS,
        ),
        "pack_wide",
    )
    wide_came = along_dp(wide_packs, dps)

    partial = nt(expanded_back, expand_weight)
    first_back = partial + swap(partial) + residual_two_back
    first_gain_grad = jnp.sum(first_back * normed_one, axis=0)
    first_shift_grad = jnp.sum(first_back, axis=0)
    residual_one_back = norm_back(first_back * first_gain, normed_one, inverse_one)
    branch_back = residual_one_back.astype(BF)
    out_weight_grad = tn(attended, half_of(branch_back)).astype(BF)
    out_bias_grad = column_sum(branch_back)
    attended_back = row_major(nt(branch_back, out_rows).astype(BF).reshape(streams, chip_rows, HALF))

    query_back, key_back, value_back = attend_back(
        query_ids, key_ids, queries, key_values, lse, attended_back
    )
    flat_query_back = query_back.reshape(rows, HALF)
    key_back = key_back.reshape(-1, HALF)
    value_back = value_back.reshape(-1, HALF)

    tokens_part = nt(key_back, qkv_weight[:, HALF : 2 * HALF]) + nt(value_back, qkv_weight[:, 2 * HALF :])
    tokens_part = lax.psum_scatter(
        tokens_part.astype(BF).reshape(streams, -1, D), "seq", scatter_dimension=1, tiled=True
    )
    query_part = nt(flat_query_back, qkv_weight[:, :HALF]).astype(BF)
    query_part = own(query_part).astype(F32) + own(swap(query_part)).astype(F32)
    tokens_gradient = own(residual_one_back) + query_part + tokens_part.astype(F32)

    query_weight_grad = tn(chip_tokens, flat_query_back).astype(BF)
    key_weight_grad = tn(flat_all, key_back).astype(BF)
    value_weight_grad = tn(flat_all, value_back).astype(BF)

    half_sums = jnp.stack([column_sum(flat_query_back), column_sum(value_back)])
    full_sums = in_core_order(half_sums, swap(half_sums), 1)
    small_grads = jnp.concatenate(
        [
            full_sums,
            jnp.stack(
                [
                    out_bias_grad,
                    first_gain_grad,
                    first_shift_grad,
                    reduce_bias_grad,
                    second_gain_grad,
                    second_shift_grad,
                ]
            ),
            expand_bias_grad.reshape(chips, 2, both).transpose(1, 0, 2).reshape(2, D),
        ],
        axis=0,
    ).T.astype(BF)
    small_grads = jnp.pad(small_grads, ((0, 0), (0, 128 - small_grads.shape[1])))
    four = (query_weight_grad, key_weight_grad, value_weight_grad, out_weight_grad)
    narrow_packs = local_copies(
        place,
        [g.reshape(dps, zs, both, HALF) for g in four] + [small_grads.reshape(dps, zs, both, 128)],
        *scatter_plan(
            [(i, lambda d, zz: (d, zz), i * HALF, HALF) for i in range(4)]
            + [(4, lambda d, zz: (d, zz), 4 * HALF, 128)],
            4 * HALF + 128,
        ),
        "pack_narrow",
    )
    narrow_grads = add_along_z(along_dp(narrow_packs, dps), seq)
    wide_came = list(lax.optimization_barrier((tuple(wide_came), query_back))[0])
    wide_grads = add_along_z(wide_came, seq)

    def own_rows(grads):
        split = grads.reshape(2, block, grads.shape[1])
        mine = lax.dynamic_index_in_dim(split, core, 0, keepdims=False)
        return mine, swap(lax.dynamic_index_in_dim(split, 1 - core, 0, keepdims=False))

    mine, other = own_rows(narrow_grads[:, : 4 * HALF])
    matrices = [
        in_core_order(mine[:, i * HALF : (i + 1) * HALF], other[:, i * HALF : (i + 1) * HALF], 1)
        for i in range(4)
    ]
    small = narrow_grads[:, 4 * HALF :]
    own_small = lax.dynamic_slice_in_dim(small, core * block, block, 0).T
    expand_bias_grad = small[:, 8:10].T.reshape(wide)
    mine, other = own_rows(wide_grads[:, 2 * D :])
    expand_grads = in_core_order(
        mine.reshape(block, chips, 1, wide), other.reshape(block, chips, 1, wide), 2
    ).reshape(block, FF)
    reduce_grads = jnp.concatenate([wide_grads[:, :D], wide_grads[:, D : 2 * D]], axis=0)

    return (
        activations,
        tokens_gradient,
        matrices[0],
        own_small[0],
        matrices[1],
        matrices[2],
        own_small[1],
        matrices[3],
        own_small[2],
        own_small[3],
        own_small[4],
        expand_grads,
        expand_bias_grad,
        reduce_grads,
        own_small[5],
        own_small[6],
        own_small[7],
    )


def solution(mesh):
    sharded = ("dp", "seq")
    matrix = P(sharded, None)
    vector = P(sharded)
    token = P("dp", "seq", None)
    params = (
        matrix,
        vector,
        matrix,
        matrix,
        vector,
        matrix,
        vector,
        vector,
        vector,
        matrix,
        vector,
        matrix,
        vector,
        vector,
        vector,
    )
    return jax.shard_map(
        functools.partial(body, dps=mesh.shape["dp"], seq=mesh.shape["seq"]),
        mesh=mesh,
        in_specs=(token,) + params + (P("dp", None), token),
        out_specs=(token, token) + params,
        check_vma=False,
    )
```

```python
import functools

import jax
import jax.numpy as jnp
from jax import lax
from jax.experimental.layout import Layout, with_layout_constraint
from jax.experimental import pallas as pl
from jax.experimental.pallas import tpu as pltpu
from jax.sharding import PartitionSpec as P

D = 768
HEADS = 12
HD = 64
FF = 3072
HALF = D // 2
UNITS = FF // 2
PAIR = 2 * HD
PAIRS = HALF // PAIR
NEGATIVE = -1e30
EPSILON = 1e-12
BF = jnp.bfloat16
F32 = jnp.float32
VMEM_LIMIT = 56 * 1024 * 1024
QUICK = pl.CostEstimate(flops=0, bytes_accessed=0, transcendentals=0)


def nn(left, right):
    return lax.dot_general(left, right, (((1,), (0,)), ((), ())), preferred_element_type=F32)


def nt(left, right):
    return lax.dot_general(left, right, (((1,), (1,)), ((), ())), preferred_element_type=F32)


def tn(left, right):
    return lax.dot_general(left, right, (((0,), (0,)), ((), ())), preferred_element_type=F32)


def local_copies(place, sources, shapes, plan, name, late=()):
    def kernel(place_ref, *refs):
        ins = refs[: len(sources)]
        outs = refs[len(sources) + len(late) :]
        dp = place_ref[0]
        z = place_ref[1]
        for source, source_index, target, target_index in plan:
            outs[target][target_index(dp, z)] = ins[source][source_index(dp, z)]

    moved = 2 * sum(functools.reduce(lambda a, b: a * b, s) for s in shapes)
    return pl.pallas_call(
        kernel,
        in_specs=[pl.BlockSpec(memory_space=pltpu.SMEM)]
        + [pl.BlockSpec(memory_space=pltpu.VMEM)] * len(sources)
        + [pl.BlockSpec(memory_space=pl.ANY)] * len(late),
        out_specs=[pl.BlockSpec(memory_space=pltpu.VMEM)] * len(shapes),
        out_shape=[jax.ShapeDtypeStruct(shape, BF) for shape in shapes],
        compiler_params=pltpu.CompilerParams(vmem_limit_bytes=VMEM_LIMIT),
        cost_estimate=QUICK,
        name=name,
    )(place, *sources, *late)


def first_columns(place, weights, vectors):
    block = weights[0].shape[0]
    lanes = len(weights) * HALF + 128

    def kernel(place_ref, *refs):
        ins, (mine_ref, theirs_ref, square_ref) = refs[: len(weights) + len(vectors)], refs[-3:]
        core = place_ref[2]
        square_ref[...] = jnp.zeros_like(square_ref)
        row = 0
        for ref in ins[len(weights) :]:
            for part in range(ref.shape[0] // block):
                square_ref[row : row + 1, 0:block] = ref[part * block : (part + 1) * block].reshape(1, block)
                row += 1
        columns = square_ref[...].T[:block].astype(BF)
        for out, side in ((mine_ref, core), (theirs_ref, 1 - core)):
            for i in range(len(weights)):
                picked = ins[i][:, pl.ds(pl.multiple_of(side * HALF, 128), HALF)]
                out[:, i * HALF : (i + 1) * HALF] = picked.astype(BF)
            out[:, len(weights) * HALF :] = columns

    shape = jax.ShapeDtypeStruct((block, lanes), BF)
    return pl.pallas_call(
        kernel,
        in_specs=[pl.BlockSpec(memory_space=pltpu.SMEM)]
        + [pl.BlockSpec(memory_space=pltpu.VMEM)] * (len(weights) + len(vectors)),
        out_specs=[pl.BlockSpec(memory_space=pltpu.VMEM)] * 2,
        out_shape=[shape, shape],
        scratch_shapes=[pltpu.VMEM((128, 128), F32)],
        name="first_columns",
    )(place, *weights, *vectors)


def at_lanes(start, count):
    return pl.ds(start, count)


def core_swap(value, seq):
    return lax.ppermute(value, "seq", [(i, i ^ 1) for i in range(seq)])


def z_move(value, step, seq):
    return lax.ppermute(value, "seq", [(i, i ^ (2 * step)) for i in range(seq)])


def dp_move(value, step, dps):
    return lax.ppermute(value, "dp", [(i, i ^ step) for i in range(dps)])


def tied(value, *others):
    return lax.optimization_barrier((value, others))[0]


def z_moves(value, seq):
    return [value] + [z_move(value, j, seq) for j in range(1, seq // 2)]


def gather_dp_first(value, dps):
    return [value] + [dp_move(value, k, dps) for k in range(1, 3 if dps == 4 else dps)]


def gather_dp_rest(blocks, dps):
    if dps != 4:
        return blocks
    half = blocks[0].shape[0] // 2
    return blocks + [dp_move(blocks[2][:half], 1, dps), dp_move(blocks[1][half:], 2, dps)]


def dp_pieces(dps, zs):
    half = zs // 2
    for k in range(dps):
        for j in range(zs):
            if dps == 4 and k == 3:
                yield (3, j, k, j) if j < half else (4, j - half, k, j)
            else:
                yield k, j, k, j


def scatter_slots(dps, zs):
    if dps != 4:
        return {(k, j): (k, j) for k in range(dps) for j in range(zs)}, [zs] * dps
    half = zs // 2
    slots = {}
    for j in range(half):
        low, high = j, half + j
        slots[0, low], slots[0, high] = (0, low), (0, high)
        slots[1, low], slots[3, low] = (1, low), (1, half + j)
        slots[2, high], slots[3, high] = (2, j), (2, half + j)
        slots[1, high] = (3, j)
        slots[2, low] = (4, j)
    return slots, [zs, zs, zs, half, half]


def wide_sum(terms):
    return functools.reduce(jnp.add, [t.astype(F32) for t in terms])


def scatter_dp_first(packs, dps):
    if dps != 4:
        return [dp_move(packs[k], k, dps) for k in range(1, dps)]
    return [dp_move(packs[1], 1, dps), dp_move(packs[2], 2, dps)]


def scatter_dp_middle(packs, came, dps):
    if dps != 4:
        return []
    half = packs[3].shape[0]
    return [
        wide_sum([packs[4], came[0][half:]]).astype(BF),
        wide_sum([packs[3], came[1][half:]]).astype(BF),
    ]


def scatter_dp_rest(packs, came, onward, dps, tie=lambda came: came):
    if dps != 4:
        came = tie(came)
        return [wide_sum([packs[0][j]] + [c[j] for c in came]) for j in range(packs[0].shape[0])]
    half = packs[3].shape[0]
    again_two, again_one = tie([dp_move(onward[0], 2, dps), dp_move(onward[1], 1, dps)])
    low = [wide_sum([packs[0][j], came[0][j], again_two[j]]) for j in range(half)]
    return low + [wide_sum([packs[0][half + j], came[1][j], again_one[j]]) for j in range(half)]


def scatter_z(totals, seq, tie=lambda moved: moved):
    moved = tie([z_move(totals[j].astype(BF), j, seq) for j in range(1, seq // 2)])
    return wide_sum([totals[0]] + moved)


def stacked_heads(pair_rows):
    lanes = lax.broadcasted_iota(jnp.int32, pair_rows.shape, 1)
    zero = jnp.zeros_like(pair_rows)
    return jnp.concatenate(
        [jnp.where(lanes < HD, pair_rows, zero), jnp.where(lanes < HD, zero, pair_rows)], axis=0
    )


def unstacked_heads(stacked):
    rows = stacked.shape[0] // 2
    lanes = lax.broadcasted_iota(jnp.int32, (rows, PAIR), 1)
    return jnp.where(lanes < HD, stacked[:rows], stacked[rows:])


def masked_scores(queries, keys, query_ids, key_ids):
    rows = query_ids.shape[0]
    bias = jnp.where(query_ids == key_ids, 0.0, NEGATIVE)
    scores = nt(queries, keys)
    return jnp.concatenate([scores[:rows] + bias, scores[rows:] + bias], axis=0)


def forward_kernel(qid_ref, kid_ref, q_ref, k_ref, v_ref, out_ref, lse_ref):
    keys = k_ref[0]
    values = v_ref[0]
    rows = q_ref.shape[1] // 2
    for side in range(2):
        span = slice(side * rows, (side + 1) * rows)
        queries = stacked_heads(q_ref[0, span])
        scores = masked_scores(queries, keys, qid_ref[0, span][:, :1], kid_ref[0][:1, :])
        highest = jnp.max(scores, axis=-1, keepdims=True)
        weights = jnp.exp(scores - highest)
        total = jnp.sum(weights, axis=-1, keepdims=True)
        probs = (weights * (1.0 / total)).astype(BF)
        out_ref[0, span] = unstacked_heads(nn(probs, values)).astype(BF)
        lse_ref[0, 0, side] = jnp.broadcast_to(highest + jnp.log(total), lse_ref.shape[3:])


def backward_kernel(
    qid_ref, kid_ref, q_ref, k_ref, v_ref, lse_ref, up_ref, dq_ref, dk_ref, dv_ref
):
    keys = k_ref[0]
    values = v_ref[0]
    rows = q_ref.shape[1] // 2
    key_sum, value_sum = 0.0, 0.0
    for side in range(2):
        span = slice(side * rows, (side + 1) * rows)
        queries = stacked_heads(q_ref[0, span])
        upward = stacked_heads(up_ref[0, span])
        scores = masked_scores(queries, keys, qid_ref[0, span][:, :1], kid_ref[0][:1, :])
        probs = jnp.exp(scores - lse_ref[0, 0, side][:, :1])
        dprobs = nt(upward, values)
        correction = jnp.sum(probs * dprobs, axis=-1, keepdims=True)
        dscores = (probs * (dprobs - correction)).astype(BF)
        back = unstacked_heads(nn(dscores, keys)).astype(BF).astype(F32)
        dq_ref[0, span] = (back * 0.125).astype(BF)
        key_sum += tn(dscores, queries)
        value_sum += tn(probs.astype(BF), upward)
    dk_ref[0] = key_sum.astype(BF)
    dv_ref[0] = value_sum.astype(BF)


def attention_specs(rows, count):
    return dict(
        qid=pl.BlockSpec((1, rows, 128), lambda s, p: (s, 0, 0)),
        kid=pl.BlockSpec((1, 8, count), lambda s, p: (s, 0, 0)),
        row=pl.BlockSpec((1, rows, PAIR), lambda s, p: (s, 0, p)),
        key=pl.BlockSpec((1, count, PAIR), lambda s, p: (s, 0, p)),
        value=pl.BlockSpec((1, count, PAIR), lambda s, p: (s, 0, PAIRS + p)),
        lse=pl.BlockSpec((1, 1, 2, rows, 128), lambda s, p: (s, p, 0, 0, 0)),
    )


def attend(query_ids, key_ids, queries, key_values):
    streams, rows, _ = queries.shape
    count = key_values.shape[1]
    specs = attention_specs(rows, count)
    macs = streams * 2 * PAIRS * rows * count * HD
    return pl.pallas_call(
        forward_kernel,
        grid=(streams, PAIRS),
        in_specs=[specs["qid"], specs["kid"], specs["row"], specs["key"], specs["value"]],
        out_specs=[specs["row"], specs["lse"]],
        out_shape=[
            jax.ShapeDtypeStruct((streams, rows, HALF), BF),
            jax.ShapeDtypeStruct((streams, PAIRS, 2, rows, 128), F32),
        ],
        compiler_params=pltpu.CompilerParams(vmem_limit_bytes=VMEM_LIMIT),
        cost_estimate=QUICK,
        name="attend",
    )(query_ids, key_ids, queries, key_values, key_values)


def attend_back(query_ids, key_ids, queries, key_values, lse, upward):
    streams, rows, _ = queries.shape
    count = key_values.shape[1]
    specs = attention_specs(rows, count)
    macs = streams * 2 * PAIRS * rows * count * HD
    key_shape = jax.ShapeDtypeStruct((streams, count, HALF), BF)
    return pl.pallas_call(
        backward_kernel,
        grid=(streams, PAIRS),
        in_specs=[
            specs["qid"],
            specs["kid"],
            specs["row"],
            specs["key"],
            specs["value"],
            specs["lse"],
            specs["row"],
        ],
        out_specs=[specs["row"], specs["key"], specs["key"]],
        out_shape=[jax.ShapeDtypeStruct((streams, rows, HALF), BF), key_shape, key_shape],
        compiler_params=pltpu.CompilerParams(vmem_limit_bytes=VMEM_LIMIT),
        cost_estimate=QUICK,
        name="attend_back",
    )(query_ids, key_ids, queries, key_values, key_values, lse, upward)


TILE = 256
CHUNK = 384
QUERY_BIAS, VALUE_BIAS, OUT_BIAS, FIRST_GAIN, FIRST_SHIFT, REDUCE_BIAS, SECOND_GAIN, SECOND_SHIFT = range(8)


def norm_rows(value_rows):
    centre = jnp.mean(value_rows, axis=-1, keepdims=True)
    centred = value_rows - centre
    inverse = lax.rsqrt(jnp.mean(centred * centred, axis=-1, keepdims=True) + EPSILON)
    return (centred * inverse, inverse)


def norm_back(upward, normed, inverse):
    mean_up = jnp.mean(upward, axis=-1, keepdims=True)
    mean_cross = jnp.mean(upward * normed, axis=-1, keepdims=True)
    return inverse * (upward - mean_up - normed * mean_cross)


def add_rows(sum_ref, index, values):
    sum_ref[index] += jnp.sum(values.reshape(-1, 8, values.shape[1]), axis=0)


def vector_of(vec_ref, index):
    return vec_ref[index : index + 1, :]


def middle_kernel(
    place_ref, mine_ref, other_ref, tok_ref, vec_ref, unit_ref, out_ref, expand_ref,
    normed_ref, inverse_ref, low_ref, hidden_ref, slope_ref,
):
    core = place_ref[2]
    for_mine = out_ref[pl.ds(pl.multiple_of(core * HALF, 128), HALF), :]
    for_other = out_ref[pl.ds(pl.multiple_of((1 - core) * HALF, 128), HALF), :]
    branch = nn(mine_ref[...], for_mine) + nn(other_ref[...], for_other) + vector_of(vec_ref, OUT_BIAS)
    normed, inverse = norm_rows(tok_ref[...].astype(F32) + branch)
    normed_ref[...] = normed
    inverse_ref[...] = jnp.broadcast_to(inverse, inverse_ref.shape)
    first = normed * vector_of(vec_ref, FIRST_GAIN) + vector_of(vec_ref, FIRST_SHIFT)
    low = first.astype(BF)
    low_ref[...] = low
    for start in range(0, UNITS, CHUNK):
        span = slice(start, start + CHUNK)
        expanded = nn(low, expand_ref[:, span]) + unit_ref[:, span]
        share = 0.5 * (1.0 + lax.erf(expanded * (0.5**0.5)))
        hidden_ref[:, span] = (expanded * share).astype(BF)
        bell = jnp.exp(-0.5 * expanded * expanded) * 0.3989422804014327
        slope_ref[:, span] = (share + expanded * bell).astype(BF)


def turn_kernel(
    part_ref, came_ref, normed_ref, cot_ref, slope_ref, vec_ref, reduce_ref, expand_ref,
    act_ref, residual_ref, low_ref, back_ref, next_ref, sum_ref, unit_sum_ref,
):
    @pl.when(pl.program_id(0) == 0)
    def _():
        sum_ref[...] = jnp.zeros_like(sum_ref)
        unit_sum_ref[...] = jnp.zeros_like(unit_sum_ref)

    first = normed_ref[...] * vector_of(vec_ref, FIRST_GAIN) + vector_of(vec_ref, FIRST_SHIFT)
    reduced = part_ref[...] + came_ref[...] + vector_of(vec_ref, REDUCE_BIAS)
    normed, inverse = norm_rows(first + reduced)
    gain = vector_of(vec_ref, SECOND_GAIN)
    act_ref[...] = (normed * gain + vector_of(vec_ref, SECOND_SHIFT)).astype(BF)
    upward = cot_ref[...].astype(F32)
    residual = norm_back(upward * gain, normed, inverse)
    low = residual.astype(BF)
    residual_ref[...] = residual
    low_ref[...] = low
    add_rows(sum_ref, 0, low.astype(F32))
    add_rows(sum_ref, 1, upward * normed)
    add_rows(sum_ref, 2, upward)
    total = jnp.zeros(next_ref.shape, F32)
    for start in range(0, UNITS, CHUNK):
        span = slice(start, start + CHUNK)
        back = (nt(low, reduce_ref[span, :]) * slope_ref[:, span].astype(F32)).astype(BF)
        back_ref[:, span] = back
        unit_sum_ref[:, span] += jnp.sum(back.astype(F32).reshape(-1, 8, CHUNK), axis=0)
        total += nt(back, expand_ref[:, span])
    next_ref[...] = total


def first_back_kernel(
    place_ref, part_ref, came_ref, residual_ref, normed_ref, inverse_ref, vec_ref, out_ref,
    back_ref, low_ref, attended_ref, sum_ref,
):
    @pl.when(pl.program_id(0) == 0)
    def _():
        sum_ref[...] = jnp.zeros_like(sum_ref)

    core = place_ref[2]
    upward = part_ref[...] + came_ref[...] + residual_ref[...]
    normed = normed_ref[...]
    add_rows(sum_ref, 1, upward * normed)
    add_rows(sum_ref, 2, upward)
    back = norm_back(upward * vector_of(vec_ref, FIRST_GAIN), normed, inverse_ref[:, :1])
    low = back.astype(BF)
    back_ref[...] = back
    low_ref[...] = low
    add_rows(sum_ref, 0, low.astype(F32))
    mine = out_ref[pl.ds(pl.multiple_of(core * HALF, 128), HALF), :]
    attended_ref[...] = nt(low, mine).astype(BF)


def over_rows(kernel, place, tiled, whole, outs, sums, name, macs):
    rows = tiled[0].shape[0]
    tile = lambda lanes: pl.BlockSpec((TILE, lanes), lambda t: (t, 0))
    keep = lambda shape: pl.BlockSpec(shape, lambda t: (0,) * len(shape))
    places = [] if place is None else [place]
    return pl.pallas_call(
        kernel,
        grid=(rows // TILE,),
        in_specs=[pl.BlockSpec(memory_space=pltpu.SMEM)] * len(places)
        + [tile(v.shape[1]) for v in tiled]
        + [pl.BlockSpec(memory_space=pltpu.VMEM)] * len(whole),
        out_specs=[tile(lanes) for lanes, _ in outs] + [keep(shape) for shape in sums],
        out_shape=[jax.ShapeDtypeStruct((rows, lanes), dtype) for lanes, dtype in outs]
        + [jax.ShapeDtypeStruct(shape, F32) for shape in sums],
        compiler_params=pltpu.CompilerParams(vmem_limit_bytes=VMEM_LIMIT),
        cost_estimate=QUICK,
        name=name,
    )(*places, *tiled, *whole)


def column_sum(value_rows):
    return jnp.sum(value_rows.astype(F32), axis=0)


def item_ids(lengths, places):
    items = lengths.shape[1]
    slot = jnp.arange(items, dtype=jnp.int32)
    ends = jnp.sum(jnp.where(slot[:, None] <= slot[None, :], lengths[:, :, None], 0), axis=1)
    return jnp.sum((ends[:, None, :] <= places[None, :, None]).astype(jnp.int32), axis=2)


def body(
    tokens,
    query_weight,
    query_bias,
    key_weight,
    value_weight,
    value_bias,
    out_weight,
    out_bias,
    first_gain,
    attention_norm_shift,
    expand_weight,
    expand_bias,
    reduce_weight,
    reduce_bias,
    second_gain,
    second_shift,
    lengths,
    cotangent,
    *,
    dps,
    seq,
):
    streams, row_count, _ = tokens.shape
    zs = seq // 2
    chips = dps * zs
    block = D // (2 * chips)
    both = 2 * block
    wide = FF // (2 * chips)
    chip_rows = 2 * row_count
    rows = streams * chip_rows
    dp = lax.axis_index("dp")
    z = lax.axis_index("seq") // 2
    core = lax.axis_index("seq") % 2
    place = jnp.stack([dp, z, core]).astype(jnp.int32)
    swap = functools.partial(core_swap, seq=seq)

    def row_major(value):
        return with_layout_constraint(value, Layout(major_to_minor=tuple(range(value.ndim))))

    def in_core_order(mine, other, axis):
        return jnp.where(
            core == 0,
            jnp.concatenate([mine, other], axis=axis),
            jnp.concatenate([other, mine], axis=axis),
        )

    mine, theirs = first_columns(
        place,
        (query_weight, key_weight, value_weight),
        (
            query_bias,
            value_bias,
            out_bias,
            first_gain,
            attention_norm_shift,
            reduce_bias,
            second_gain,
            second_shift,
            expand_bias,
        ),
    )
    early = in_core_order(mine[None], swap(theirs)[None], 0)

    out_weight = out_weight.astype(BF)
    units = expand_weight.astype(BF).reshape(block, chips, 2, wide)

    def columns_for(side):
        unit = lax.dynamic_index_in_dim(units, side, 2, keepdims=False).reshape(block, UNITS)
        return jnp.concatenate([out_weight, unit], axis=1)

    late = in_core_order(columns_for(core)[None], swap(columns_for(1 - core))[None], 0)
    early = jnp.stack(tied(z_moves(early, seq), late))
    late = z_moves(tied(late, early), seq)
    early, late = lax.optimization_barrier((gather_dp_first(early, dps), late))
    early = gather_dp_rest(early, dps)
    late = jnp.stack(late)
    all_tokens = row_major(lax.all_gather(tied(tokens, late), "seq", axis=1, tiled=True))
    last = z_moves(tied(reduce_weight.astype(BF), late), seq)
    late = gather_dp_rest(gather_dp_first(late, dps), dps)
    last = gather_dp_first(jnp.stack(last), dps)
    cotangent = in_core_order(cotangent, swap(cotangent), 1)

    def gather_plan(parts):
        return [
            (
                piece,
                lambda dp, z, row=row, first=first, count=count: (
                    row,
                    Ellipsis,
                    at_lanes(first, count),
                ),
                target,
                lambda dp, z, j=j, k=k: (dp ^ k, z ^ j),
            )
            for piece, row, k, j in dp_pieces(dps, zs)
            for first, count, target in parts
        ]

    qkv_weight, small = local_copies(
        place,
        early,
        [(dps, zs, 2, block, 3 * HALF), (dps, zs, 2, block, 128)],
        gather_plan([(0, 3 * HALF, 0), (3 * HALF, 128, 1)]),
        "place_early",
    )
    qkv_weight = qkv_weight.reshape(D, 3 * HALF)
    small = small.astype(F32).reshape(D, 128)[:, :12].T
    query_bias, value_bias = small[QUERY_BIAS : QUERY_BIAS + 1], small[VALUE_BIAS : VALUE_BIAS + 1]
    expand_bias = small[8:12].reshape(4, chips, 2, block)
    expand_bias = lax.dynamic_index_in_dim(expand_bias, core, 2, keepdims=False)
    expand_bias = expand_bias.transpose(1, 0, 2).reshape(1, UNITS)

    def half_of(vector):
        return lax.dynamic_slice_in_dim(vector, core * HALF, HALF, 1)

    chip_tokens = lax.dynamic_slice_in_dim(all_tokens, z * chip_rows, chip_rows, 1).reshape(rows, D)
    flat_all = all_tokens.reshape(-1, D)
    ids = item_ids(lengths, jnp.arange(all_tokens.shape[1], dtype=jnp.int32))
    key_ids = jnp.broadcast_to(ids[:, None, :], (streams, 8, ids.shape[1]))
    query_ids = lax.dynamic_slice_in_dim(ids, z * chip_rows, chip_rows, 1)
    query_ids = jnp.broadcast_to(query_ids[..., None], (streams, chip_rows, 128))

    queries = ((nn(chip_tokens, qkv_weight[:, :HALF]) + half_of(query_bias)) * 0.125).astype(BF)
    queries = row_major(queries.reshape(streams, chip_rows, HALF))
    key_value_bias = jnp.concatenate([jnp.zeros((1, HALF), F32), half_of(value_bias)], axis=1)
    key_values = (nn(flat_all, qkv_weight[:, HALF:]) + key_value_bias).astype(BF)
    key_values = row_major(key_values.reshape(streams, -1, D))
    last = gather_dp_rest(tied(last, key_values), dps)
    attended, lse = attend(query_ids, key_ids, queries, key_values)
    other_attended = swap(attended).reshape(rows, HALF)
    attended = attended.reshape(rows, HALF)

    out_weight, expand_weight = local_copies(
        place,
        late,
        [(dps, zs, 2, block, D), (dps, zs, 2, block, UNITS)],
        gather_plan([(0, D, 0), (D, UNITS, 1)]),
        "place_late",
    )
    out_weight = out_weight.reshape(D, D)
    expand_weight = expand_weight.reshape(D, UNITS)
    (reduce_weight,) = local_copies(
        place, last, [(dps, zs, wide, D)], gather_plan([(0, D, 0)]), "place_last"
    )
    reduce_weight = reduce_weight.reshape(UNITS, D)

    def own(value):
        value = value.reshape(streams, chip_rows, -1)
        return lax.dynamic_slice_in_dim(value, core * row_count, row_count, 1)

    normed_one, inverse_one, first_low, hidden, slope = over_rows(
        middle_kernel,
        place,
        [attended, other_attended, chip_tokens],
        [small, expand_bias, out_weight, expand_weight],
        [(D, F32), (128, F32), (D, BF), (UNITS, BF), (UNITS, BF)],
        [],
        "middle",
        rows * D * (D + UNITS),
    )
    partial = nn(hidden, reduce_weight)
    activations, residual_two_back, reduced_back, expanded_back, next_partial, sums_two, unit_sums = over_rows(
        turn_kernel,
        None,
        [partial, swap(partial), normed_one, cotangent.reshape(rows, D), slope],
        [small, reduce_weight, expand_weight],
        [(D, BF), (D, F32), (D, BF), (UNITS, BF), (D, F32)],
        [(3, 8, D), (8, UNITS)],
        "turn",
        2 * rows * D * UNITS,
    )
    reduce_bias_grad, second_gain_grad, second_shift_grad = jnp.sum(sums_two, axis=1)
    expand_bias_grad = jnp.sum(unit_sums, axis=0)
    came_partial = swap(next_partial)
    reduce_weight_grad = tn(hidden, reduced_back).astype(BF)
    expand_weight_grad = tn(first_low, expanded_back).astype(BF)

    def scatter_plan(parts, lanes):
        slots, counts = scatter_slots(dps, zs)
        plan = [
            (
                source,
                lambda dp, z, j=j, k=k, index=index: index(dp ^ k, z ^ j),
                array,
                lambda dp, z, row=row, first=first, count=count: (
                    row,
                    slice(None),
                    at_lanes(first, count),
                ),
            )
            for (k, j), (array, row) in slots.items()
            for source, index, first, count in parts
        ]
        return [(count, both, lanes) for count in counts], plan

    wide_packs = local_copies(
        place,
        [
            reduce_weight_grad.reshape(dps, zs, 2, both, D),
            expand_weight_grad.reshape(dps, zs, both, UNITS),
        ],
        *scatter_plan(
            [
                (0, lambda d, zz: (d, zz, 0), 0, D),
                (0, lambda d, zz: (d, zz, 1), D, D),
                (1, lambda d, zz: (d, zz), 2 * D, UNITS),
            ],
            2 * D + UNITS,
        ),
        "pack_wide",
    )

    wide_came = scatter_dp_first(wide_packs, dps)

    residual_one_back, branch_back, attended_back, sums_one = over_rows(
        first_back_kernel,
        place,
        [next_partial, came_partial, residual_two_back, normed_one, inverse_one],
        [small, out_weight],
        [(D, F32), (D, BF), (HALF, BF)],
        [(3, 8, D)],
        "first_back",
        rows * D * HALF,
    )
    out_bias_grad, first_gain_grad, first_shift_grad = jnp.sum(sums_one, axis=1)
    attended_back = attended_back.reshape(streams, chip_rows, HALF)

    query_back, key_back, value_back = attend_back(
        query_ids, key_ids, queries, key_values, lse, attended_back
    )
    flat_query_back = query_back.reshape(rows, HALF)
    key_back = key_back.reshape(-1, HALF)
    value_back = value_back.reshape(-1, HALF)

    tokens_part = nt(key_back, qkv_weight[:, HALF : 2 * HALF]) + nt(value_back, qkv_weight[:, 2 * HALF :])
    tokens_part = tokens_part.astype(BF).reshape(streams, -1, D)
    tokens_total = lax.psum_scatter(tokens_part, "seq", scatter_dimension=1, tiled=True)
    wide_came = tied(wide_came, tokens_part)
    wide_onward = scatter_dp_middle(wide_packs, wide_came, dps)
    key_back, value_back, flat_query_back, out_side = tied(
        (key_back, value_back, flat_query_back, half_of(branch_back)), wide_onward
    )
    key_weight_grad = tn(flat_all, key_back).astype(BF)
    value_weight_grad = tn(flat_all, value_back).astype(BF)
    query_weight_grad = tn(chip_tokens, flat_query_back).astype(BF)
    out_weight_grad = in_core_order(tn(attended, out_side), tn(other_attended, out_side), 0).astype(BF)
    half_sums = jnp.stack([column_sum(flat_query_back), column_sum(value_back)])
    full_sums = in_core_order(half_sums, swap(half_sums), 1)
    small_grads = jnp.concatenate(
        [
            full_sums,
            jnp.stack(
                [
                    out_bias_grad,
                    first_gain_grad,
                    first_shift_grad,
                    reduce_bias_grad,
                    second_gain_grad,
                    second_shift_grad,
                ]
            ),
            expand_bias_grad.reshape(chips, 2, both).transpose(1, 0, 2).reshape(2, D),
        ],
        axis=0,
    ).T.astype(BF)
    small_grads = jnp.pad(small_grads, ((0, 0), (0, 128 - small_grads.shape[1])))
    four = (query_weight_grad, key_weight_grad, value_weight_grad, out_weight_grad)
    wide_totals = scatter_dp_rest(wide_packs, wide_came, wide_onward, dps)
    four = tied(four, wide_totals)
    narrow_packs = local_copies(
        place,
        [g.reshape(dps, zs, both, HALF) for g in four] + [small_grads.reshape(dps, zs, both, 128)],
        *scatter_plan(
            [(i, lambda d, zz: (d, zz), i * HALF, HALF) for i in range(4)]
            + [(4, lambda d, zz: (d, zz), 4 * HALF, 128)],
            4 * HALF + 128,
        ),
        "pack_narrow",
    )
    came = tied(scatter_dp_first(narrow_packs, dps), wide_totals)
    narrow_onward = scatter_dp_middle(narrow_packs, came, dps)
    wide_grads = scatter_z(wide_totals, seq, lambda moved: tied(moved, narrow_onward))
    narrow_totals = scatter_dp_rest(
        narrow_packs, came, narrow_onward, dps, lambda came: tied(came, wide_grads, tokens_total)
    )
    narrow_grads = scatter_z(narrow_totals, seq)
    query_part = nt(flat_query_back, qkv_weight[:, :HALF]).astype(BF)
    query_part = own(query_part).astype(F32) + own(swap(query_part)).astype(F32)
    tokens_gradient = own(residual_one_back) + query_part + tokens_total.astype(F32)

    def own_rows(grads):
        split = grads.reshape(2, block, grads.shape[1])
        mine = lax.dynamic_index_in_dim(split, core, 0, keepdims=False)
        return mine, swap(lax.dynamic_index_in_dim(split, 1 - core, 0, keepdims=False))

    mine, other = own_rows(narrow_grads[:, : 4 * HALF])
    matrices = [
        in_core_order(mine[:, i * HALF : (i + 1) * HALF], other[:, i * HALF : (i + 1) * HALF], 1)
        for i in range(4)
    ]
    small = narrow_grads[:, 4 * HALF :]
    own_small = lax.dynamic_slice_in_dim(small, core * block, block, 0).T
    expand_bias_grad = small[:, 8:10].T.reshape(wide)
    mine, other = own_rows(wide_grads[:, 2 * D :])
    expand_grads = in_core_order(
        mine.reshape(block, chips, 1, wide), other.reshape(block, chips, 1, wide), 2
    ).reshape(block, FF)
    reduce_grads = jnp.concatenate([wide_grads[:, :D], wide_grads[:, D : 2 * D]], axis=0)

    return (
        own(activations),
        tokens_gradient,
        matrices[0],
        own_small[0],
        matrices[1],
        matrices[2],
        own_small[1],
        matrices[3],
        own_small[2],
        own_small[3],
        own_small[4],
        expand_grads,
        expand_bias_grad,
        reduce_grads,
        own_small[5],
        own_small[6],
        own_small[7],
    )


def solution(mesh):
    sharded = ("dp", "seq")
    matrix = P(sharded, None)
    vector = P(sharded)
    token = P("dp", "seq", None)
    params = (
        matrix,
        vector,
        matrix,
        matrix,
        vector,
        matrix,
        vector,
        vector,
        vector,
        matrix,
        vector,
        matrix,
        vector,
        vector,
        vector,
    )
    return jax.shard_map(
        functools.partial(body, dps=mesh.shape["dp"], seq=mesh.shape["seq"]),
        mesh=mesh,
        in_specs=(token,) + params + (P("dp", None), token),
        out_specs=(token, token) + params,
        check_vma=False,
    )
```

```python
import functools

import jax
import jax.numpy as jnp
from jax import lax
from jax.experimental.layout import Layout, with_layout_constraint
from jax.experimental import pallas as pl
from jax.experimental.pallas import tpu as pltpu
from jax.sharding import PartitionSpec as P

D = 768
HEADS = 12
HD = 64
FF = 3072
HALF = D // 2
UNITS = FF // 2
PAIR = 2 * HD
PAIRS = HALF // PAIR
NEGATIVE = -1e30
EPSILON = 1e-12
BF = jnp.bfloat16
F32 = jnp.float32
VMEM_LIMIT = 28 * 1024 * 1024
VMEM_LARGE = 56 * 1024 * 1024
QUICK = pl.CostEstimate(flops=0, bytes_accessed=0, transcendentals=0)


def nn(left, right):
    return lax.dot_general(left, right, (((1,), (0,)), ((), ())), preferred_element_type=F32)


def nt(left, right):
    return lax.dot_general(left, right, (((1,), (1,)), ((), ())), preferred_element_type=F32)


def tn(left, right):
    return lax.dot_general(left, right, (((0,), (0,)), ((), ())), preferred_element_type=F32)


def local_copies(place, sources, shapes, plan, name, late=()):
    def kernel(place_ref, *refs):
        ins = refs[: len(sources)]
        outs = refs[len(sources) + len(late) :]
        dp = place_ref[0]
        z = place_ref[1]
        for source, source_index, target, target_index in plan:
            outs[target][target_index(dp, z)] = ins[source][source_index(dp, z)]

    moved = 2 * sum(functools.reduce(lambda a, b: a * b, s) for s in shapes)
    return pl.pallas_call(
        kernel,
        in_specs=[pl.BlockSpec(memory_space=pltpu.SMEM)]
        + [pl.BlockSpec(memory_space=pltpu.VMEM)] * len(sources)
        + [pl.BlockSpec(memory_space=pl.ANY)] * len(late),
        out_specs=[pl.BlockSpec(memory_space=pltpu.VMEM)] * len(shapes),
        out_shape=[jax.ShapeDtypeStruct(shape, BF) for shape in shapes],
        compiler_params=pltpu.CompilerParams(vmem_limit_bytes=VMEM_LIMIT),
        cost_estimate=QUICK,
        name=name,
    )(place, *sources, *late)


def first_columns(place, weights, vectors):
    block = weights[0].shape[0]
    lanes = len(weights) * HALF + 128

    def kernel(place_ref, *refs):
        ins, (mine_ref, theirs_ref, square_ref) = refs[: len(weights) + len(vectors)], refs[-3:]
        core = place_ref[2]
        square_ref[...] = jnp.zeros_like(square_ref)
        row = 0
        for ref in ins[len(weights) :]:
            for part in range(ref.shape[0] // block):
                square_ref[row : row + 1, 0:block] = ref[part * block : (part + 1) * block].reshape(1, block)
                row += 1
        columns = square_ref[...].T[:block].astype(BF)
        for out, side in ((mine_ref, core), (theirs_ref, 1 - core)):
            for i in range(len(weights)):
                picked = ins[i][:, pl.ds(pl.multiple_of(side * HALF, 128), HALF)]
                out[:, i * HALF : (i + 1) * HALF] = picked.astype(BF)
            out[:, len(weights) * HALF :] = columns

    shape = jax.ShapeDtypeStruct((block, lanes), BF)
    return pl.pallas_call(
        kernel,
        in_specs=[pl.BlockSpec(memory_space=pltpu.SMEM)]
        + [pl.BlockSpec(memory_space=pltpu.VMEM)] * (len(weights) + len(vectors)),
        out_specs=[pl.BlockSpec(memory_space=pltpu.VMEM)] * 2,
        out_shape=[shape, shape],
        scratch_shapes=[pltpu.VMEM((128, 128), F32)],
        name="first_columns",
    )(place, *weights, *vectors)


def at_lanes(start, count):
    return pl.ds(start, count)


def core_swap(value, seq):
    return lax.ppermute(value, "seq", [(i, i ^ 1) for i in range(seq)])


def z_move(value, step, seq):
    return lax.ppermute(value, "seq", [(i, i ^ (2 * step)) for i in range(seq)])


def dp_move(value, step, dps):
    return lax.ppermute(value, "dp", [(i, i ^ step) for i in range(dps)])


def tied(value, *others):
    return lax.optimization_barrier((value, others))[0]


def z_moves(value, seq):
    return [value] + [z_move(value, j, seq) for j in range(1, seq // 2)]


def gather_dp_direct(value, dps):
    return [value] + [dp_move(value, k, dps) for k in range(1, dps)]


def gather_dp_first(value, dps):
    return [value] + [dp_move(value, k, dps) for k in range(1, 3 if dps == 4 else dps)]


def gather_dp_rest(blocks, dps):
    if dps != 4:
        return blocks
    half = blocks[0].shape[0] // 2
    return blocks + [dp_move(blocks[2][:half], 1, dps), dp_move(blocks[1][half:], 2, dps)]


def dp_pieces(dps, zs, direct):
    half = zs // 2
    for k in range(dps):
        for j in range(zs):
            if dps == 4 and k == 3 and not direct:
                yield (3, j, k, j) if j < half else (4, j - half, k, j)
            else:
                yield k, j, k, j


def scatter_slots(dps, zs):
    if dps != 4:
        return {(k, j): (k, j) for k in range(dps) for j in range(zs)}, [zs] * dps
    half = zs // 2
    slots = {}
    for j in range(half):
        low, high = j, half + j
        slots[0, low], slots[0, high] = (0, low), (0, high)
        slots[1, low], slots[3, low] = (1, low), (1, half + j)
        slots[2, high], slots[3, high] = (2, j), (2, half + j)
        slots[1, high] = (3, j)
        slots[2, low] = (4, j)
    return slots, [zs, zs, zs, half, half]


def wide_sum(terms):
    return functools.reduce(jnp.add, [t.astype(F32) for t in terms])


def scatter_dp_first(packs, dps):
    if dps != 4:
        return [dp_move(packs[k], k, dps) for k in range(1, dps)]
    return [dp_move(packs[1], 1, dps), dp_move(packs[2], 2, dps)]


def scatter_dp_middle(packs, came, dps):
    if dps != 4:
        return []
    half = packs[3].shape[0]
    return [
        wide_sum([packs[4], came[0][half:]]).astype(BF),
        wide_sum([packs[3], came[1][half:]]).astype(BF),
    ]


def scatter_dp_rest(packs, came, onward, dps, tie=lambda came: came):
    if dps != 4:
        came = tie(came)
        return [wide_sum([packs[0][j]] + [c[j] for c in came]) for j in range(packs[0].shape[0])]
    half = packs[3].shape[0]
    again_two, again_one = tie([dp_move(onward[0], 2, dps), dp_move(onward[1], 1, dps)])
    low = [wide_sum([packs[0][j], came[0][j], again_two[j]]) for j in range(half)]
    return low + [wide_sum([packs[0][half + j], came[1][j], again_one[j]]) for j in range(half)]


def scatter_z(totals, seq, tie=lambda moved: moved):
    moved = tie([z_move(totals[j].astype(BF), j, seq) for j in range(1, seq // 2)])
    return wide_sum([totals[0]] + moved)


def stacked_heads(pair_rows):
    lanes = lax.broadcasted_iota(jnp.int32, pair_rows.shape, 1)
    zero = jnp.zeros_like(pair_rows)
    return jnp.concatenate(
        [jnp.where(lanes < HD, pair_rows, zero), jnp.where(lanes < HD, zero, pair_rows)], axis=0
    )


def unstacked_heads(stacked):
    rows = stacked.shape[0] // 2
    lanes = lax.broadcasted_iota(jnp.int32, (rows, PAIR), 1)
    return jnp.where(lanes < HD, stacked[:rows], stacked[rows:])


def masked_scores(queries, keys, query_ids, key_ids):
    rows = query_ids.shape[0]
    bias = jnp.where(query_ids == key_ids, 0.0, NEGATIVE)
    scores = nt(queries, keys)
    return jnp.concatenate([scores[:rows] + bias, scores[rows:] + bias], axis=0)


def forward_kernel(qid_ref, kid_ref, q_ref, k_ref, v_ref, out_ref, lse_ref):
    keys = k_ref[0]
    values = v_ref[0]
    rows = q_ref.shape[1] // 2
    for side in range(2):
        span = slice(side * rows, (side + 1) * rows)
        queries = stacked_heads(q_ref[0, span])
        scores = masked_scores(queries, keys, qid_ref[0, span][:, :1], kid_ref[0][:1, :])
        highest = jnp.max(scores, axis=-1, keepdims=True)
        weights = jnp.exp(scores - highest)
        total = jnp.sum(weights, axis=-1, keepdims=True)
        probs = (weights * (1.0 / total)).astype(BF)
        out_ref[0, span] = unstacked_heads(nn(probs, values)).astype(BF)
        lse_ref[0, 0, side] = jnp.broadcast_to(highest + jnp.log(total), lse_ref.shape[3:])


def backward_kernel(
    qid_ref, kid_ref, q_ref, k_ref, v_ref, lse_ref, up_ref, dq_ref, dk_ref, dv_ref
):
    keys = k_ref[0]
    values = v_ref[0]
    rows = q_ref.shape[1] // 2
    key_sum, value_sum = 0.0, 0.0
    for side in range(2):
        span = slice(side * rows, (side + 1) * rows)
        queries = stacked_heads(q_ref[0, span])
        upward = stacked_heads(up_ref[0, span])
        scores = masked_scores(queries, keys, qid_ref[0, span][:, :1], kid_ref[0][:1, :])
        probs = jnp.exp(scores - lse_ref[0, 0, side][:, :1])
        dprobs = nt(upward, values)
        correction = jnp.sum(probs * dprobs, axis=-1, keepdims=True)
        dscores = (probs * (dprobs - correction)).astype(BF)
        back = unstacked_heads(nn(dscores, keys)).astype(BF).astype(F32)
        dq_ref[0, span] = (back * 0.125).astype(BF)
        key_sum += tn(dscores, queries)
        value_sum += tn(probs.astype(BF), upward)
    dk_ref[0] = key_sum.astype(BF)
    dv_ref[0] = value_sum.astype(BF)


def attention_specs(rows, count):
    return dict(
        qid=pl.BlockSpec((1, rows, 128), lambda s, p: (s, 0, 0)),
        kid=pl.BlockSpec((1, 8, count), lambda s, p: (s, 0, 0)),
        row=pl.BlockSpec((1, rows, PAIR), lambda s, p: (s, 0, p)),
        key=pl.BlockSpec((1, count, PAIR), lambda s, p: (s, 0, p)),
        value=pl.BlockSpec((1, count, PAIR), lambda s, p: (s, 0, PAIRS + p)),
        lse=pl.BlockSpec((1, 1, 2, rows, 128), lambda s, p: (s, p, 0, 0, 0)),
    )


def attend(query_ids, key_ids, queries, key_values):
    streams, rows, _ = queries.shape
    count = key_values.shape[1]
    specs = attention_specs(rows, count)
    macs = streams * 2 * PAIRS * rows * count * HD
    return pl.pallas_call(
        forward_kernel,
        grid=(streams, PAIRS),
        in_specs=[specs["qid"], specs["kid"], specs["row"], specs["key"], specs["value"]],
        out_specs=[specs["row"], specs["lse"]],
        out_shape=[
            jax.ShapeDtypeStruct((streams, rows, HALF), BF),
            jax.ShapeDtypeStruct((streams, PAIRS, 2, rows, 128), F32),
        ],
        compiler_params=pltpu.CompilerParams(vmem_limit_bytes=VMEM_LIMIT if count <= 1024 else VMEM_LARGE),
        cost_estimate=QUICK,
        name="attend",
    )(query_ids, key_ids, queries, key_values, key_values)


def attend_back(query_ids, key_ids, queries, key_values, lse, upward):
    streams, rows, _ = queries.shape
    count = key_values.shape[1]
    specs = attention_specs(rows, count)
    macs = streams * 2 * PAIRS * rows * count * HD
    key_shape = jax.ShapeDtypeStruct((streams, count, HALF), BF)
    return pl.pallas_call(
        backward_kernel,
        grid=(streams, PAIRS),
        in_specs=[
            specs["qid"],
            specs["kid"],
            specs["row"],
            specs["key"],
            specs["value"],
            specs["lse"],
            specs["row"],
        ],
        out_specs=[specs["row"], specs["key"], specs["key"]],
        out_shape=[jax.ShapeDtypeStruct((streams, rows, HALF), BF), key_shape, key_shape],
        compiler_params=pltpu.CompilerParams(vmem_limit_bytes=VMEM_LIMIT if count <= 1024 else VMEM_LARGE),
        cost_estimate=QUICK,
        name="attend_back",
    )(query_ids, key_ids, queries, key_values, key_values, lse, upward)


CHUNK = 384
QUERY_BIAS, VALUE_BIAS, OUT_BIAS, FIRST_GAIN, FIRST_SHIFT, REDUCE_BIAS, SECOND_GAIN, SECOND_SHIFT = range(8)


def norm_rows(value_rows):
    centre = jnp.mean(value_rows, axis=-1, keepdims=True)
    centred = value_rows - centre
    inverse = lax.rsqrt(jnp.mean(centred * centred, axis=-1, keepdims=True) + EPSILON)
    return (centred * inverse, inverse)


def norm_back(upward, normed, inverse):
    mean_up = jnp.mean(upward, axis=-1, keepdims=True)
    mean_cross = jnp.mean(upward * normed, axis=-1, keepdims=True)
    return inverse * (upward - mean_up - normed * mean_cross)


def add_rows(sum_ref, index, values):
    sum_ref[index] += jnp.sum(values.reshape(-1, 8, values.shape[1]), axis=0)


def vector_of(vec_ref, index):
    return vec_ref[index : index + 1, :]


def half_of_ref(place_ref):
    return pl.ds(pl.multiple_of(place_ref[2] * HALF, 128), HALF)


def other_half_of_ref(place_ref):
    return pl.ds(pl.multiple_of((1 - place_ref[2]) * HALF, 128), HALF)


def project_kernel(place_ref, tok_ref, vec_ref, weight_ref, pairs_ref, query_ref, rows_ref):
    half = half_of_ref(place_ref)
    pairs = nn(tok_ref[0], weight_ref[:, HALF:])
    pairs_ref[0, :, :HALF] = pairs[:, :HALF].astype(BF)
    pairs_ref[0, :, HALF:] = (pairs[:, HALF:] + vec_ref[VALUE_BIAS : VALUE_BIAS + 1, half]).astype(BF)
    chip_rows = rows_ref.shape[1]
    tiles = tok_ref.shape[1] // chip_rows

    @pl.when(pl.program_id(1) == place_ref[1] // tiles)
    def _():
        first = pl.multiple_of(place_ref[1] % tiles * chip_rows, chip_rows)
        tokens = tok_ref[0, pl.ds(first, chip_rows), :]
        queries = nn(tokens, weight_ref[:, :HALF]) + vec_ref[QUERY_BIAS : QUERY_BIAS + 1, half]
        query_ref[0] = (queries * 0.125).astype(BF)
        rows_ref[0] = tokens


def project(place, tokens, vectors, weight, chip_rows):
    streams, count, _ = tokens.shape
    shape = lambda rows, lanes: jax.ShapeDtypeStruct((streams, rows, lanes), BF)
    tile = 4 * chip_rows
    return pl.pallas_call(
        project_kernel,
        grid=(streams, count // tile),
        in_specs=[
            pl.BlockSpec(memory_space=pltpu.SMEM),
            pl.BlockSpec((1, tile, D), lambda s, t: (s, t, 0)),
            pl.BlockSpec(memory_space=pltpu.VMEM),
            pl.BlockSpec(memory_space=pltpu.VMEM),
        ],
        out_specs=[
            pl.BlockSpec((1, tile, D), lambda s, t: (s, t, 0)),
            pl.BlockSpec((1, chip_rows, HALF), lambda s, t: (s, 0, 0)),
            pl.BlockSpec((1, chip_rows, D), lambda s, t: (s, 0, 0)),
        ],
        out_shape=[shape(count, D), shape(chip_rows, HALF), shape(chip_rows, D)],
        compiler_params=pltpu.CompilerParams(vmem_limit_bytes=VMEM_LIMIT),
        cost_estimate=QUICK,
        name="project",
    )(place, tokens, vectors, weight)


def unproject_kernel(place_ref, query_ref, key_ref, value_ref, weight_ref, out_ref):
    back = jnp.concatenate([key_ref[0], value_ref[0]], axis=1)
    out_ref[0] = nt(back, weight_ref[:, HALF:]).astype(BF)
    chip_rows = query_ref.shape[1]
    tiles = out_ref.shape[1] // chip_rows

    @pl.when(pl.program_id(1) == place_ref[1] // tiles)
    def _():
        span = pl.ds(pl.multiple_of(place_ref[1] % tiles * chip_rows, chip_rows), chip_rows)
        own = jnp.concatenate([query_ref[0], key_ref[0, span, :], value_ref[0, span, :]], axis=1)
        out_ref[0, span, :] = nt(own, weight_ref[...]).astype(BF)


def unproject(place, query_back, key_back, value_back, weight):
    streams, count, _ = key_back.shape
    chip_rows = query_back.shape[1]
    tile = 4 * chip_rows
    block = lambda lanes: pl.BlockSpec((1, tile, lanes), lambda s, t: (s, t, 0))
    return pl.pallas_call(
        unproject_kernel,
        grid=(streams, count // tile),
        in_specs=[
            pl.BlockSpec(memory_space=pltpu.SMEM),
            pl.BlockSpec((1, chip_rows, HALF), lambda s, t: (s, 0, 0)),
            block(HALF),
            block(HALF),
            pl.BlockSpec(memory_space=pltpu.VMEM),
        ],
        out_specs=block(D),
        out_shape=jax.ShapeDtypeStruct((streams, count, D), BF),
        compiler_params=pltpu.CompilerParams(vmem_limit_bytes=VMEM_LIMIT),
        cost_estimate=QUICK,
        name="unproject",
    )(place, query_back, key_back, value_back, weight)


def middle_kernel(
    place_ref, mine_ref, other_ref, tok_ref, vec_ref, unit_ref, out_ref, expand_ref, reduce_ref,
    normed_ref, inverse_ref, low_ref, hidden_ref, slope_ref, part_ref, send_ref,
):
    branch = nn(mine_ref[...], out_ref[half_of_ref(place_ref), :])
    branch += nn(other_ref[...], out_ref[other_half_of_ref(place_ref), :])
    branch += vector_of(vec_ref, OUT_BIAS)
    normed, inverse = norm_rows(tok_ref[...].astype(F32) + branch)
    normed_ref[...] = normed
    inverse_ref[...] = jnp.broadcast_to(inverse, inverse_ref.shape)
    first = normed * vector_of(vec_ref, FIRST_GAIN) + vector_of(vec_ref, FIRST_SHIFT)
    low = first.astype(BF)
    low_ref[...] = low
    total = jnp.zeros(part_ref.shape, F32)
    for start in range(0, UNITS, CHUNK):
        span = slice(start, start + CHUNK)
        expanded = nn(low, expand_ref[:, span]) + unit_ref[:, span]
        share = 0.5 * (1.0 + lax.erf(expanded * (0.5**0.5)))
        hidden = (expanded * share).astype(BF)
        hidden_ref[:, span] = hidden
        bell = jnp.exp(-0.5 * expanded * expanded) * 0.3989422804014327
        slope_ref[:, span] = (share + expanded * bell).astype(BF)
        total += nn(hidden, reduce_ref[span, :])
    part_ref[...] = total
    send_ref[...] = total.astype(BF)


def turn_kernel(
    place_ref, part_ref, came_ref, normed_ref, mine_ref, other_ref, slope_ref, vec_ref, reduce_ref, expand_ref,
    act_ref, residual_ref, low_ref, back_ref, next_ref, send_ref, sum_ref, unit_sum_ref,
):
    @pl.when(pl.program_id(0) == 0)
    def _():
        sum_ref[...] = jnp.zeros_like(sum_ref)
        unit_sum_ref[...] = jnp.zeros_like(unit_sum_ref)

    core = place_ref[2]
    first = normed_ref[...] * vector_of(vec_ref, FIRST_GAIN) + vector_of(vec_ref, FIRST_SHIFT)
    reduced = part_ref[...] + came_ref[...].astype(F32) + vector_of(vec_ref, REDUCE_BIAS)
    normed, inverse = norm_rows(first + reduced)
    gain = vector_of(vec_ref, SECOND_GAIN)
    half = normed.shape[0] // 2
    mine = jnp.where(core == 0, normed[:half], normed[half:])
    act_ref[...] = (mine * gain + vector_of(vec_ref, SECOND_SHIFT)).astype(BF)
    mine, other = mine_ref[...].astype(F32), other_ref[...].astype(F32)
    upward = jnp.concatenate(
        [jnp.where(core == 0, mine, other), jnp.where(core == 0, other, mine)], axis=0
    )
    residual = norm_back(upward * gain, normed, inverse)
    low = residual.astype(BF)
    residual_ref[...] = residual
    low_ref[...] = low
    add_rows(sum_ref, 0, low.astype(F32))
    add_rows(sum_ref, 1, upward * normed)
    add_rows(sum_ref, 2, upward)
    total = jnp.zeros(next_ref.shape, F32)
    for start in range(0, UNITS, CHUNK):
        span = slice(start, start + CHUNK)
        back = (nt(low, reduce_ref[span, :]) * slope_ref[:, span].astype(F32)).astype(BF)
        back_ref[:, span] = back
        unit_sum_ref[:, span] += jnp.sum(back.astype(F32).reshape(-1, 8, CHUNK), axis=0)
        total += nt(back, expand_ref[:, span])
    next_ref[...] = total
    send_ref[...] = total.astype(BF)


def first_back_kernel(
    place_ref, part_ref, came_ref, residual_ref, normed_ref, inverse_ref, vec_ref, out_ref,
    back_ref, low_ref, attended_ref, sum_ref,
):
    @pl.when(pl.program_id(0) == 0)
    def _():
        sum_ref[...] = jnp.zeros_like(sum_ref)

    upward = part_ref[...] + came_ref[...].astype(F32) + residual_ref[...]
    normed = normed_ref[...]
    add_rows(sum_ref, 1, upward * normed)
    add_rows(sum_ref, 2, upward)
    back = norm_back(upward * vector_of(vec_ref, FIRST_GAIN), normed, inverse_ref[:, :1])
    low = back.astype(BF)
    half = back.shape[0] // 2
    back_ref[...] = jnp.where(place_ref[2] == 0, back[:half], back[half:])
    low_ref[...] = low
    add_rows(sum_ref, 0, low.astype(F32))
    attended_ref[...] = nt(low, out_ref[half_of_ref(place_ref), :]).astype(BF)


def over_rows(kernel, place, steps, tiled, whole, outs, sums, name):
    tile = lambda shape: pl.BlockSpec((shape[0] // steps, shape[1]), lambda t: (t, 0))
    keep = lambda shape: pl.BlockSpec(shape, lambda t: (0,) * len(shape))
    return pl.pallas_call(
        kernel,
        grid=(steps,),
        in_specs=[pl.BlockSpec(memory_space=pltpu.SMEM)]
        + [tile(v.shape) for v in tiled]
        + [pl.BlockSpec(memory_space=pltpu.VMEM)] * len(whole),
        out_specs=[tile(out) for out in outs] + [keep(shape) for shape in sums],
        out_shape=[jax.ShapeDtypeStruct(out[:2], out[2]) for out in outs]
        + [jax.ShapeDtypeStruct(shape, F32) for shape in sums],
        compiler_params=pltpu.CompilerParams(vmem_limit_bytes=VMEM_LIMIT),
        cost_estimate=QUICK,
        name=name,
    )(place, *tiled, *whole)


def packed_call(kernel, place, sources, shapes, scratch, name):
    return pl.pallas_call(
        kernel,
        in_specs=[pl.BlockSpec(memory_space=pltpu.SMEM)]
        + [pl.BlockSpec(memory_space=pltpu.VMEM)] * len(sources),
        out_specs=[pl.BlockSpec(memory_space=pltpu.VMEM)] * len(shapes),
        out_shape=[jax.ShapeDtypeStruct(shape, BF) for shape in shapes],
        scratch_shapes=scratch,
        compiler_params=pltpu.CompilerParams(vmem_limit_bytes=VMEM_LIMIT),
        cost_estimate=QUICK,
        name=name,
    )(place, *sources)


def wide_packs_of(place, hidden, reduced_back, first_low, expanded_back, dps, zs):
    chips = dps * zs
    both, wide = D // chips, UNITS // chips
    slots, counts = scatter_slots(dps, zs)
    lanes = 2 * D + UNITS

    def kernel(place_ref, hidden_ref, reduced_ref, low_ref, expanded_ref, *refs):
        outs, (reduce_ref, expand_ref) = refs[: len(counts)], refs[len(counts) :]
        for start in range(0, UNITS, CHUNK):
            span = slice(start, start + CHUNK)
            reduce_ref[span, :] = tn(hidden_ref[:, span], reduced_ref[...]).astype(BF)
        for start in range(0, D, 256):
            span = slice(start, start + 256)
            expand_ref[span, :] = tn(low_ref[:, span], expanded_ref[...]).astype(BF)
        for (k, j), (array, row) in slots.items():
            chip = (place_ref[0] ^ k) * zs + (place_ref[1] ^ j)
            first = pl.multiple_of(chip * wide, 16)
            outs[array][row, :, :D] = reduce_ref[pl.ds(first, both), :]
            outs[array][row, :, D : 2 * D] = reduce_ref[pl.ds(pl.multiple_of(first + both, 16), both), :]
            outs[array][row, :, 2 * D :] = expand_ref[pl.ds(pl.multiple_of(chip * both, 16), both), :]

    return packed_call(
        kernel,
        place,
        [hidden, reduced_back, first_low, expanded_back],
        [(count, both, lanes) for count in counts],
        [pltpu.VMEM((UNITS, D), BF), pltpu.VMEM((D, UNITS), BF)],
        "wide_packs",
    )


def narrow_packs_of(place, tokens, chip_tokens, backs, mine, other, branch_back, sums, dps, zs):
    chips = dps * zs
    both = D // chips
    slots, counts = scatter_slots(dps, zs)
    lanes = 4 * HALF + 128
    query_back, key_back, value_back = backs

    def kernel(
        place_ref, tok_ref, chip_ref, query_ref, key_ref, value_ref, mine_ref, other_ref, branch_ref,
        one_ref, two_ref, unit_ref, *refs,
    ):
        outs, (all_ref, square_ref) = refs[: len(counts)], refs[len(counts) :]
        half = half_of_ref(place_ref)
        for start in range(0, D, 256):
            span = slice(start, start + 256)
            turned = tok_ref[:, span].T
            all_ref[span, :HALF] = tn(chip_ref[:, span], query_ref[...]).astype(BF)
            all_ref[span, HALF : 2 * HALF] = nn(turned, key_ref[...]).astype(BF)
            all_ref[span, 2 * HALF : 3 * HALF] = nn(turned, value_ref[...]).astype(BF)
        branch = branch_ref[:, half]
        all_ref[half, 3 * HALF : 4 * HALF] = tn(mine_ref[...], branch).astype(BF)
        all_ref[other_half_of_ref(place_ref), 3 * HALF : 4 * HALF] = tn(other_ref[...], branch).astype(BF)
        square_ref[...] = jnp.zeros_like(square_ref)
        for row, ref in ((0, query_ref), (1, value_ref)):
            square_ref[row : row + 1, half] = jnp.sum(ref[...].astype(F32), axis=0, keepdims=True)
        for i in range(3):
            square_ref[2 + i : 3 + i, :] = jnp.sum(one_ref[i], axis=0, keepdims=True)
            square_ref[5 + i : 6 + i, :] = jnp.sum(two_ref[i], axis=0, keepdims=True)
        unit = jnp.sum(unit_ref[...], axis=0, keepdims=True)
        for chip in range(chips):
            for h in range(2):
                first = (2 * chip + h) * both
                square_ref[8 + h : 9 + h, chip * both : (chip + 1) * both] = unit[:, first : first + both]
        all_ref[:, 4 * HALF :] = square_ref[...].T.astype(BF)
        for (k, j), (array, row) in slots.items():
            chip = (place_ref[0] ^ k) * zs + (place_ref[1] ^ j)
            outs[array][row] = all_ref[pl.ds(pl.multiple_of(chip * both, 16), both), :]

    return packed_call(
        kernel,
        place,
        [tokens, chip_tokens, query_back, key_back, value_back, mine, other, branch_back, *sums],
        [(count, both, lanes) for count in counts],
        [pltpu.VMEM((D, lanes), BF), pltpu.VMEM((128, D), F32)],
        "narrow_packs",
    )


def column_sum(value_rows):
    return jnp.sum(value_rows.astype(F32), axis=0)


def item_ids(lengths, places):
    items = lengths.shape[1]
    slot = jnp.arange(items, dtype=jnp.int32)
    ends = jnp.sum(jnp.where(slot[:, None] <= slot[None, :], lengths[:, :, None], 0), axis=1)
    return jnp.sum((ends[:, None, :] <= places[None, :, None]).astype(jnp.int32), axis=2)


def body(
    tokens,
    query_weight,
    query_bias,
    key_weight,
    value_weight,
    value_bias,
    out_weight,
    out_bias,
    first_gain,
    attention_norm_shift,
    expand_weight,
    expand_bias,
    reduce_weight,
    reduce_bias,
    second_gain,
    second_shift,
    lengths,
    cotangent,
    *,
    dps,
    seq,
):
    streams, row_count, _ = tokens.shape
    zs = seq // 2
    chips = dps * zs
    block = D // (2 * chips)
    both = 2 * block
    wide = FF // (2 * chips)
    chip_rows = 2 * row_count
    rows = streams * chip_rows
    dp = lax.axis_index("dp")
    z = lax.axis_index("seq") // 2
    core = lax.axis_index("seq") % 2
    place = jnp.stack([dp, z, core]).astype(jnp.int32)
    swap = functools.partial(core_swap, seq=seq)

    def row_major(value):
        return with_layout_constraint(value, Layout(major_to_minor=tuple(range(value.ndim))))

    def in_core_order(mine, other, axis):
        return jnp.where(
            core == 0,
            jnp.concatenate([mine, other], axis=axis),
            jnp.concatenate([other, mine], axis=axis),
        )

    mine, theirs = first_columns(
        place,
        (query_weight, key_weight, value_weight),
        (
            query_bias,
            value_bias,
            out_bias,
            first_gain,
            attention_norm_shift,
            reduce_bias,
            second_gain,
            second_shift,
            expand_bias,
        ),
    )
    early = in_core_order(mine[None], swap(theirs)[None], 0)

    out_weight = out_weight.astype(BF)
    units = expand_weight.astype(BF).reshape(block, chips, 2, wide)

    def columns_for(side):
        unit = lax.dynamic_index_in_dim(units, side, 2, keepdims=False).reshape(block, UNITS)
        return jnp.concatenate([out_weight, unit], axis=1)

    late = in_core_order(columns_for(core)[None], swap(columns_for(1 - core))[None], 0)
    early = jnp.stack(tied(z_moves(early, seq), late))
    late = z_moves(tied(late, early), seq)
    early, late = lax.optimization_barrier((gather_dp_first(early, dps), late))
    early = gather_dp_rest(early, dps)
    late = jnp.stack(late)
    all_tokens = row_major(lax.all_gather(tied(tokens, late), "seq", axis=1, tiled=True))
    last = z_moves(tied(reduce_weight.astype(BF), late), seq)
    late = gather_dp_rest(gather_dp_first(late, dps), dps)
    last = gather_dp_direct(jnp.stack(last), dps)
    other_cotangent = swap(cotangent).reshape(-1, D)
    cotangent = cotangent.reshape(-1, D)

    def gather_plan(parts, direct=False):
        return [
            (
                piece,
                lambda dp, z, row=row, first=first, count=count: (
                    row,
                    Ellipsis,
                    at_lanes(first, count),
                ),
                target,
                lambda dp, z, j=j, k=k: (dp ^ k, z ^ j),
            )
            for piece, row, k, j in dp_pieces(dps, zs, direct)
            for first, count, target in parts
        ]

    qkv_weight, small = local_copies(
        place,
        early,
        [(dps, zs, 2, block, 3 * HALF), (dps, zs, 2, block, 128)],
        gather_plan([(0, 3 * HALF, 0), (3 * HALF, 128, 1)]),
        "place_early",
    )
    qkv_weight = qkv_weight.reshape(D, 3 * HALF)
    small = small.astype(F32).reshape(D, 128)[:, :12].T
    expand_bias = small[8:12].reshape(4, chips, 2, block)
    expand_bias = lax.dynamic_index_in_dim(expand_bias, core, 2, keepdims=False)
    expand_bias = expand_bias.transpose(1, 0, 2).reshape(1, UNITS)

    def half_of(vector):
        return lax.dynamic_slice_in_dim(vector, core * HALF, HALF, 1)

    flat_all = all_tokens.reshape(-1, D)
    ids = item_ids(lengths, jnp.arange(all_tokens.shape[1], dtype=jnp.int32))
    key_ids = jnp.broadcast_to(ids[:, None, :], (streams, 8, ids.shape[1]))
    query_ids = lax.dynamic_slice_in_dim(ids, z * chip_rows, chip_rows, 1)
    query_ids = jnp.broadcast_to(query_ids[..., None], (streams, chip_rows, 128))

    key_values, queries, chip_tokens = project(place, all_tokens, small, qkv_weight, chip_rows)
    chip_tokens = chip_tokens.reshape(rows, D)
    attended, lse = attend(query_ids, key_ids, queries, key_values)
    other_attended = swap(attended).reshape(rows, HALF)
    attended = attended.reshape(rows, HALF)

    out_weight, expand_weight = local_copies(
        place,
        late,
        [(dps, zs, 2, block, D), (dps, zs, 2, block, UNITS)],
        gather_plan([(0, D, 0), (D, UNITS, 1)]),
        "place_late",
    )
    out_weight = out_weight.reshape(D, D)
    expand_weight = expand_weight.reshape(D, UNITS)
    (reduce_weight,) = local_copies(
        place, last, [(dps, zs, wide, D)], gather_plan([(0, D, 0)], direct=True), "place_last"
    )
    reduce_weight = reduce_weight.reshape(UNITS, D)

    normed_one, inverse_one, first_low, hidden, slope, partial, sent = over_rows(
        middle_kernel,
        place,
        streams,
        [attended, other_attended, chip_tokens],
        [small, expand_bias, out_weight, expand_weight, reduce_weight],
        [
            (rows, D, F32),
            (rows, 128, F32),
            (rows, D, BF),
            (rows, UNITS, BF),
            (rows, UNITS, BF),
            (rows, D, F32),
            (rows, D, BF),
        ],
        [],
        "middle",
    )
    activations, residual_two_back, reduced_back, expanded_back, partial, sent, sums_two, unit_sums = over_rows(
        turn_kernel,
        place,
        streams,
        [partial, swap(sent), normed_one, cotangent, other_cotangent, slope],
        [small, reduce_weight, expand_weight],
        [
            (rows // 2, D, BF),
            (rows, D, F32),
            (rows, D, BF),
            (rows, UNITS, BF),
            (rows, D, F32),
            (rows, D, BF),
        ],
        [(3, 8, D), (8, UNITS)],
        "turn",
    )
    came_partial = swap(sent)
    fused = both % 16 == 0

    def scatter_plan(parts, lanes):
        slots, counts = scatter_slots(dps, zs)
        plan = [
            (
                source,
                lambda dp, z, j=j, k=k, index=index: index(dp ^ k, z ^ j),
                array,
                lambda dp, z, row=row, first=first, count=count: (
                    row,
                    slice(None),
                    at_lanes(first, count),
                ),
            )
            for (k, j), (array, row) in slots.items()
            for source, index, first, count in parts
        ]
        return [(count, both, lanes) for count in counts], plan

    if fused:
        wide_packs = wide_packs_of(place, hidden, reduced_back, first_low, expanded_back, dps, zs)
    else:
        wide_packs = local_copies(
            place,
            [
                tn(hidden, reduced_back).astype(BF).reshape(dps, zs, 2, both, D),
                tn(first_low, expanded_back).astype(BF).reshape(dps, zs, both, UNITS),
            ],
            *scatter_plan(
                [
                    (0, lambda d, zz: (d, zz, 0), 0, D),
                    (0, lambda d, zz: (d, zz, 1), D, D),
                    (1, lambda d, zz: (d, zz), 2 * D, UNITS),
                ],
                2 * D + UNITS,
            ),
            "pack_wide",
        )
    wide_came = scatter_dp_first(wide_packs, dps)

    residual_one_back, branch_back, attended_back, sums_one = over_rows(
        first_back_kernel,
        place,
        streams,
        [partial, came_partial, residual_two_back, normed_one, inverse_one],
        [small, out_weight],
        [(rows // 2, D, F32), (rows, D, BF), (rows, HALF, BF)],
        [(3, 8, D)],
        "first_back",
    )
    attended_back = attended_back.reshape(streams, chip_rows, HALF)

    query_back, key_back, value_back = attend_back(
        query_ids, key_ids, queries, key_values, lse, attended_back
    )
    tokens_part = unproject(place, query_back, key_back, value_back, qkv_weight)
    tokens_total = lax.psum_scatter(tokens_part, "seq", scatter_dimension=1, tiled=True)
    wide_came = tied(wide_came, tokens_part)
    wide_onward = scatter_dp_middle(wide_packs, wide_came, dps)
    backs = (query_back.reshape(rows, HALF), key_back.reshape(-1, HALF), value_back.reshape(-1, HALF))
    backs = tied(backs, wide_onward)
    if fused:
        narrow_packs = narrow_packs_of(
            place,
            flat_all,
            chip_tokens,
            backs,
            attended,
            other_attended,
            branch_back,
            (sums_one, sums_two, unit_sums),
            dps,
            zs,
        )
        wide_totals = scatter_dp_rest(wide_packs, wide_came, wide_onward, dps)
    else:
        out_side = half_of(branch_back)
        zeros = jnp.zeros((D,), F32)
        small_grads = jnp.concatenate(
            [
                lax.dynamic_update_slice_in_dim(zeros, column_sum(backs[0]), core * HALF, 0)[None],
                lax.dynamic_update_slice_in_dim(zeros, column_sum(backs[2]), core * HALF, 0)[None],
                jnp.sum(sums_one, axis=1),
                jnp.sum(sums_two, axis=1),
                jnp.sum(unit_sums, axis=0).reshape(chips, 2, both).transpose(1, 0, 2).reshape(2, D),
            ],
            axis=0,
        ).T.astype(BF)
        small_grads = jnp.pad(small_grads, ((0, 0), (0, 128 - small_grads.shape[1])))
        four = (
            tn(chip_tokens, backs[0]).astype(BF),
            tn(flat_all, backs[1]).astype(BF),
            tn(flat_all, backs[2]).astype(BF),
            in_core_order(tn(attended, out_side), tn(other_attended, out_side), 0).astype(BF),
        )
        wide_totals = scatter_dp_rest(wide_packs, wide_came, wide_onward, dps)
        narrow_packs = local_copies(
            place,
            [g.reshape(dps, zs, both, HALF) for g in four] + [small_grads.reshape(dps, zs, both, 128)],
            *scatter_plan(
                [(i, lambda d, zz: (d, zz), i * HALF, HALF) for i in range(4)]
                + [(4, lambda d, zz: (d, zz), 4 * HALF, 128)],
                4 * HALF + 128,
            ),
            "pack_narrow",
        )
    came = tied(scatter_dp_first(narrow_packs, dps), wide_totals)
    narrow_onward = scatter_dp_middle(narrow_packs, came, dps)
    wide_grads = scatter_z(wide_totals, seq, lambda moved: tied(moved, narrow_onward))
    narrow_totals = scatter_dp_rest(
        narrow_packs, came, narrow_onward, dps, lambda came: tied(came, wide_grads, tokens_total)
    )
    narrow_grads = scatter_z(narrow_totals, seq)
    tokens_gradient = residual_one_back.reshape(tokens.shape) + tokens_total.astype(F32)

    def own_rows(grads):
        split = grads.reshape(2, block, grads.shape[1])
        mine = lax.dynamic_index_in_dim(split, core, 0, keepdims=False)
        return mine, swap(lax.dynamic_index_in_dim(split, 1 - core, 0, keepdims=False))

    mine, other = own_rows(narrow_grads)
    matrices = [
        in_core_order(mine[:, i * HALF : (i + 1) * HALF], other[:, i * HALF : (i + 1) * HALF], 1)
        for i in range(4)
    ]
    small = narrow_grads[:, 4 * HALF :]
    own_small = mine[:, 4 * HALF :].T
    both_small = (mine[:, 4 * HALF : 4 * HALF + 2] + other[:, 4 * HALF : 4 * HALF + 2]).T
    expand_bias_grad = small[:, 8:10].T.reshape(wide)
    mine, other = own_rows(wide_grads[:, 2 * D :])
    expand_grads = in_core_order(
        mine.reshape(block, chips, 1, wide), other.reshape(block, chips, 1, wide), 2
    ).reshape(block, FF)
    reduce_grads = jnp.concatenate([wide_grads[:, :D], wide_grads[:, D : 2 * D]], axis=0)

    return (
        activations.reshape(tokens.shape),
        tokens_gradient,
        matrices[0],
        both_small[0],
        matrices[1],
        matrices[2],
        both_small[1],
        matrices[3],
        own_small[2],
        own_small[3],
        own_small[4],
        expand_grads,
        expand_bias_grad,
        reduce_grads,
        own_small[5],
        own_small[6],
        own_small[7],
    )


def solution(mesh):
    sharded = ("dp", "seq")
    matrix = P(sharded, None)
    vector = P(sharded)
    token = P("dp", "seq", None)
    params = (
        matrix,
        vector,
        matrix,
        matrix,
        vector,
        matrix,
        vector,
        vector,
        vector,
        matrix,
        vector,
        matrix,
        vector,
        vector,
        vector,
    )
    return jax.shard_map(
        functools.partial(body, dps=mesh.shape["dp"], seq=mesh.shape["seq"]),
        mesh=mesh,
        in_specs=(token,) + params + (P("dp", None), token),
        out_specs=(token, token) + params,
        check_vma=False,
    )
```

```python
import functools

import jax
import jax.numpy as jnp
from jax import lax
from jax.experimental.layout import Layout, with_layout_constraint
from jax.experimental import pallas as pl
from jax.experimental.pallas import tpu as pltpu
from jax.sharding import PartitionSpec as P

D = 768
HEADS = 12
HD = 64
FF = 3072
HALF = D // 2
UNITS = FF // 2
PAIR = 2 * HD
PAIRS = HALF // PAIR
NEGATIVE = -1e30
EPSILON = 1e-12
BF = jnp.bfloat16
F32 = jnp.float32
VMEM_LIMIT = 28 * 1024 * 1024
VMEM_LARGE = 56 * 1024 * 1024
QUICK = pl.CostEstimate(flops=0, bytes_accessed=0, transcendentals=0)


def nn(left, right):
    return lax.dot_general(left, right, (((1,), (0,)), ((), ())), preferred_element_type=F32)


def nt(left, right):
    return lax.dot_general(left, right, (((1,), (1,)), ((), ())), preferred_element_type=F32)


def tn(left, right):
    return lax.dot_general(left, right, (((0,), (0,)), ((), ())), preferred_element_type=F32)


def local_copies(place, sources, shapes, plan, name, late=()):
    def kernel(place_ref, *refs):
        ins = refs[: len(sources)]
        outs = refs[len(sources) + len(late) :]
        dp = place_ref[0]
        z = place_ref[1]
        for source, source_index, target, target_index in plan:
            outs[target][target_index(dp, z)] = ins[source][source_index(dp, z)]

    moved = 2 * sum(functools.reduce(lambda a, b: a * b, s) for s in shapes)
    return pl.pallas_call(
        kernel,
        in_specs=[pl.BlockSpec(memory_space=pltpu.SMEM)]
        + [pl.BlockSpec(memory_space=pltpu.VMEM)] * len(sources)
        + [pl.BlockSpec(memory_space=pl.ANY)] * len(late),
        out_specs=[pl.BlockSpec(memory_space=pltpu.VMEM)] * len(shapes),
        out_shape=[jax.ShapeDtypeStruct(shape, BF) for shape in shapes],
        compiler_params=pltpu.CompilerParams(vmem_limit_bytes=VMEM_LIMIT),
        cost_estimate=QUICK,
        name=name,
    )(place, *sources, *late)


def first_columns(place, weights, vectors):
    block = weights[0].shape[0]
    lanes = len(weights) * HALF + 128

    def kernel(place_ref, *refs):
        ins, (mine_ref, theirs_ref, square_ref) = refs[: len(weights) + len(vectors)], refs[-3:]
        core = place_ref[2]
        square_ref[...] = jnp.zeros_like(square_ref)
        row = 0
        for ref in ins[len(weights) :]:
            for part in range(ref.shape[0] // block):
                square_ref[row : row + 1, 0:block] = ref[part * block : (part + 1) * block].reshape(1, block)
                row += 1
        columns = square_ref[...].T[:block].astype(BF)
        for out, side in ((mine_ref, core), (theirs_ref, 1 - core)):
            for i in range(len(weights)):
                picked = ins[i][:, pl.ds(pl.multiple_of(side * HALF, 128), HALF)]
                out[:, i * HALF : (i + 1) * HALF] = picked.astype(BF)
            out[:, len(weights) * HALF :] = columns

    shape = jax.ShapeDtypeStruct((block, lanes), BF)
    return pl.pallas_call(
        kernel,
        in_specs=[pl.BlockSpec(memory_space=pltpu.SMEM)]
        + [pl.BlockSpec(memory_space=pltpu.VMEM)] * (len(weights) + len(vectors)),
        out_specs=[pl.BlockSpec(memory_space=pltpu.VMEM)] * 2,
        out_shape=[shape, shape],
        scratch_shapes=[pltpu.VMEM((128, 128), F32)],
        name="first_columns",
    )(place, *weights, *vectors)


def at_lanes(start, count):
    return pl.ds(start, count)


def core_swap(value, seq):
    return lax.ppermute(value, "seq", [(i, i ^ 1) for i in range(seq)])


def z_move(value, step, seq):
    return lax.ppermute(value, "seq", [(i, i ^ (2 * step)) for i in range(seq)])


def dp_move(value, step, dps):
    return lax.ppermute(value, "dp", [(i, i ^ step) for i in range(dps)])


def tied(value, *others):
    return lax.optimization_barrier((value, others))[0]


def z_moves(value, seq):
    return [value] + [z_move(value, j, seq) for j in range(1, seq // 2)]


def gather_dp_direct(value, dps):
    return [value] + [dp_move(value, k, dps) for k in range(1, dps)]


def gather_dp_first(value, dps):
    return [value] + [dp_move(value, k, dps) for k in range(1, 3 if dps == 4 else dps)]


def gather_dp_halves(blocks, dps):
    if dps != 4:
        return []
    half = blocks[0].shape[0] // 2
    return [blocks[2][:half], blocks[1][half:]]


def gather_dp_rest(blocks, halves):
    return blocks + [dp_move(half, step, 4) for step, half in enumerate(halves, 1)]


def dp_pieces(dps, zs, direct):
    half = zs // 2
    for k in range(dps):
        for j in range(zs):
            if dps == 4 and k == 3 and not direct:
                yield (3, j, k, j) if j < half else (4, j - half, k, j)
            else:
                yield k, j, k, j


def scatter_slots(dps, zs):
    if dps != 4:
        return {(k, j): (k, j) for k in range(dps) for j in range(zs)}, [zs] * dps
    half = zs // 2
    slots = {}
    for j in range(half):
        low, high = j, half + j
        slots[0, low], slots[0, high] = (0, low), (0, high)
        slots[1, low], slots[3, low] = (1, low), (1, half + j)
        slots[2, high], slots[3, high] = (2, j), (2, half + j)
        slots[1, high] = (3, j)
        slots[2, low] = (4, j)
    return slots, [zs, zs, zs, half, half]


def wide_sum(terms):
    return functools.reduce(jnp.add, [t.astype(F32) for t in terms])


def scatter_dp_first(packs, dps):
    if dps != 4:
        return [dp_move(packs[k], k, dps) for k in range(1, dps)]
    return [dp_move(packs[1], 1, dps), dp_move(packs[2], 2, dps)]


def scatter_dp_middle(packs, came, dps):
    if dps != 4:
        return []
    half = packs[3].shape[0]
    return [
        wide_sum([packs[4], came[0][half:]]).astype(BF),
        wide_sum([packs[3], came[1][half:]]).astype(BF),
    ]


def scatter_dp_rest(packs, came, onward, dps, tie=lambda came: came):
    if dps != 4:
        came = tie(came)
        return [wide_sum([packs[0][j]] + [c[j] for c in came]) for j in range(packs[0].shape[0])]
    half = packs[3].shape[0]
    again_two, again_one = tie([dp_move(onward[0], 2, dps), dp_move(onward[1], 1, dps)])
    low = [wide_sum([packs[0][j], came[0][j], again_two[j]]) for j in range(half)]
    return low + [wide_sum([packs[0][half + j], came[1][j], again_one[j]]) for j in range(half)]


def scatter_z(totals, seq, tie=lambda moved: moved):
    moved = tie([z_move(totals[j].astype(BF), j, seq) for j in range(1, seq // 2)])
    return wide_sum([totals[0]] + moved)


def stacked_heads(pair_rows):
    lanes = lax.broadcasted_iota(jnp.int32, pair_rows.shape, 1)
    zero = jnp.zeros_like(pair_rows)
    return jnp.concatenate(
        [jnp.where(lanes < HD, pair_rows, zero), jnp.where(lanes < HD, zero, pair_rows)], axis=0
    )


def unstacked_heads(stacked):
    rows = stacked.shape[0] // 2
    lanes = lax.broadcasted_iota(jnp.int32, (rows, PAIR), 1)
    return jnp.where(lanes < HD, stacked[:rows], stacked[rows:])


def masked_scores(queries, keys, query_ids, key_ids):
    rows = query_ids.shape[0]
    bias = jnp.where(query_ids == key_ids, 0.0, NEGATIVE)
    scores = nt(queries, keys)
    return jnp.concatenate([scores[:rows] + bias, scores[rows:] + bias], axis=0)


def forward_kernel(qid_ref, kid_ref, q_ref, k_ref, v_ref, out_ref, lse_ref):
    keys = k_ref[0]
    values = v_ref[0]
    rows = q_ref.shape[1] // 2
    for side in range(2):
        span = slice(side * rows, (side + 1) * rows)
        queries = stacked_heads(q_ref[0, span])
        scores = masked_scores(queries, keys, qid_ref[0, span][:, :1], kid_ref[0][:1, :])
        highest = jnp.max(scores, axis=-1, keepdims=True)
        weights = jnp.exp(scores - highest)
        total = jnp.sum(weights, axis=-1, keepdims=True)
        probs = (weights * (1.0 / total)).astype(BF)
        out_ref[0, span] = unstacked_heads(nn(probs, values)).astype(BF)
        lse_ref[0, 0, side] = jnp.broadcast_to(highest + jnp.log(total), lse_ref.shape[3:])


def backward_kernel(
    qid_ref, kid_ref, q_ref, k_ref, v_ref, lse_ref, up_ref, dq_ref, dk_ref, dv_ref
):
    keys = k_ref[0]
    values = v_ref[0]
    rows = q_ref.shape[1] // 2
    key_sum, value_sum = 0.0, 0.0
    for side in range(2):
        span = slice(side * rows, (side + 1) * rows)
        queries = stacked_heads(q_ref[0, span])
        upward = stacked_heads(up_ref[0, span])
        scores = masked_scores(queries, keys, qid_ref[0, span][:, :1], kid_ref[0][:1, :])
        probs = jnp.exp(scores - lse_ref[0, 0, side][:, :1])
        dprobs = nt(upward, values)
        correction = jnp.sum(probs * dprobs, axis=-1, keepdims=True)
        dscores = (probs * (dprobs - correction)).astype(BF)
        back = unstacked_heads(nn(dscores, keys)).astype(BF).astype(F32)
        dq_ref[0, span] = (back * 0.125).astype(BF)
        key_sum += tn(dscores, queries)
        value_sum += tn(probs.astype(BF), upward)
    dk_ref[0] = key_sum.astype(BF)
    dv_ref[0] = value_sum.astype(BF)


def attention_specs(rows, count):
    return dict(
        qid=pl.BlockSpec((1, rows, 128), lambda s, p: (s, 0, 0)),
        kid=pl.BlockSpec((1, 8, count), lambda s, p: (s, 0, 0)),
        row=pl.BlockSpec((1, rows, PAIR), lambda s, p: (s, 0, p)),
        key=pl.BlockSpec((1, count, PAIR), lambda s, p: (s, 0, p)),
        value=pl.BlockSpec((1, count, PAIR), lambda s, p: (s, 0, PAIRS + p)),
        lse=pl.BlockSpec((1, 1, 2, rows, 128), lambda s, p: (s, p, 0, 0, 0)),
    )


def attend(query_ids, key_ids, queries, key_values):
    streams, rows, _ = queries.shape
    count = key_values.shape[1]
    specs = attention_specs(rows, count)
    macs = streams * 2 * PAIRS * rows * count * HD
    return pl.pallas_call(
        forward_kernel,
        grid=(streams, PAIRS),
        in_specs=[specs["qid"], specs["kid"], specs["row"], specs["key"], specs["value"]],
        out_specs=[specs["row"], specs["lse"]],
        out_shape=[
            jax.ShapeDtypeStruct((streams, rows, HALF), BF),
            jax.ShapeDtypeStruct((streams, PAIRS, 2, rows, 128), F32),
        ],
        compiler_params=pltpu.CompilerParams(vmem_limit_bytes=VMEM_LIMIT if count <= 1024 else VMEM_LARGE),
        cost_estimate=QUICK,
        name="attend",
    )(query_ids, key_ids, queries, key_values, key_values)


def attend_back(query_ids, key_ids, queries, key_values, lse, upward):
    streams, rows, _ = queries.shape
    count = key_values.shape[1]
    specs = attention_specs(rows, count)
    macs = streams * 2 * PAIRS * rows * count * HD
    key_shape = jax.ShapeDtypeStruct((streams, count, HALF), BF)
    return pl.pallas_call(
        backward_kernel,
        grid=(streams, PAIRS),
        in_specs=[
            specs["qid"],
            specs["kid"],
            specs["row"],
            specs["key"],
            specs["value"],
            specs["lse"],
            specs["row"],
        ],
        out_specs=[specs["row"], specs["key"], specs["key"]],
        out_shape=[jax.ShapeDtypeStruct((streams, rows, HALF), BF), key_shape, key_shape],
        compiler_params=pltpu.CompilerParams(vmem_limit_bytes=VMEM_LIMIT if count <= 1024 else VMEM_LARGE),
        cost_estimate=QUICK,
        name="attend_back",
    )(query_ids, key_ids, queries, key_values, key_values, lse, upward)


CHUNK = 384
QUERY_BIAS, VALUE_BIAS, OUT_BIAS, FIRST_GAIN, FIRST_SHIFT, REDUCE_BIAS, SECOND_GAIN, SECOND_SHIFT = range(8)


def norm_rows(value_rows):
    centre = jnp.mean(value_rows, axis=-1, keepdims=True)
    centred = value_rows - centre
    inverse = lax.rsqrt(jnp.mean(centred * centred, axis=-1, keepdims=True) + EPSILON)
    return (centred * inverse, inverse)


def norm_back(upward, normed, inverse):
    mean_up = jnp.mean(upward, axis=-1, keepdims=True)
    mean_cross = jnp.mean(upward * normed, axis=-1, keepdims=True)
    return inverse * (upward - mean_up - normed * mean_cross)


def add_rows(sum_ref, index, values):
    sum_ref[index] += jnp.sum(values.reshape(-1, 8, values.shape[1]), axis=0)


def vector_of(vec_ref, index):
    return vec_ref[index : index + 1, :]


def half_of_ref(place_ref):
    return pl.ds(pl.multiple_of(place_ref[2] * HALF, 128), HALF)


def other_half_of_ref(place_ref):
    return pl.ds(pl.multiple_of((1 - place_ref[2]) * HALF, 128), HALF)


def project_kernel(place_ref, tok_ref, vec_ref, weight_ref, pairs_ref, query_ref, rows_ref):
    half = half_of_ref(place_ref)
    pairs = nn(tok_ref[0], weight_ref[:, HALF:])
    pairs_ref[0, :, :HALF] = pairs[:, :HALF].astype(BF)
    pairs_ref[0, :, HALF:] = (pairs[:, HALF:] + vec_ref[VALUE_BIAS : VALUE_BIAS + 1, half]).astype(BF)
    chip_rows = rows_ref.shape[1]
    tiles = tok_ref.shape[1] // chip_rows

    @pl.when(pl.program_id(1) == place_ref[1] // tiles)
    def _():
        first = pl.multiple_of(place_ref[1] % tiles * chip_rows, chip_rows)
        tokens = tok_ref[0, pl.ds(first, chip_rows), :]
        queries = nn(tokens, weight_ref[:, :HALF]) + vec_ref[QUERY_BIAS : QUERY_BIAS + 1, half]
        query_ref[0] = (queries * 0.125).astype(BF)
        rows_ref[0] = tokens


def project(place, tokens, vectors, weight, chip_rows):
    streams, count, _ = tokens.shape
    shape = lambda rows, lanes: jax.ShapeDtypeStruct((streams, rows, lanes), BF)
    tile = 4 * chip_rows
    return pl.pallas_call(
        project_kernel,
        grid=(streams, count // tile),
        in_specs=[
            pl.BlockSpec(memory_space=pltpu.SMEM),
            pl.BlockSpec((1, tile, D), lambda s, t: (s, t, 0)),
            pl.BlockSpec(memory_space=pltpu.VMEM),
            pl.BlockSpec(memory_space=pltpu.VMEM),
        ],
        out_specs=[
            pl.BlockSpec((1, tile, D), lambda s, t: (s, t, 0)),
            pl.BlockSpec((1, chip_rows, HALF), lambda s, t: (s, 0, 0)),
            pl.BlockSpec((1, chip_rows, D), lambda s, t: (s, 0, 0)),
        ],
        out_shape=[shape(count, D), shape(chip_rows, HALF), shape(chip_rows, D)],
        compiler_params=pltpu.CompilerParams(vmem_limit_bytes=VMEM_LIMIT),
        cost_estimate=QUICK,
        name="project",
    )(place, pltpu.with_memory_space_constraint(tokens, pltpu.HBM), vectors, weight)


def unproject_kernel(place_ref, query_ref, key_ref, value_ref, weight_ref, out_ref):
    back = jnp.concatenate([key_ref[0], value_ref[0]], axis=1)
    out_ref[0] = nt(back, weight_ref[:, HALF:]).astype(BF)
    chip_rows = query_ref.shape[1]
    tiles = out_ref.shape[1] // chip_rows

    @pl.when(pl.program_id(1) == place_ref[1] // tiles)
    def _():
        span = pl.ds(pl.multiple_of(place_ref[1] % tiles * chip_rows, chip_rows), chip_rows)
        own = jnp.concatenate([query_ref[0], key_ref[0, span, :], value_ref[0, span, :]], axis=1)
        out_ref[0, span, :] = nt(own, weight_ref[...]).astype(BF)


def unproject(place, query_back, key_back, value_back, weight):
    streams, count, _ = key_back.shape
    chip_rows = query_back.shape[1]
    tile = 4 * chip_rows
    block = lambda lanes: pl.BlockSpec((1, tile, lanes), lambda s, t: (s, t, 0))
    return pl.pallas_call(
        unproject_kernel,
        grid=(streams, count // tile),
        in_specs=[
            pl.BlockSpec(memory_space=pltpu.SMEM),
            pl.BlockSpec((1, chip_rows, HALF), lambda s, t: (s, 0, 0)),
            block(HALF),
            block(HALF),
            pl.BlockSpec(memory_space=pltpu.VMEM),
        ],
        out_specs=block(D),
        out_shape=pltpu.HBM((streams, count, D), BF),
        compiler_params=pltpu.CompilerParams(vmem_limit_bytes=VMEM_LIMIT),
        cost_estimate=QUICK,
        name="unproject",
    )(place, query_back, key_back, value_back, weight)


def middle_kernel(
    place_ref, mine_ref, other_ref, tok_ref, vec_ref, unit_ref, out_ref, expand_ref, reduce_ref,
    normed_ref, inverse_ref, low_ref, hidden_ref, slope_ref, part_ref, send_ref,
):
    branch = nn(mine_ref[...], out_ref[half_of_ref(place_ref), :])
    branch += nn(other_ref[...], out_ref[other_half_of_ref(place_ref), :])
    branch += vector_of(vec_ref, OUT_BIAS)
    normed, inverse = norm_rows(tok_ref[...].astype(F32) + branch)
    normed_ref[...] = normed
    inverse_ref[...] = jnp.broadcast_to(inverse, inverse_ref.shape)
    first = normed * vector_of(vec_ref, FIRST_GAIN) + vector_of(vec_ref, FIRST_SHIFT)
    low = first.astype(BF)
    low_ref[...] = low
    total = jnp.zeros(part_ref.shape, F32)
    for start in range(0, UNITS, CHUNK):
        span = slice(start, start + CHUNK)
        expanded = nn(low, expand_ref[:, span]) + unit_ref[:, span]
        share = 0.5 * (1.0 + lax.erf(expanded * (0.5**0.5)))
        hidden = (expanded * share).astype(BF)
        hidden_ref[:, span] = hidden
        bell = jnp.exp(-0.5 * expanded * expanded) * 0.3989422804014327
        slope_ref[:, span] = (share + expanded * bell).astype(BF)
        total += nn(hidden, reduce_ref[span, :])
    part_ref[...] = total
    send_ref[...] = total.astype(BF)


def turn_kernel(
    place_ref, part_ref, came_ref, normed_ref, mine_ref, other_ref, slope_ref, vec_ref, reduce_ref, expand_ref,
    act_ref, residual_ref, low_ref, back_ref, next_ref, send_ref, sum_ref, unit_sum_ref,
):
    core = place_ref[2]
    first = normed_ref[...] * vector_of(vec_ref, FIRST_GAIN) + vector_of(vec_ref, FIRST_SHIFT)
    reduced = part_ref[...] + came_ref[...].astype(F32) + vector_of(vec_ref, REDUCE_BIAS)
    normed, inverse = norm_rows(first + reduced)
    gain = vector_of(vec_ref, SECOND_GAIN)
    half = normed.shape[0] // 2
    mine = jnp.where(core == 0, normed[:half], normed[half:])
    act_ref[...] = (mine * gain + vector_of(vec_ref, SECOND_SHIFT)).astype(BF)
    mine, other = mine_ref[...].astype(F32), other_ref[...].astype(F32)
    upward = jnp.concatenate(
        [jnp.where(core == 0, mine, other), jnp.where(core == 0, other, mine)], axis=0
    )
    residual = norm_back(upward * gain, normed, inverse)
    low = residual.astype(BF)
    residual_ref[...] = residual
    low_ref[...] = low
    add_rows(sum_ref, 0, low.astype(F32))
    add_rows(sum_ref, 1, upward * normed)
    add_rows(sum_ref, 2, upward)
    total = jnp.zeros(next_ref.shape, F32)
    for start in range(0, UNITS, CHUNK):
        span = slice(start, start + CHUNK)
        back = (nt(low, reduce_ref[span, :]) * slope_ref[:, span].astype(F32)).astype(BF)
        back_ref[:, span] = back
        unit_sum_ref[:, span] += jnp.sum(back.astype(F32).reshape(-1, 8, CHUNK), axis=0)
        total += nt(back, expand_ref[:, span])
    next_ref[...] = total
    send_ref[...] = total.astype(BF)


def first_back_kernel(
    place_ref, part_ref, came_ref, residual_ref, normed_ref, inverse_ref, vec_ref, out_ref,
    back_ref, low_ref, attended_ref, sum_ref,
):
    upward = part_ref[...] + came_ref[...].astype(F32) + residual_ref[...]
    normed = normed_ref[...]
    add_rows(sum_ref, 1, upward * normed)
    add_rows(sum_ref, 2, upward)
    back = norm_back(upward * vector_of(vec_ref, FIRST_GAIN), normed, inverse_ref[:, :1])
    low = back.astype(BF)
    half = back.shape[0] // 2
    back_ref[...] = jnp.where(place_ref[2] == 0, back[:half], back[half:])
    low_ref[...] = low
    add_rows(sum_ref, 0, low.astype(F32))
    attended_ref[...] = nt(low, out_ref[half_of_ref(place_ref), :]).astype(BF)


def over_rows(body, place, steps, tiled, whole, outs, sums, name):
    def tile_of(ref, step):
        rows = ref.shape[0] // steps
        return ref.at[step * rows : (step + 1) * rows]

    def kernel(place_ref, *refs):
        tiles, refs = refs[: len(tiled)], refs[len(tiled) :]
        kept, refs = refs[: len(whole)], refs[len(whole) :]
        results, totals = refs[: len(outs)], refs[len(outs) :]
        for total in totals:
            total[...] = jnp.zeros_like(total)
        for step in range(steps):
            body(
                place_ref,
                *[tile_of(ref, step) for ref in tiles],
                *kept,
                *[tile_of(ref, step) for ref in results],
                *totals,
            )

    return pl.pallas_call(
        kernel,
        in_specs=[pl.BlockSpec(memory_space=pltpu.SMEM)]
        + [pl.BlockSpec(memory_space=pltpu.VMEM)] * (len(tiled) + len(whole)),
        out_specs=[pl.BlockSpec(memory_space=pltpu.VMEM)] * (len(outs) + len(sums)),
        out_shape=[jax.ShapeDtypeStruct(out[:2], out[2]) for out in outs]
        + [jax.ShapeDtypeStruct(shape, F32) for shape in sums],
        compiler_params=pltpu.CompilerParams(vmem_limit_bytes=VMEM_LIMIT),
        cost_estimate=QUICK,
        name=name,
    )(place, *tiled, *whole)


def packed_call(kernel, place, sources, shapes, scratch, name):
    return pl.pallas_call(
        kernel,
        in_specs=[pl.BlockSpec(memory_space=pltpu.SMEM)]
        + [pl.BlockSpec(memory_space=pltpu.VMEM)] * len(sources),
        out_specs=[pl.BlockSpec(memory_space=pltpu.VMEM)] * len(shapes),
        out_shape=[jax.ShapeDtypeStruct(shape, BF) for shape in shapes],
        scratch_shapes=scratch,
        compiler_params=pltpu.CompilerParams(vmem_limit_bytes=VMEM_LIMIT),
        cost_estimate=QUICK,
        name=name,
    )(place, *sources)


def wide_packs_of(place, hidden, reduced_back, first_low, expanded_back, dps, zs):
    chips = dps * zs
    both, wide = D // chips, UNITS // chips
    slots, counts = scatter_slots(dps, zs)
    lanes = 2 * D + UNITS

    def kernel(place_ref, hidden_ref, reduced_ref, low_ref, expanded_ref, *refs):
        outs, (reduce_ref, expand_ref) = refs[: len(counts)], refs[len(counts) :]
        for start in range(0, UNITS, CHUNK):
            span = slice(start, start + CHUNK)
            reduce_ref[span, :] = tn(hidden_ref[:, span], reduced_ref[...]).astype(BF)
        for start in range(0, D, 256):
            span = slice(start, start + 256)
            expand_ref[span, :] = tn(low_ref[:, span], expanded_ref[...]).astype(BF)
        for (k, j), (array, row) in slots.items():
            chip = (place_ref[0] ^ k) * zs + (place_ref[1] ^ j)
            first = pl.multiple_of(chip * wide, 16)
            outs[array][row, :, :D] = reduce_ref[pl.ds(first, both), :]
            outs[array][row, :, D : 2 * D] = reduce_ref[pl.ds(pl.multiple_of(first + both, 16), both), :]
            outs[array][row, :, 2 * D :] = expand_ref[pl.ds(pl.multiple_of(chip * both, 16), both), :]

    return packed_call(
        kernel,
        place,
        [hidden, reduced_back, first_low, expanded_back],
        [(count, both, lanes) for count in counts],
        [pltpu.VMEM((UNITS, D), BF), pltpu.VMEM((D, UNITS), BF)],
        "wide_packs",
    )


def narrow_packs_of(place, tokens, chip_tokens, backs, mine, other, branch_back, sums, dps, zs):
    chips = dps * zs
    both = D // chips
    slots, counts = scatter_slots(dps, zs)
    lanes = 4 * HALF + 128
    query_back, key_back, value_back = backs

    def kernel(
        place_ref, tok_ref, chip_ref, query_ref, key_ref, value_ref, mine_ref, other_ref, branch_ref,
        one_ref, two_ref, unit_ref, *refs,
    ):
        outs, (all_ref, square_ref) = refs[: len(counts)], refs[len(counts) :]
        half = half_of_ref(place_ref)
        for start in range(0, D, 256):
            span = slice(start, start + 256)
            turned = tok_ref[:, span].T
            all_ref[span, :HALF] = tn(chip_ref[:, span], query_ref[...]).astype(BF)
            all_ref[span, HALF : 2 * HALF] = nn(turned, key_ref[...]).astype(BF)
            all_ref[span, 2 * HALF : 3 * HALF] = nn(turned, value_ref[...]).astype(BF)
        branch = branch_ref[:, half]
        all_ref[half, 3 * HALF : 4 * HALF] = tn(mine_ref[...], branch).astype(BF)
        all_ref[other_half_of_ref(place_ref), 3 * HALF : 4 * HALF] = tn(other_ref[...], branch).astype(BF)
        square_ref[...] = jnp.zeros_like(square_ref)
        for row, ref in ((0, query_ref), (1, value_ref)):
            square_ref[row : row + 1, half] = jnp.sum(ref[...].astype(F32), axis=0, keepdims=True)
        for i in range(3):
            square_ref[2 + i : 3 + i, :] = jnp.sum(one_ref[i], axis=0, keepdims=True)
            square_ref[5 + i : 6 + i, :] = jnp.sum(two_ref[i], axis=0, keepdims=True)
        unit = jnp.sum(unit_ref[...], axis=0, keepdims=True)
        for chip in range(chips):
            for h in range(2):
                first = (2 * chip + h) * both
                square_ref[8 + h : 9 + h, chip * both : (chip + 1) * both] = unit[:, first : first + both]
        all_ref[:, 4 * HALF :] = square_ref[...].T.astype(BF)
        for (k, j), (array, row) in slots.items():
            chip = (place_ref[0] ^ k) * zs + (place_ref[1] ^ j)
            outs[array][row] = all_ref[pl.ds(pl.multiple_of(chip * both, 16), both), :]

    return packed_call(
        kernel,
        place,
        [tokens, chip_tokens, query_back, key_back, value_back, mine, other, branch_back, *sums],
        [(count, both, lanes) for count in counts],
        [pltpu.VMEM((D, lanes), BF), pltpu.VMEM((128, D), F32)],
        "narrow_packs",
    )


def column_sum(value_rows):
    return jnp.sum(value_rows.astype(F32), axis=0)


def item_ids(lengths, places):
    items = lengths.shape[1]
    slot = jnp.arange(items, dtype=jnp.int32)
    ends = jnp.sum(jnp.where(slot[:, None] <= slot[None, :], lengths[:, :, None], 0), axis=1)
    return jnp.sum((ends[:, None, :] <= places[None, :, None]).astype(jnp.int32), axis=2)


def body(
    tokens,
    query_weight,
    query_bias,
    key_weight,
    value_weight,
    value_bias,
    out_weight,
    out_bias,
    first_gain,
    attention_norm_shift,
    expand_weight,
    expand_bias,
    reduce_weight,
    reduce_bias,
    second_gain,
    second_shift,
    lengths,
    cotangent,
    *,
    dps,
    seq,
):
    streams, row_count, _ = tokens.shape
    zs = seq // 2
    chips = dps * zs
    block = D // (2 * chips)
    both = 2 * block
    wide = FF // (2 * chips)
    chip_rows = 2 * row_count
    rows = streams * chip_rows
    dp = lax.axis_index("dp")
    z = lax.axis_index("seq") // 2
    core = lax.axis_index("seq") % 2
    place = jnp.stack([dp, z, core]).astype(jnp.int32)
    swap = functools.partial(core_swap, seq=seq)

    def row_major(value):
        return with_layout_constraint(value, Layout(major_to_minor=tuple(range(value.ndim))))

    def in_core_order(mine, other, axis):
        return jnp.where(
            core == 0,
            jnp.concatenate([mine, other], axis=axis),
            jnp.concatenate([other, mine], axis=axis),
        )

    mine, theirs = first_columns(
        place,
        (query_weight, key_weight, value_weight),
        (
            query_bias,
            value_bias,
            out_bias,
            first_gain,
            attention_norm_shift,
            reduce_bias,
            second_gain,
            second_shift,
            expand_bias,
        ),
    )
    early = in_core_order(mine[None], swap(theirs)[None], 0)

    out_weight = out_weight.astype(BF)
    units = expand_weight.astype(BF).reshape(block, chips, 2, wide)

    def columns_for(side):
        unit = lax.dynamic_index_in_dim(units, side, 2, keepdims=False).reshape(block, UNITS)
        return jnp.concatenate([out_weight, unit], axis=1)

    late = in_core_order(columns_for(core)[None], swap(columns_for(1 - core))[None], 0)
    early = jnp.stack(tied(z_moves(early, seq), late))
    late = z_moves(tied(late, early), seq)
    early, late = lax.optimization_barrier((gather_dp_first(early, dps), late))
    all_tokens = row_major(lax.all_gather(tied(tokens, late), "seq", axis=1, tiled=True))
    early = gather_dp_rest(early, gather_dp_halves(early, dps))
    late = jnp.stack(tied(late, early))
    last = z_moves(tied(reduce_weight.astype(BF), late), seq)
    late = gather_dp_first(late, dps)
    other_cotangent = swap(cotangent).reshape(-1, D)
    cotangent = cotangent.reshape(-1, D)

    def gather_plan(parts, direct=False):
        return [
            (
                piece,
                lambda dp, z, row=row, first=first, count=count: (
                    row,
                    Ellipsis,
                    at_lanes(first, count),
                ),
                target,
                lambda dp, z, j=j, k=k: (dp ^ k, z ^ j),
            )
            for piece, row, k, j in dp_pieces(dps, zs, direct)
            for first, count, target in parts
        ]

    qkv_weight, small = local_copies(
        place,
        early,
        [(dps, zs, 2, block, 3 * HALF), (dps, zs, 2, block, 128)],
        gather_plan([(0, 3 * HALF, 0), (3 * HALF, 128, 1)]),
        "place_early",
    )
    qkv_weight = qkv_weight.reshape(D, 3 * HALF)
    small = small.astype(F32).reshape(D, 128)[:, :12].T
    expand_bias = small[8:12].reshape(4, chips, 2, block)
    expand_bias = lax.dynamic_index_in_dim(expand_bias, core, 2, keepdims=False)
    expand_bias = expand_bias.transpose(1, 0, 2).reshape(1, UNITS)

    def half_of(vector):
        return lax.dynamic_slice_in_dim(vector, core * HALF, HALF, 1)

    qkv_weight = tied(qkv_weight, expand_bias, other_cotangent)
    late = tied(late, qkv_weight)
    halves = gather_dp_halves(late, dps)
    late = gather_dp_rest(late, halves)
    last = gather_dp_direct(jnp.stack(tied(last, halves)), dps)

    flat_all = all_tokens.reshape(-1, D)
    ids = item_ids(lengths, jnp.arange(all_tokens.shape[1], dtype=jnp.int32))
    key_ids = jnp.broadcast_to(ids[:, None, :], (streams, 8, ids.shape[1]))
    query_ids = lax.dynamic_slice_in_dim(ids, z * chip_rows, chip_rows, 1)
    query_ids = jnp.broadcast_to(query_ids[..., None], (streams, chip_rows, 128))

    key_values, queries, chip_tokens = project(place, all_tokens, small, qkv_weight, chip_rows)
    queries = tied(queries, late)
    chip_tokens = chip_tokens.reshape(rows, D)
    attended, lse = attend(query_ids, key_ids, queries, key_values)
    other_attended = swap(attended).reshape(rows, HALF)
    attended = attended.reshape(rows, HALF)

    out_weight, expand_weight = local_copies(
        place,
        late,
        [(dps, zs, 2, block, D), (dps, zs, 2, block, UNITS)],
        gather_plan([(0, D, 0), (D, UNITS, 1)]),
        "place_late",
    )
    out_weight = out_weight.reshape(D, D)
    expand_weight = expand_weight.reshape(D, UNITS)
    (reduce_weight,) = local_copies(
        place, last, [(dps, zs, wide, D)], gather_plan([(0, D, 0)], direct=True), "place_last"
    )
    reduce_weight = reduce_weight.reshape(UNITS, D)

    normed_one, inverse_one, first_low, hidden, slope, partial, sent = over_rows(
        middle_kernel,
        place,
        streams,
        [attended, other_attended, chip_tokens],
        [small, expand_bias, out_weight, expand_weight, reduce_weight],
        [
            (rows, D, F32),
            (rows, 128, F32),
            (rows, D, BF),
            (rows, UNITS, BF),
            (rows, UNITS, BF),
            (rows, D, F32),
            (rows, D, BF),
        ],
        [],
        "middle",
    )
    activations, residual_two_back, reduced_back, expanded_back, partial, sent, sums_two, unit_sums = over_rows(
        turn_kernel,
        place,
        streams,
        [partial, swap(sent), normed_one, cotangent, other_cotangent, slope],
        [small, reduce_weight, expand_weight],
        [
            (rows // 2, D, BF),
            (rows, D, F32),
            (rows, D, BF),
            (rows, UNITS, BF),
            (rows, D, F32),
            (rows, D, BF),
        ],
        [(3, 8, D), (8, UNITS)],
        "turn",
    )
    came_partial = swap(sent)
    fused = both % 16 == 0

    def scatter_plan(parts, lanes):
        slots, counts = scatter_slots(dps, zs)
        plan = [
            (
                source,
                lambda dp, z, j=j, k=k, index=index: index(dp ^ k, z ^ j),
                array,
                lambda dp, z, row=row, first=first, count=count: (
                    row,
                    slice(None),
                    at_lanes(first, count),
                ),
            )
            for (k, j), (array, row) in slots.items()
            for source, index, first, count in parts
        ]
        return [(count, both, lanes) for count in counts], plan

    if fused:
        wide_packs = wide_packs_of(place, hidden, reduced_back, first_low, expanded_back, dps, zs)
    else:
        wide_packs = local_copies(
            place,
            [
                tn(hidden, reduced_back).astype(BF).reshape(dps, zs, 2, both, D),
                tn(first_low, expanded_back).astype(BF).reshape(dps, zs, both, UNITS),
            ],
            *scatter_plan(
                [
                    (0, lambda d, zz: (d, zz, 0), 0, D),
                    (0, lambda d, zz: (d, zz, 1), D, D),
                    (1, lambda d, zz: (d, zz), 2 * D, UNITS),
                ],
                2 * D + UNITS,
            ),
            "pack_wide",
        )
    wide_came = scatter_dp_first(wide_packs, dps)

    residual_one_back, branch_back, attended_back, sums_one = over_rows(
        first_back_kernel,
        place,
        streams,
        [partial, came_partial, residual_two_back, normed_one, inverse_one],
        [small, out_weight],
        [(rows // 2, D, F32), (rows, D, BF), (rows, HALF, BF)],
        [(3, 8, D)],
        "first_back",
    )
    attended_back = attended_back.reshape(streams, chip_rows, HALF)

    query_back, key_back, value_back = attend_back(
        query_ids, key_ids, queries, key_values, lse, attended_back
    )
    tokens_part = unproject(place, query_back, key_back, value_back, qkv_weight)
    tokens_total = lax.psum_scatter(tokens_part, "seq", scatter_dimension=1, tiled=True)
    wide_came = tied(wide_came, tokens_part)
    wide_onward = scatter_dp_middle(wide_packs, wide_came, dps)
    backs = (query_back.reshape(rows, HALF), key_back.reshape(-1, HALF), value_back.reshape(-1, HALF))
    backs = tied(backs, wide_onward)
    if fused:
        narrow_packs = narrow_packs_of(
            place,
            flat_all,
            chip_tokens,
            backs,
            attended,
            other_attended,
            branch_back,
            (sums_one, sums_two, unit_sums),
            dps,
            zs,
        )
        wide_totals = scatter_dp_rest(wide_packs, wide_came, wide_onward, dps)
    else:
        out_side = half_of(branch_back)
        zeros = jnp.zeros((D,), F32)
        small_grads = jnp.concatenate(
            [
                lax.dynamic_update_slice_in_dim(zeros, column_sum(backs[0]), core * HALF, 0)[None],
                lax.dynamic_update_slice_in_dim(zeros, column_sum(backs[2]), core * HALF, 0)[None],
                jnp.sum(sums_one, axis=1),
                jnp.sum(sums_two, axis=1),
                jnp.sum(unit_sums, axis=0).reshape(chips, 2, both).transpose(1, 0, 2).reshape(2, D),
            ],
            axis=0,
        ).T.astype(BF)
        small_grads = jnp.pad(small_grads, ((0, 0), (0, 128 - small_grads.shape[1])))
        four = (
            tn(chip_tokens, backs[0]).astype(BF),
            tn(flat_all, backs[1]).astype(BF),
            tn(flat_all, backs[2]).astype(BF),
            in_core_order(tn(attended, out_side), tn(other_attended, out_side), 0).astype(BF),
        )
        wide_totals = scatter_dp_rest(wide_packs, wide_came, wide_onward, dps)
        narrow_packs = local_copies(
            place,
            [g.reshape(dps, zs, both, HALF) for g in four] + [small_grads.reshape(dps, zs, both, 128)],
            *scatter_plan(
                [(i, lambda d, zz: (d, zz), i * HALF, HALF) for i in range(4)]
                + [(4, lambda d, zz: (d, zz), 4 * HALF, 128)],
                4 * HALF + 128,
            ),
            "pack_narrow",
        )
    came = tied(scatter_dp_first(narrow_packs, dps), wide_totals)
    narrow_onward = scatter_dp_middle(narrow_packs, came, dps)
    wide_grads = scatter_z(wide_totals, seq, lambda moved: tied(moved, narrow_onward))
    narrow_totals = scatter_dp_rest(
        narrow_packs, came, narrow_onward, dps, lambda came: tied(came, wide_grads, tokens_total)
    )
    narrow_grads = scatter_z(narrow_totals, seq)
    tokens_gradient = residual_one_back.reshape(tokens.shape) + tokens_total.astype(F32)

    def own_rows(grads):
        split = grads.reshape(2, block, grads.shape[1])
        mine = lax.dynamic_index_in_dim(split, core, 0, keepdims=False)
        return mine, swap(lax.dynamic_index_in_dim(split, 1 - core, 0, keepdims=False))

    mine, other = own_rows(narrow_grads)
    matrices = [
        in_core_order(mine[:, i * HALF : (i + 1) * HALF], other[:, i * HALF : (i + 1) * HALF], 1)
        for i in range(4)
    ]
    small = narrow_grads[:, 4 * HALF :]
    own_small = mine[:, 4 * HALF :].T
    both_small = (mine[:, 4 * HALF : 4 * HALF + 2] + other[:, 4 * HALF : 4 * HALF + 2]).T
    expand_bias_grad = small[:, 8:10].T.reshape(wide)
    mine, other = own_rows(wide_grads[:, 2 * D :])
    expand_grads = in_core_order(
        mine.reshape(block, chips, 1, wide), other.reshape(block, chips, 1, wide), 2
    ).reshape(block, FF)
    reduce_grads = jnp.concatenate([wide_grads[:, :D], wide_grads[:, D : 2 * D]], axis=0)

    return (
        activations.reshape(tokens.shape),
        tokens_gradient,
        matrices[0],
        both_small[0],
        matrices[1],
        matrices[2],
        both_small[1],
        matrices[3],
        own_small[2],
        own_small[3],
        own_small[4],
        expand_grads,
        expand_bias_grad,
        reduce_grads,
        own_small[5],
        own_small[6],
        own_small[7],
    )


def solution(mesh):
    sharded = ("dp", "seq")
    matrix = P(sharded, None)
    vector = P(sharded)
    token = P("dp", "seq", None)
    params = (
        matrix,
        vector,
        matrix,
        matrix,
        vector,
        matrix,
        vector,
        vector,
        vector,
        matrix,
        vector,
        matrix,
        vector,
        vector,
        vector,
    )
    return jax.shard_map(
        functools.partial(body, dps=mesh.shape["dp"], seq=mesh.shape["seq"]),
        mesh=mesh,
        in_specs=(token,) + params + (P("dp", None), token),
        out_specs=(token, token) + params,
        check_vma=False,
    )
```

```python
import functools

import jax
import jax.numpy as jnp
from jax import lax
from jax.experimental.layout import Layout, with_layout_constraint
from jax.experimental import pallas as pl
from jax.experimental.pallas import tpu as pltpu
from jax.sharding import PartitionSpec as P

D = 768
HEADS = 12
HD = 64
FF = 3072
HALF = D // 2
UNITS = FF // 2
PAIR = 2 * HD
PAIRS = HALF // PAIR
NEGATIVE = -1e30
EPSILON = 1e-12
BF = jnp.bfloat16
F32 = jnp.float32
VMEM_LIMIT = 28 * 1024 * 1024
VMEM_LARGE = 56 * 1024 * 1024
QUICK = pl.CostEstimate(flops=0, bytes_accessed=0, transcendentals=0)


def nn(left, right):
    return lax.dot_general(left, right, (((1,), (0,)), ((), ())), preferred_element_type=F32)


def nt(left, right):
    return lax.dot_general(left, right, (((1,), (1,)), ((), ())), preferred_element_type=F32)


def tn(left, right):
    return lax.dot_general(left, right, (((0,), (0,)), ((), ())), preferred_element_type=F32)


def local_copies(place, sources, shapes, plan, name, late=()):
    def kernel(place_ref, *refs):
        ins = refs[: len(sources)]
        outs = refs[len(sources) + len(late) :]
        dp = place_ref[0]
        z = place_ref[1]
        for source, source_index, target, target_index in plan:
            outs[target][target_index(dp, z)] = ins[source][source_index(dp, z)]

    moved = 2 * sum(functools.reduce(lambda a, b: a * b, s) for s in shapes)
    return pl.pallas_call(
        kernel,
        in_specs=[pl.BlockSpec(memory_space=pltpu.SMEM)]
        + [pl.BlockSpec(memory_space=pltpu.VMEM)] * len(sources)
        + [pl.BlockSpec(memory_space=pl.ANY)] * len(late),
        out_specs=[pl.BlockSpec(memory_space=pltpu.VMEM)] * len(shapes),
        out_shape=[jax.ShapeDtypeStruct(shape, BF) for shape in shapes],
        compiler_params=pltpu.CompilerParams(vmem_limit_bytes=VMEM_LIMIT),
        cost_estimate=QUICK,
        name=name,
    )(place, *sources, *late)


def first_columns(place, weights, vectors):
    block = weights[0].shape[0]
    lanes = len(weights) * HALF + 128

    def kernel(place_ref, *refs):
        ins, (mine_ref, theirs_ref, square_ref) = refs[: len(weights) + len(vectors)], refs[-3:]
        core = place_ref[2]
        square_ref[...] = jnp.zeros_like(square_ref)
        row = 0
        for ref in ins[len(weights) :]:
            for part in range(ref.shape[0] // block):
                square_ref[row : row + 1, 0:block] = ref[part * block : (part + 1) * block].reshape(1, block)
                row += 1
        columns = square_ref[...].T[:block].astype(BF)
        for out, side in ((mine_ref, core), (theirs_ref, 1 - core)):
            for i in range(len(weights)):
                picked = ins[i][:, pl.ds(pl.multiple_of(side * HALF, 128), HALF)]
                out[:, i * HALF : (i + 1) * HALF] = picked.astype(BF)
            out[:, len(weights) * HALF :] = columns

    shape = jax.ShapeDtypeStruct((block, lanes), BF)
    return pl.pallas_call(
        kernel,
        in_specs=[pl.BlockSpec(memory_space=pltpu.SMEM)]
        + [pl.BlockSpec(memory_space=pltpu.VMEM)] * (len(weights) + len(vectors)),
        out_specs=[pl.BlockSpec(memory_space=pltpu.VMEM)] * 2,
        out_shape=[shape, shape],
        scratch_shapes=[pltpu.VMEM((128, 128), F32)],
        name="first_columns",
    )(place, *weights, *vectors)


def at_lanes(start, count):
    return pl.ds(start, count)


def core_swap(value, seq):
    return lax.ppermute(value, "seq", [(i, i ^ 1) for i in range(seq)])


def z_move(value, step, seq):
    return lax.ppermute(value, "seq", [(i, i ^ (2 * step)) for i in range(seq)])


def dp_move(value, step, dps):
    return lax.ppermute(value, "dp", [(i, i ^ step) for i in range(dps)])


def tied(value, *others):
    return lax.optimization_barrier((value, others))[0]


def z_moves(value, seq):
    return [value] + [z_move(value, j, seq) for j in range(1, seq // 2)]


def gather_dp_direct(value, dps):
    return [value] + [dp_move(value, k, dps) for k in range(1, dps)]


def gather_dp_first(value, dps):
    return [value] + [dp_move(value, k, dps) for k in range(1, 3 if dps == 4 else dps)]


def gather_dp_halves(blocks, dps):
    if dps != 4:
        return []
    half = blocks[0].shape[0] // 2
    return [blocks[2][:half], blocks[1][half:]]


def gather_dp_rest(blocks, halves):
    return blocks + [dp_move(half, step, 4) for step, half in enumerate(halves, 1)]


def dp_pieces(dps, zs, direct):
    half = zs // 2
    for k in range(dps):
        for j in range(zs):
            if dps == 4 and k == 3 and not direct:
                yield (3, j, k, j) if j < half else (4, j - half, k, j)
            else:
                yield k, j, k, j


def scatter_slots(dps, zs):
    if dps != 4:
        return {(k, j): (k, j) for k in range(dps) for j in range(zs)}, [zs] * dps
    half = zs // 2
    slots = {}
    for j in range(half):
        low, high = j, half + j
        slots[0, low], slots[0, high] = (0, low), (0, high)
        slots[1, low], slots[3, low] = (1, low), (1, half + j)
        slots[2, high], slots[3, high] = (2, j), (2, half + j)
        slots[1, high] = (3, j)
        slots[2, low] = (4, j)
    return slots, [zs, zs, zs, half, half]


def wide_sum(terms):
    return functools.reduce(jnp.add, [t.astype(F32) for t in terms])


def scatter_dp_first(packs, dps):
    if dps != 4:
        return [dp_move(packs[k], k, dps) for k in range(1, dps)]
    return [dp_move(packs[1], 1, dps), dp_move(packs[2], 2, dps)]


def scatter_dp_middle(packs, came, dps):
    if dps != 4:
        return []
    half = packs[3].shape[0]
    return [
        wide_sum([packs[4], came[0][half:]]).astype(BF),
        wide_sum([packs[3], came[1][half:]]).astype(BF),
    ]


def scatter_dp_rest(packs, came, onward, dps, tie=lambda came: came):
    if dps != 4:
        came = tie(came)
        return [wide_sum([packs[0][j]] + [c[j] for c in came]) for j in range(packs[0].shape[0])]
    half = packs[3].shape[0]
    again_two, again_one = tie([dp_move(onward[0], 2, dps), dp_move(onward[1], 1, dps)])
    low = [wide_sum([packs[0][j], came[0][j], again_two[j]]) for j in range(half)]
    return low + [wide_sum([packs[0][half + j], came[1][j], again_one[j]]) for j in range(half)]


def scatter_z(totals, seq, tie=lambda moved: moved):
    moved = tie([z_move(totals[j].astype(BF), j, seq) for j in range(1, seq // 2)])
    return wide_sum([totals[0]] + moved)


def stacked_heads(pair_rows):
    lanes = lax.broadcasted_iota(jnp.int32, pair_rows.shape, 1)
    zero = jnp.zeros_like(pair_rows)
    return jnp.concatenate(
        [jnp.where(lanes < HD, pair_rows, zero), jnp.where(lanes < HD, zero, pair_rows)], axis=0
    )


def unstacked_heads(stacked):
    rows = stacked.shape[0] // 2
    lanes = lax.broadcasted_iota(jnp.int32, (rows, PAIR), 1)
    return jnp.where(lanes < HD, stacked[:rows], stacked[rows:])


def masked_scores(queries, keys, query_ids, key_ids):
    rows = query_ids.shape[0]
    bias = jnp.where(query_ids == key_ids, 0.0, NEGATIVE)
    scores = nt(queries, keys)
    return jnp.concatenate([scores[:rows] + bias, scores[rows:] + bias], axis=0)


def forward_kernel(qid_ref, kid_ref, q_ref, k_ref, v_ref, out_ref, lse_ref):
    rows = q_ref.shape[1] // 2

    @pl.loop(0, 2)
    def _(side):
        span = pl.ds(pl.multiple_of(side * rows, rows), rows)
        queries = stacked_heads(q_ref[0, span, :])
        scores = masked_scores(queries, k_ref[0], qid_ref[0, span, :][:, :1], kid_ref[0][:1, :])
        highest = jnp.max(scores, axis=-1, keepdims=True)
        weights = jnp.exp(scores - highest)
        total = jnp.sum(weights, axis=-1, keepdims=True)
        probs = (weights * (1.0 / total)).astype(BF)
        out_ref[0, span, :] = unstacked_heads(nn(probs, v_ref[0])).astype(BF)
        lse_ref[0, 0, side] = jnp.broadcast_to(highest + jnp.log(total), lse_ref.shape[3:])


def backward_kernel(
    qid_ref, kid_ref, q_ref, k_ref, v_ref, lse_ref, up_ref, dq_ref, dk_ref, dv_ref, key_ref, value_ref
):
    rows = q_ref.shape[1] // 2
    key_ref[...] = jnp.zeros_like(key_ref)
    value_ref[...] = jnp.zeros_like(value_ref)

    @pl.loop(0, 2)
    def _(side):
        span = pl.ds(pl.multiple_of(side * rows, rows), rows)
        keys = k_ref[0]
        queries = stacked_heads(q_ref[0, span, :])
        upward = stacked_heads(up_ref[0, span, :])
        scores = masked_scores(queries, keys, qid_ref[0, span, :][:, :1], kid_ref[0][:1, :])
        probs = jnp.exp(scores - lse_ref[0, 0, side][:, :1])
        dprobs = nt(upward, v_ref[0])
        correction = jnp.sum(probs * dprobs, axis=-1, keepdims=True)
        dscores = (probs * (dprobs - correction)).astype(BF)
        back = unstacked_heads(nn(dscores, keys)).astype(BF).astype(F32)
        dq_ref[0, span, :] = (back * 0.125).astype(BF)
        key_ref[...] += tn(dscores, queries)
        value_ref[...] += tn(probs.astype(BF), upward)

    dk_ref[0] = key_ref[...].astype(BF)
    dv_ref[0] = value_ref[...].astype(BF)


def attention_specs(rows, count):
    return dict(
        qid=pl.BlockSpec((1, rows, 128), lambda s, p: (s, 0, 0)),
        kid=pl.BlockSpec((1, 8, count), lambda s, p: (s, 0, 0)),
        row=pl.BlockSpec((1, rows, PAIR), lambda s, p: (s, 0, p)),
        key=pl.BlockSpec((1, count, PAIR), lambda s, p: (s, 0, p)),
        value=pl.BlockSpec((1, count, PAIR), lambda s, p: (s, 0, PAIRS + p)),
        lse=pl.BlockSpec((1, 1, 2, rows, 128), lambda s, p: (s, p, 0, 0, 0)),
    )


def attend(query_ids, key_ids, queries, key_values):
    streams, rows, _ = queries.shape
    count = key_values.shape[1]
    specs = attention_specs(rows, count)
    macs = streams * 2 * PAIRS * rows * count * HD
    return pl.pallas_call(
        forward_kernel,
        grid=(streams, PAIRS),
        in_specs=[specs["qid"], specs["kid"], specs["row"], specs["key"], specs["value"]],
        out_specs=[specs["row"], specs["lse"]],
        out_shape=[
            jax.ShapeDtypeStruct((streams, rows, HALF), BF),
            jax.ShapeDtypeStruct((streams, PAIRS, 2, rows, 128), F32),
        ],
        compiler_params=pltpu.CompilerParams(vmem_limit_bytes=VMEM_LIMIT if count <= 1024 else VMEM_LARGE),
        cost_estimate=QUICK,
        name="attend",
    )(query_ids, key_ids, queries, key_values, key_values)


def attend_back(query_ids, key_ids, queries, key_values, lse, upward):
    streams, rows, _ = queries.shape
    count = key_values.shape[1]
    specs = attention_specs(rows, count)
    macs = streams * 2 * PAIRS * rows * count * HD
    key_shape = jax.ShapeDtypeStruct((streams, count, HALF), BF)
    return pl.pallas_call(
        backward_kernel,
        grid=(streams, PAIRS),
        in_specs=[
            specs["qid"],
            specs["kid"],
            specs["row"],
            specs["key"],
            specs["value"],
            specs["lse"],
            specs["row"],
        ],
        out_specs=[specs["row"], specs["key"], specs["key"]],
        out_shape=[jax.ShapeDtypeStruct((streams, rows, HALF), BF), key_shape, key_shape],
        scratch_shapes=[pltpu.VMEM((count, PAIR), F32)] * 2,
        compiler_params=pltpu.CompilerParams(vmem_limit_bytes=VMEM_LIMIT if count <= 1024 else VMEM_LARGE),
        cost_estimate=QUICK,
        name="attend_back",
    )(query_ids, key_ids, queries, key_values, key_values, lse, upward)


CHUNK = 384
QUERY_BIAS, VALUE_BIAS, OUT_BIAS, FIRST_GAIN, FIRST_SHIFT, REDUCE_BIAS, SECOND_GAIN, SECOND_SHIFT = range(8)


def norm_rows(value_rows):
    centre = jnp.mean(value_rows, axis=-1, keepdims=True)
    centred = value_rows - centre
    inverse = lax.rsqrt(jnp.mean(centred * centred, axis=-1, keepdims=True) + EPSILON)
    return (centred * inverse, inverse)


def norm_back(upward, normed, inverse):
    mean_up = jnp.mean(upward, axis=-1, keepdims=True)
    mean_cross = jnp.mean(upward * normed, axis=-1, keepdims=True)
    return inverse * (upward - mean_up - normed * mean_cross)


def add_rows(sum_ref, index, values):
    sum_ref[index] += jnp.sum(values.reshape(-1, 8, values.shape[1]), axis=0)


def vector_of(vec_ref, index):
    return vec_ref[index : index + 1, :]


def half_of_ref(place_ref):
    return pl.ds(pl.multiple_of(place_ref[2] * HALF, 128), HALF)


def other_half_of_ref(place_ref):
    return pl.ds(pl.multiple_of((1 - place_ref[2]) * HALF, 128), HALF)


def project(place, mine, other, vectors, weight):
    streams, rows, _ = mine[0].shape
    zs = len(mine)
    chip_rows = 2 * rows
    count = zs * chip_rows
    tile = min(count, 1024)

    def kernel(place_ref, *refs):
        mine_refs, other_refs, (vec_ref, weight_ref) = refs[:zs], refs[zs : 2 * zs], refs[2 * zs : 2 * zs + 2]
        all_ref, pairs_ref, query_ref, rows_ref = refs[2 * zs + 2 :]
        half = half_of_ref(place_ref)
        for j in range(zs):
            here = pl.ds(pl.multiple_of(j * chip_rows + place_ref[2] * rows, rows), rows)
            there = pl.ds(pl.multiple_of(j * chip_rows + (1 - place_ref[2]) * rows, rows), rows)
            for s in range(streams):
                all_ref[s, here, :] = mine_refs[j][s]
                all_ref[s, there, :] = other_refs[j][s]

        @pl.loop(0, streams)
        def _(s):
            for start in range(0, count, tile):
                span = slice(start, start + tile)
                pairs = nn(all_ref[s, span, :], weight_ref[:, HALF:])
                pairs_ref[s, span, :HALF] = pairs[:, :HALF].astype(BF)
                values = pairs[:, HALF:] + vec_ref[VALUE_BIAS : VALUE_BIAS + 1, half]
                pairs_ref[s, span, HALF:] = values.astype(BF)
            tokens = all_ref[s, :chip_rows, :]
            rows_ref[s] = tokens
            queries = nn(tokens, weight_ref[:, :HALF]) + vec_ref[QUERY_BIAS : QUERY_BIAS + 1, half]
            query_ref[s] = (queries * 0.125).astype(BF)

    shape = lambda rows, lanes: jax.ShapeDtypeStruct((streams, rows, lanes), BF)
    return pl.pallas_call(
        kernel,
        in_specs=[pl.BlockSpec(memory_space=pltpu.SMEM)]
        + [pl.BlockSpec(memory_space=pltpu.VMEM)] * (2 * zs + 2),
        out_specs=[pl.BlockSpec(memory_space=pltpu.VMEM)] * 4,
        out_shape=[shape(count, D), shape(count, D), shape(chip_rows, HALF), shape(chip_rows, D)],
        compiler_params=pltpu.CompilerParams(
            vmem_limit_bytes=VMEM_LIMIT if count <= 1024 else VMEM_LARGE
        ),
        cost_estimate=QUICK,
        name="project",
    )(place, *mine, *other, vectors, weight)


def unproject(place, query_back, key_back, value_back, weight):
    streams, count, _ = key_back.shape
    chip_rows = query_back.shape[1]
    rows = chip_rows // 2
    zs = count // chip_rows
    tile = min(count, 1024)

    def kernel(place_ref, query_ref, key_ref, value_ref, weight_ref, mine_ref, other_ref):
        first_core = place_ref[2] == 0

        @pl.loop(0, streams)
        def _(s):
            for start in range(0, count, tile):
                span = slice(start, start + tile)
                back = jnp.concatenate([key_ref[s, span, :], value_ref[s, span, :]], axis=1)
                total = nt(back, weight_ref[:, HALF:])
                for offset in range(0, tile, chip_rows):
                    j = (start + offset) // chip_rows
                    chip = total[offset : offset + chip_rows]
                    if j == 0:
                        chip += nt(query_ref[s], weight_ref[:, :HALF])
                    mine_ref[j, s] = jnp.where(first_core, chip[:rows], chip[rows:]).astype(BF)
                    other_ref[j, s] = jnp.where(first_core, chip[rows:], chip[:rows]).astype(BF)

    shape = jax.ShapeDtypeStruct((zs, streams, rows, D), BF)
    return pl.pallas_call(
        kernel,
        in_specs=[pl.BlockSpec(memory_space=pltpu.SMEM)]
        + [pl.BlockSpec(memory_space=pltpu.VMEM)] * 4,
        out_specs=[pl.BlockSpec(memory_space=pltpu.VMEM)] * 2,
        out_shape=[shape, shape],
        compiler_params=pltpu.CompilerParams(
            vmem_limit_bytes=VMEM_LIMIT if count <= 1024 else VMEM_LARGE
        ),
        cost_estimate=QUICK,
        name="unproject",
    )(place, query_back, key_back, value_back, weight)


def middle_kernel(
    place_ref, mine_ref, other_ref, tok_ref, vec_ref, unit_ref, out_ref, expand_ref, reduce_ref,
    normed_ref, inverse_ref, low_ref, hidden_ref, slope_ref, part_ref, send_ref,
):
    branch = nn(mine_ref[...], out_ref[half_of_ref(place_ref), :])
    branch += nn(other_ref[...], out_ref[other_half_of_ref(place_ref), :])
    branch += vector_of(vec_ref, OUT_BIAS)
    normed, inverse = norm_rows(tok_ref[...].astype(F32) + branch)
    normed_ref[...] = normed
    inverse_ref[...] = jnp.broadcast_to(inverse, inverse_ref.shape)
    first = normed * vector_of(vec_ref, FIRST_GAIN) + vector_of(vec_ref, FIRST_SHIFT)
    low = first.astype(BF)
    low_ref[...] = low
    total = jnp.zeros(part_ref.shape, F32)
    for start in range(0, UNITS, CHUNK):
        span = slice(start, start + CHUNK)
        expanded = nn(low, expand_ref[:, span]) + unit_ref[:, span]
        share = 0.5 * (1.0 + lax.erf(expanded * (0.5**0.5)))
        hidden = (expanded * share).astype(BF)
        hidden_ref[:, span] = hidden
        bell = jnp.exp(-0.5 * expanded * expanded) * 0.3989422804014327
        slope_ref[:, span] = (share + expanded * bell).astype(BF)
        total += nn(hidden, reduce_ref[span, :])
    part_ref[...] = total
    send_ref[...] = total.astype(BF)


def turn_kernel(
    place_ref, part_ref, came_ref, normed_ref, mine_ref, other_ref, slope_ref, vec_ref, reduce_ref, expand_ref,
    act_ref, residual_ref, low_ref, back_ref, next_ref, send_ref, sum_ref, unit_sum_ref,
):
    core = place_ref[2]
    first = normed_ref[...] * vector_of(vec_ref, FIRST_GAIN) + vector_of(vec_ref, FIRST_SHIFT)
    reduced = part_ref[...] + came_ref[...].astype(F32) + vector_of(vec_ref, REDUCE_BIAS)
    normed, inverse = norm_rows(first + reduced)
    gain = vector_of(vec_ref, SECOND_GAIN)
    half = normed.shape[0] // 2
    mine = jnp.where(core == 0, normed[:half], normed[half:])
    act_ref[...] = (mine * gain + vector_of(vec_ref, SECOND_SHIFT)).astype(BF)
    mine, other = mine_ref[...].astype(F32), other_ref[...].astype(F32)
    upward = jnp.concatenate(
        [jnp.where(core == 0, mine, other), jnp.where(core == 0, other, mine)], axis=0
    )
    residual = norm_back(upward * gain, normed, inverse)
    low = residual.astype(BF)
    residual_ref[...] = residual
    low_ref[...] = low
    add_rows(sum_ref, 0, low.astype(F32))
    add_rows(sum_ref, 1, upward * normed)
    add_rows(sum_ref, 2, upward)
    total = jnp.zeros(next_ref.shape, F32)
    for start in range(0, UNITS, CHUNK):
        span = slice(start, start + CHUNK)
        back = (nt(low, reduce_ref[span, :]) * slope_ref[:, span].astype(F32)).astype(BF)
        back_ref[:, span] = back
        unit_sum_ref[:, span] += jnp.sum(back.astype(F32).reshape(-1, 8, CHUNK), axis=0)
        total += nt(back, expand_ref[:, span])
    next_ref[...] = total
    send_ref[...] = total.astype(BF)


def first_back_kernel(
    place_ref, part_ref, came_ref, residual_ref, normed_ref, inverse_ref, vec_ref, out_ref,
    back_ref, low_ref, attended_ref, sum_ref,
):
    upward = part_ref[...] + came_ref[...].astype(F32) + residual_ref[...]
    normed = normed_ref[...]
    add_rows(sum_ref, 1, upward * normed)
    add_rows(sum_ref, 2, upward)
    back = norm_back(upward * vector_of(vec_ref, FIRST_GAIN), normed, inverse_ref[:, :1])
    low = back.astype(BF)
    half = back.shape[0] // 2
    back_ref[...] = jnp.where(place_ref[2] == 0, back[:half], back[half:])
    low_ref[...] = low
    add_rows(sum_ref, 0, low.astype(F32))
    attended_ref[...] = nt(low, out_ref[half_of_ref(place_ref), :]).astype(BF)


def over_rows(body, place, steps, tiled, whole, outs, sums, name):
    def tile_of(ref, step):
        rows = ref.shape[0] // steps
        return ref.at[pl.ds(pl.multiple_of(step * rows, rows), rows)]

    def kernel(place_ref, *refs):
        tiles, refs = refs[: len(tiled)], refs[len(tiled) :]
        kept, refs = refs[: len(whole)], refs[len(whole) :]
        results, totals = refs[: len(outs)], refs[len(outs) :]
        for total in totals:
            total[...] = jnp.zeros_like(total)

        @pl.loop(0, steps)
        def _(step):
            body(
                place_ref,
                *[tile_of(ref, step) for ref in tiles],
                *kept,
                *[tile_of(ref, step) for ref in results],
                *totals,
            )

    return pl.pallas_call(
        kernel,
        in_specs=[pl.BlockSpec(memory_space=pltpu.SMEM)]
        + [pl.BlockSpec(memory_space=pltpu.VMEM)] * (len(tiled) + len(whole)),
        out_specs=[pl.BlockSpec(memory_space=pltpu.VMEM)] * (len(outs) + len(sums)),
        out_shape=[jax.ShapeDtypeStruct(out[:2], out[2]) for out in outs]
        + [jax.ShapeDtypeStruct(shape, F32) for shape in sums],
        compiler_params=pltpu.CompilerParams(vmem_limit_bytes=VMEM_LIMIT),
        cost_estimate=QUICK,
        name=name,
    )(place, *tiled, *whole)


def packed_call(kernel, place, sources, shapes, scratch, name):
    return pl.pallas_call(
        kernel,
        in_specs=[pl.BlockSpec(memory_space=pltpu.SMEM)]
        + [pl.BlockSpec(memory_space=pltpu.VMEM)] * len(sources),
        out_specs=[pl.BlockSpec(memory_space=pltpu.VMEM)] * len(shapes),
        out_shape=[jax.ShapeDtypeStruct(shape, BF) for shape in shapes],
        scratch_shapes=scratch,
        compiler_params=pltpu.CompilerParams(vmem_limit_bytes=VMEM_LIMIT),
        cost_estimate=QUICK,
        name=name,
    )(place, *sources)


def wide_packs_of(place, hidden, reduced_back, first_low, expanded_back, dps, zs):
    chips = dps * zs
    both, wide = D // chips, UNITS // chips
    slots, counts = scatter_slots(dps, zs)
    lanes = 2 * D + UNITS

    def kernel(place_ref, hidden_ref, reduced_ref, low_ref, expanded_ref, *refs):
        outs, (reduce_ref, expand_ref) = refs[: len(counts)], refs[len(counts) :]
        for start in range(0, UNITS, CHUNK):
            span = slice(start, start + CHUNK)
            reduce_ref[span, :] = tn(hidden_ref[:, span], reduced_ref[...]).astype(BF)
        for start in range(0, D, 256):
            span = slice(start, start + 256)
            expand_ref[span, :] = tn(low_ref[:, span], expanded_ref[...]).astype(BF)
        for (k, j), (array, row) in slots.items():
            chip = (place_ref[0] ^ k) * zs + (place_ref[1] ^ j)
            first = pl.multiple_of(chip * wide, 16)
            outs[array][row, :, :D] = reduce_ref[pl.ds(first, both), :]
            outs[array][row, :, D : 2 * D] = reduce_ref[pl.ds(pl.multiple_of(first + both, 16), both), :]
            outs[array][row, :, 2 * D :] = expand_ref[pl.ds(pl.multiple_of(chip * both, 16), both), :]

    return packed_call(
        kernel,
        place,
        [hidden, reduced_back, first_low, expanded_back],
        [(count, both, lanes) for count in counts],
        [pltpu.VMEM((UNITS, D), BF), pltpu.VMEM((D, UNITS), BF)],
        "wide_packs",
    )


def narrow_packs_of(place, tokens, chip_tokens, backs, mine, other, branch_back, sums, dps, zs):
    chips = dps * zs
    both = D // chips
    slots, counts = scatter_slots(dps, zs)
    lanes = 4 * HALF + 128
    query_back, key_back, value_back = backs

    def kernel(
        place_ref, tok_ref, chip_ref, query_ref, key_ref, value_ref, mine_ref, other_ref, branch_ref,
        one_ref, two_ref, unit_ref, *refs,
    ):
        outs, (all_ref, square_ref) = refs[: len(counts)], refs[len(counts) :]
        half = half_of_ref(place_ref)
        for start in range(0, D, 256):
            span = slice(start, start + 256)
            turned = tok_ref[:, span].T
            all_ref[span, :HALF] = tn(chip_ref[:, span], query_ref[...]).astype(BF)
            all_ref[span, HALF : 2 * HALF] = nn(turned, key_ref[...]).astype(BF)
            all_ref[span, 2 * HALF : 3 * HALF] = nn(turned, value_ref[...]).astype(BF)
        branch = branch_ref[:, half]
        all_ref[half, 3 * HALF : 4 * HALF] = tn(mine_ref[...], branch).astype(BF)
        all_ref[other_half_of_ref(place_ref), 3 * HALF : 4 * HALF] = tn(other_ref[...], branch).astype(BF)
        square_ref[...] = jnp.zeros_like(square_ref)
        for row, ref in ((0, query_ref), (1, value_ref)):
            square_ref[row : row + 1, half] = jnp.sum(ref[...].astype(F32), axis=0, keepdims=True)
        for i in range(3):
            square_ref[2 + i : 3 + i, :] = jnp.sum(one_ref[i], axis=0, keepdims=True)
            square_ref[5 + i : 6 + i, :] = jnp.sum(two_ref[i], axis=0, keepdims=True)
        unit = jnp.sum(unit_ref[...], axis=0, keepdims=True)
        for chip in range(chips):
            for h in range(2):
                first = (2 * chip + h) * both
                square_ref[8 + h : 9 + h, chip * both : (chip + 1) * both] = unit[:, first : first + both]
        all_ref[:, 4 * HALF :] = square_ref[...].T.astype(BF)
        for (k, j), (array, row) in slots.items():
            chip = (place_ref[0] ^ k) * zs + (place_ref[1] ^ j)
            outs[array][row] = all_ref[pl.ds(pl.multiple_of(chip * both, 16), both), :]

    return packed_call(
        kernel,
        place,
        [tokens, chip_tokens, query_back, key_back, value_back, mine, other, branch_back, *sums],
        [(count, both, lanes) for count in counts],
        [pltpu.VMEM((D, lanes), BF), pltpu.VMEM((128, D), F32)],
        "narrow_packs",
    )


def column_sum(value_rows):
    return jnp.sum(value_rows.astype(F32), axis=0)


def item_ids(lengths, places):
    items = lengths.shape[1]
    slot = jnp.arange(items, dtype=jnp.int32)
    ends = jnp.sum(jnp.where(slot[:, None] <= slot[None, :], lengths[:, :, None], 0), axis=1)
    return jnp.sum((ends[:, None, :] <= places[None, :, None]).astype(jnp.int32), axis=2)


def body(
    tokens,
    query_weight,
    query_bias,
    key_weight,
    value_weight,
    value_bias,
    out_weight,
    out_bias,
    first_gain,
    attention_norm_shift,
    expand_weight,
    expand_bias,
    reduce_weight,
    reduce_bias,
    second_gain,
    second_shift,
    lengths,
    cotangent,
    *,
    dps,
    seq,
):
    streams, row_count, _ = tokens.shape
    zs = seq // 2
    chips = dps * zs
    block = D // (2 * chips)
    both = 2 * block
    wide = FF // (2 * chips)
    chip_rows = 2 * row_count
    rows = streams * chip_rows
    dp = lax.axis_index("dp")
    z = lax.axis_index("seq") // 2
    core = lax.axis_index("seq") % 2
    place = jnp.stack([dp, z, core]).astype(jnp.int32)
    swap = functools.partial(core_swap, seq=seq)

    def row_major(value):
        return with_layout_constraint(value, Layout(major_to_minor=tuple(range(value.ndim))))

    def in_core_order(mine, other, axis):
        return jnp.where(
            core == 0,
            jnp.concatenate([mine, other], axis=axis),
            jnp.concatenate([other, mine], axis=axis),
        )

    mine, theirs = first_columns(
        place,
        (query_weight, key_weight, value_weight),
        (
            query_bias,
            value_bias,
            out_bias,
            first_gain,
            attention_norm_shift,
            reduce_bias,
            second_gain,
            second_shift,
            expand_bias,
        ),
    )
    early = in_core_order(mine[None], swap(theirs)[None], 0)

    out_weight = out_weight.astype(BF)
    units = expand_weight.astype(BF).reshape(block, chips, 2, wide)

    def columns_for(side):
        unit = lax.dynamic_index_in_dim(units, side, 2, keepdims=False).reshape(block, UNITS)
        return jnp.concatenate([out_weight, unit], axis=1)

    late = in_core_order(columns_for(core)[None], swap(columns_for(1 - core))[None], 0)
    parts = reduce_weight.astype(BF).reshape(2, 2, block, D)
    late = jnp.concatenate([late, parts[:, 0], parts[:, 1]], axis=2)
    other_cotangent = swap(cotangent).reshape(-1, D)
    cotangent = cotangent.reshape(-1, D)
    other_tokens = swap(tokens)
    early = jnp.stack(tied(z_moves(early, seq), late, other_tokens, other_cotangent))
    late = z_moves(tied(late, early), seq)
    early, late = lax.optimization_barrier((gather_dp_first(early, dps), late))
    early = gather_dp_rest(early, gather_dp_halves(early, dps))
    moved = z_moves(tied(tokens, late), seq)
    late = gather_dp_first(jnp.stack(tied(late, early)), dps)

    def gather_plan(parts, direct=False):
        return [
            (
                piece,
                lambda dp, z, row=row, first=first, count=count: (
                    row,
                    Ellipsis,
                    at_lanes(first, count),
                ),
                target,
                lambda dp, z, j=j, k=k: (dp ^ k, z ^ j),
            )
            for piece, row, k, j in dp_pieces(dps, zs, direct)
            for first, count, target in parts
        ]

    qkv_weight, small = local_copies(
        place,
        early,
        [(dps, zs, 2, block, 3 * HALF), (dps, zs, 2, block, 128)],
        gather_plan([(0, 3 * HALF, 0), (3 * HALF, 128, 1)]),
        "place_early",
    )
    qkv_weight = qkv_weight.reshape(D, 3 * HALF)
    small = small.astype(F32).reshape(D, 128)[:, :12].T
    expand_bias = small[8:12].reshape(4, chips, 2, block)
    expand_bias = lax.dynamic_index_in_dim(expand_bias, core, 2, keepdims=False)
    expand_bias = expand_bias.transpose(1, 0, 2).reshape(1, UNITS)

    def half_of(vector):
        return lax.dynamic_slice_in_dim(vector, core * HALF, HALF, 1)

    qkv_weight = tied(qkv_weight, expand_bias)
    halves = gather_dp_halves(tied(late, qkv_weight), dps)
    late = gather_dp_rest(late, halves)
    qkv_weight = tied(qkv_weight, halves)
    others = [other_tokens] + [swap(m) for m in tied(moved[1:], halves)]

    all_tokens, key_values, queries, chip_tokens = project(
        place, moved, others, small, qkv_weight
    )
    flat_all = all_tokens.reshape(-1, D)
    spot = jnp.arange(row_count, dtype=jnp.int32)
    steps = jnp.arange(zs, dtype=jnp.int32) ^ z
    starts = (steps[:, None] * 2 + jnp.arange(2, dtype=jnp.int32)) * row_count
    ids = item_ids(lengths, (starts[:, :, None] + spot).reshape(-1))
    key_ids = jnp.broadcast_to(ids[:, None, :], (streams, 8, ids.shape[1]))
    query_ids = jnp.broadcast_to(ids[:, :chip_rows, None], (streams, chip_rows, 128))

    chip_tokens = chip_tokens.reshape(rows, D)
    attended, lse = attend(query_ids, key_ids, queries, key_values)
    other_attended = swap(attended).reshape(rows, HALF)
    attended = attended.reshape(rows, HALF)

    out_weight, expand_weight, reduce_weight = local_copies(
        place,
        late,
        [(dps, zs, 2, block, D), (dps, zs, 2, block, UNITS), (dps, zs, 4, block, D)],
        gather_plan([(0, D, 0), (D, UNITS, 1)])
        + [
            (
                piece,
                lambda dp, z, row=row, c=c, h=h: (row, c, slice(None), at_lanes(D + UNITS + h * D, D)),
                2,
                lambda dp, z, j=j, k=k, c=c, h=h: (dp ^ k, z ^ j, 2 * c + h),
            )
            for piece, row, k, j in dp_pieces(dps, zs, False)
            for c in range(2)
            for h in range(2)
        ],
        "place_late",
    )
    out_weight = out_weight.reshape(D, D)
    expand_weight = expand_weight.reshape(D, UNITS)
    reduce_weight = reduce_weight.reshape(UNITS, D)

    normed_one, inverse_one, first_low, hidden, slope, partial, sent = over_rows(
        middle_kernel,
        place,
        streams,
        [attended, other_attended, chip_tokens],
        [small, expand_bias, out_weight, expand_weight, reduce_weight],
        [
            (rows, D, F32),
            (rows, 128, F32),
            (rows, D, BF),
            (rows, UNITS, BF),
            (rows, UNITS, BF),
            (rows, D, F32),
            (rows, D, BF),
        ],
        [],
        "middle",
    )
    activations, residual_two_back, reduced_back, expanded_back, partial, sent, sums_two, unit_sums = over_rows(
        turn_kernel,
        place,
        streams,
        [partial, swap(sent), normed_one, cotangent, other_cotangent, slope],
        [small, reduce_weight, expand_weight],
        [
            (rows // 2, D, BF),
            (rows, D, F32),
            (rows, D, BF),
            (rows, UNITS, BF),
            (rows, D, F32),
            (rows, D, BF),
        ],
        [(3, 8, D), (8, UNITS)],
        "turn",
    )
    came_partial = swap(sent)
    fused = both % 16 == 0

    def scatter_plan(parts, lanes):
        slots, counts = scatter_slots(dps, zs)
        plan = [
            (
                source,
                lambda dp, z, j=j, k=k, index=index: index(dp ^ k, z ^ j),
                array,
                lambda dp, z, row=row, first=first, count=count: (
                    row,
                    slice(None),
                    at_lanes(first, count),
                ),
            )
            for (k, j), (array, row) in slots.items()
            for source, index, first, count in parts
        ]
        return [(count, both, lanes) for count in counts], plan

    if fused:
        wide_packs = wide_packs_of(place, hidden, reduced_back, first_low, expanded_back, dps, zs)
    else:
        wide_packs = local_copies(
            place,
            [
                tn(hidden, reduced_back).astype(BF).reshape(dps, zs, 2, both, D),
                tn(first_low, expanded_back).astype(BF).reshape(dps, zs, both, UNITS),
            ],
            *scatter_plan(
                [
                    (0, lambda d, zz: (d, zz, 0), 0, D),
                    (0, lambda d, zz: (d, zz, 1), D, D),
                    (1, lambda d, zz: (d, zz), 2 * D, UNITS),
                ],
                2 * D + UNITS,
            ),
            "pack_wide",
        )
    wide_came = scatter_dp_first(wide_packs, dps)

    residual_one_back, branch_back, attended_back, sums_one = over_rows(
        first_back_kernel,
        place,
        streams,
        [partial, came_partial, residual_two_back, normed_one, inverse_one],
        [small, out_weight],
        [(rows // 2, D, F32), (rows, D, BF), (rows, HALF, BF)],
        [(3, 8, D)],
        "first_back",
    )
    attended_back = attended_back.reshape(streams, chip_rows, HALF)

    query_back, key_back, value_back = attend_back(
        query_ids, key_ids, queries, key_values, lse, attended_back
    )
    mine_part, other_part = unproject(place, query_back, key_back, value_back, qkv_weight)
    came_part = swap(other_part)
    wide_came = tied(wide_came, other_part)
    wide_onward = scatter_dp_middle(wide_packs, wide_came, dps)
    mine_part, came_part = tied((mine_part, came_part), wide_onward)
    tokens_total = wide_sum([mine_part, came_part])
    tokens_first = tokens_total[zs // 2 :].astype(BF)

    def halved(total, bit, sent):
        return total[:bit] + z_move(sent, bit, seq).astype(F32)

    tokens_total = halved(tokens_total, zs // 2, tokens_first)
    backs = (query_back.reshape(rows, HALF), key_back.reshape(-1, HALF), value_back.reshape(-1, HALF))
    backs = tied(backs, tokens_first)
    if fused:
        narrow_packs = narrow_packs_of(
            place,
            flat_all,
            chip_tokens,
            backs,
            attended,
            other_attended,
            branch_back,
            (sums_one, sums_two, unit_sums),
            dps,
            zs,
        )
        wide_totals = scatter_dp_rest(
            wide_packs, wide_came, wide_onward, dps, lambda came: tied(came, narrow_packs)
        )
    else:
        out_side = half_of(branch_back)
        zeros = jnp.zeros((D,), F32)
        small_grads = jnp.concatenate(
            [
                lax.dynamic_update_slice_in_dim(zeros, column_sum(backs[0]), core * HALF, 0)[None],
                lax.dynamic_update_slice_in_dim(zeros, column_sum(backs[2]), core * HALF, 0)[None],
                jnp.sum(sums_one, axis=1),
                jnp.sum(sums_two, axis=1),
                jnp.sum(unit_sums, axis=0).reshape(chips, 2, both).transpose(1, 0, 2).reshape(2, D),
            ],
            axis=0,
        ).T.astype(BF)
        small_grads = jnp.pad(small_grads, ((0, 0), (0, 128 - small_grads.shape[1])))
        four = (
            tn(chip_tokens, backs[0]).astype(BF),
            tn(flat_all, backs[1]).astype(BF),
            tn(flat_all, backs[2]).astype(BF),
            in_core_order(tn(attended, out_side), tn(other_attended, out_side), 0).astype(BF),
        )
        wide_totals = scatter_dp_rest(wide_packs, wide_came, wide_onward, dps)
        narrow_packs = local_copies(
            place,
            [g.reshape(dps, zs, both, HALF) for g in four] + [small_grads.reshape(dps, zs, both, 128)],
            *scatter_plan(
                [(i, lambda d, zz: (d, zz), i * HALF, HALF) for i in range(4)]
                + [(4, lambda d, zz: (d, zz), 4 * HALF, 128)],
                4 * HALF + 128,
            ),
            "pack_narrow",
        )
    came = tied(scatter_dp_first(narrow_packs, dps), wide_totals)
    narrow_onward = scatter_dp_middle(narrow_packs, came, dps)
    narrow_totals = scatter_dp_rest(narrow_packs, came, narrow_onward, dps)
    wide_grads = scatter_z(tied(wide_totals, tokens_total), seq)
    bit = zs // 4
    while bit:
        tokens_total = halved(tokens_total, bit, tokens_total[bit:].astype(BF))
        bit //= 2
    narrow_totals, tokens_total, wide_grads = lax.optimization_barrier(
        (narrow_totals, tokens_total, wide_grads)
    )
    narrow_grads = scatter_z(narrow_totals, seq)
    tokens_gradient = residual_one_back.reshape(tokens.shape) + tokens_total[0]

    def own_rows(grads):
        split = grads.reshape(2, block, grads.shape[1])
        mine = lax.dynamic_index_in_dim(split, core, 0, keepdims=False)
        return mine, swap(lax.dynamic_index_in_dim(split, 1 - core, 0, keepdims=False))

    mine, other = own_rows(wide_grads[:, 2 * D :])
    expand_grads = in_core_order(
        mine.reshape(block, chips, 1, wide), other.reshape(block, chips, 1, wide), 2
    ).reshape(block, FF)
    reduce_grads = jnp.concatenate([wide_grads[:, :D], wide_grads[:, D : 2 * D]], axis=0)
    mine, other = own_rows(narrow_grads)
    matrices = [
        in_core_order(mine[:, i * HALF : (i + 1) * HALF], other[:, i * HALF : (i + 1) * HALF], 1)
        for i in range(4)
    ]
    own_small = mine[:, 4 * HALF :].T
    both_small = (mine[:, 4 * HALF : 4 * HALF + 2] + other[:, 4 * HALF : 4 * HALF + 2]).T
    expand_bias_grad = narrow_grads[:, 4 * HALF :][:, 8:10].T.reshape(wide)

    return (
        activations.reshape(tokens.shape),
        tokens_gradient,
        matrices[0],
        both_small[0],
        matrices[1],
        matrices[2],
        both_small[1],
        matrices[3],
        own_small[2],
        own_small[3],
        own_small[4],
        expand_grads,
        expand_bias_grad,
        reduce_grads,
        own_small[5],
        own_small[6],
        own_small[7],
    )


def solution(mesh):
    sharded = ("dp", "seq")
    matrix = P(sharded, None)
    vector = P(sharded)
    token = P("dp", "seq", None)
    params = (
        matrix,
        vector,
        matrix,
        matrix,
        vector,
        matrix,
        vector,
        vector,
        vector,
        matrix,
        vector,
        matrix,
        vector,
        vector,
        vector,
    )
    return jax.shard_map(
        functools.partial(body, dps=mesh.shape["dp"], seq=mesh.shape["seq"]),
        mesh=mesh,
        in_specs=(token,) + params + (P("dp", None), token),
        out_specs=(token, token) + params,
        check_vma=False,
    )
```

```python
import functools

import jax
import jax.numpy as jnp
from jax import lax
from jax.experimental.layout import Layout, with_layout_constraint
from jax.experimental import pallas as pl
from jax.experimental.pallas import tpu as pltpu
from jax.sharding import PartitionSpec as P

D = 768
HEADS = 12
HD = 64
FF = 3072
HALF = D // 2
UNITS = FF // 2
PAIR = 2 * HD
PAIRS = HALF // PAIR
NEGATIVE = -1e30
EPSILON = 1e-12
BF = jnp.bfloat16
F32 = jnp.float32
VMEM_LIMIT = 28 * 1024 * 1024
VMEM_LARGE = 56 * 1024 * 1024
QUICK = pl.CostEstimate(flops=0, bytes_accessed=0, transcendentals=0)


def nn(left, right):
    return lax.dot_general(left, right, (((1,), (0,)), ((), ())), preferred_element_type=F32)


def nt(left, right):
    return lax.dot_general(left, right, (((1,), (1,)), ((), ())), preferred_element_type=F32)


def tn(left, right):
    return lax.dot_general(left, right, (((0,), (0,)), ((), ())), preferred_element_type=F32)


def local_copies(place, sources, shapes, plan, name, late=()):
    def kernel(place_ref, *refs):
        ins = refs[: len(sources)]
        outs = refs[len(sources) + len(late) :]
        dp = place_ref[0]
        z = place_ref[1]
        for source, source_index, target, target_index in plan:
            outs[target][target_index(dp, z)] = ins[source][source_index(dp, z)]

    moved = 2 * sum(functools.reduce(lambda a, b: a * b, s) for s in shapes)
    return pl.pallas_call(
        kernel,
        in_specs=[pl.BlockSpec(memory_space=pltpu.SMEM)]
        + [pl.BlockSpec(memory_space=pltpu.VMEM)] * len(sources)
        + [pl.BlockSpec(memory_space=pl.ANY)] * len(late),
        out_specs=[pl.BlockSpec(memory_space=pltpu.VMEM)] * len(shapes),
        out_shape=[jax.ShapeDtypeStruct(shape, BF) for shape in shapes],
        compiler_params=pltpu.CompilerParams(vmem_limit_bytes=VMEM_LIMIT),
        cost_estimate=QUICK,
        name=name,
    )(place, *sources, *late)


def first_columns(place, weights, vectors):
    block = weights[0].shape[0]
    lanes = len(weights) * HALF + 128

    def kernel(place_ref, *refs):
        ins, (mine_ref, theirs_ref, square_ref) = refs[: len(weights) + len(vectors)], refs[-3:]
        core = place_ref[2]
        square_ref[...] = jnp.zeros_like(square_ref)
        row = 0
        for ref in ins[len(weights) :]:
            for part in range(ref.shape[0] // block):
                square_ref[row : row + 1, 0:block] = ref[part * block : (part + 1) * block].reshape(1, block)
                row += 1
        columns = square_ref[...].T[:block].astype(BF)
        for out, side in ((mine_ref, core), (theirs_ref, 1 - core)):
            for i in range(len(weights)):
                picked = ins[i][:, pl.ds(pl.multiple_of(side * HALF, 128), HALF)]
                out[:, i * HALF : (i + 1) * HALF] = picked.astype(BF)
            out[:, len(weights) * HALF :] = columns

    shape = jax.ShapeDtypeStruct((block, lanes), BF)
    return pl.pallas_call(
        kernel,
        in_specs=[pl.BlockSpec(memory_space=pltpu.SMEM)]
        + [pl.BlockSpec(memory_space=pltpu.VMEM)] * (len(weights) + len(vectors)),
        out_specs=[pl.BlockSpec(memory_space=pltpu.VMEM)] * 2,
        out_shape=[shape, shape],
        scratch_shapes=[pltpu.VMEM((128, 128), F32)],
        name="first_columns",
    )(place, *weights, *vectors)


def at_lanes(start, count):
    return pl.ds(start, count)


def core_swap(value, seq):
    return lax.ppermute(value, "seq", [(i, i ^ 1) for i in range(seq)])


def z_move(value, step, seq):
    return lax.ppermute(value, "seq", [(i, i ^ (2 * step)) for i in range(seq)])


def dp_move(value, step, dps):
    return lax.ppermute(value, "dp", [(i, i ^ step) for i in range(dps)])


def tied(value, *others):
    return lax.optimization_barrier((value, others))[0]


def z_moves(value, seq):
    return [value] + [z_move(value, j, seq) for j in range(1, seq // 2)]


def gather_dp_direct(value, dps):
    return [value] + [dp_move(value, k, dps) for k in range(1, dps)]


def gather_dp_first(value, dps):
    return [value] + [dp_move(value, k, dps) for k in range(1, 3 if dps == 4 else dps)]


def gather_dp_halves(blocks, dps):
    if dps != 4:
        return []
    half = blocks[0].shape[0] // 2
    return [blocks[2][:half], blocks[1][half:]]


def gather_dp_rest(blocks, halves):
    return blocks + [dp_move(half, step, 4) for step, half in enumerate(halves, 1)]


def dp_pieces(dps, zs, direct):
    half = zs // 2
    for k in range(dps):
        for j in range(zs):
            if dps == 4 and k == 3 and not direct:
                yield (3, j, k, j) if j < half else (4, j - half, k, j)
            else:
                yield k, j, k, j


def scatter_slots(dps, zs):
    if dps != 4:
        return {(k, j): (k, j) for k in range(dps) for j in range(zs)}, [zs] * dps
    half = zs // 2
    slots = {}
    for j in range(half):
        low, high = j, half + j
        slots[0, low], slots[0, high] = (0, low), (0, high)
        slots[1, low], slots[3, low] = (1, low), (1, half + j)
        slots[2, high], slots[3, high] = (2, j), (2, half + j)
        slots[1, high] = (3, j)
        slots[2, low] = (4, j)
    return slots, [zs, zs, zs, half, half]


def wide_sum(terms):
    return functools.reduce(jnp.add, [t.astype(F32) for t in terms])


def scatter_dp_first(packs, dps):
    if dps != 4:
        return [dp_move(packs[k], k, dps) for k in range(1, dps)]
    return [dp_move(packs[1], 1, dps), dp_move(packs[2], 2, dps)]


def scatter_dp_middle(packs, came, dps):
    if dps != 4:
        return []
    half = packs[3].shape[0]
    return [
        wide_sum([packs[4], came[0][half:]]).astype(BF),
        wide_sum([packs[3], came[1][half:]]).astype(BF),
    ]


def scatter_dp_rest(packs, came, onward, dps, tie=lambda came: came):
    if dps != 4:
        came = tie(came)
        return [wide_sum([packs[0][j]] + [c[j] for c in came]) for j in range(packs[0].shape[0])]
    half = packs[3].shape[0]
    again_two, again_one = tie([dp_move(onward[0], 2, dps), dp_move(onward[1], 1, dps)])
    low = [wide_sum([packs[0][j], came[0][j], again_two[j]]) for j in range(half)]
    return low + [wide_sum([packs[0][half + j], came[1][j], again_one[j]]) for j in range(half)]


def scatter_z(totals, seq, tie=lambda moved: moved):
    moved = tie([z_move(totals[j].astype(BF), j, seq) for j in range(1, seq // 2)])
    return wide_sum([totals[0]] + moved)


def stacked_heads(pair_rows):
    lanes = lax.broadcasted_iota(jnp.int32, pair_rows.shape, 1)
    zero = jnp.zeros_like(pair_rows)
    return jnp.concatenate(
        [jnp.where(lanes < HD, pair_rows, zero), jnp.where(lanes < HD, zero, pair_rows)], axis=0
    )


def unstacked_heads(stacked):
    rows = stacked.shape[0] // 2
    lanes = lax.broadcasted_iota(jnp.int32, (rows, PAIR), 1)
    return jnp.where(lanes < HD, stacked[:rows], stacked[rows:])


def masked_scores(queries, keys, query_ids, key_ids):
    rows = query_ids.shape[0]
    bias = jnp.where(query_ids == key_ids, 0.0, NEGATIVE)
    scores = nt(queries, keys)
    return jnp.concatenate([scores[:rows] + bias, scores[rows:] + bias], axis=0)


def forward_kernel(qid_ref, kid_ref, q_ref, k_ref, v_ref, out_ref, lse_ref):
    rows = q_ref.shape[1] // 2

    @pl.loop(0, 2)
    def _(side):
        span = pl.ds(pl.multiple_of(side * rows, rows), rows)
        queries = stacked_heads(q_ref[0, span, :])
        scores = masked_scores(queries, k_ref[0], qid_ref[0, span, :][:, :1], kid_ref[0][:1, :])
        highest = jnp.max(scores, axis=-1, keepdims=True)
        weights = jnp.exp(scores - highest)
        total = jnp.sum(weights, axis=-1, keepdims=True)
        probs = (weights * (1.0 / total)).astype(BF)
        out_ref[0, span, :] = unstacked_heads(nn(probs, v_ref[0])).astype(BF)
        lse_ref[0, 0, side] = jnp.broadcast_to(highest + jnp.log(total), lse_ref.shape[3:])


def backward_kernel(
    qid_ref, kid_ref, q_ref, k_ref, v_ref, lse_ref, up_ref, dq_ref, dk_ref, dv_ref
):
    rows = q_ref.shape[1] // 2
    key_sum, value_sum = 0.0, 0.0
    for side in range(2):
        span = slice(side * rows, (side + 1) * rows)
        keys = k_ref[0]
        queries = stacked_heads(q_ref[0, span, :])
        upward = stacked_heads(up_ref[0, span, :])
        scores = masked_scores(queries, keys, qid_ref[0, span, :][:, :1], kid_ref[0][:1, :])
        probs = jnp.exp(scores - lse_ref[0, 0, side][:, :1])
        dprobs = nt(upward, v_ref[0])
        correction = jnp.sum(probs * dprobs, axis=-1, keepdims=True)
        dscores = (probs * (dprobs - correction)).astype(BF)
        back = unstacked_heads(nn(dscores, keys)).astype(BF).astype(F32)
        dq_ref[0, span, :] = (back * 0.125).astype(BF)
        key_sum += tn(dscores, queries)
        value_sum += tn(probs.astype(BF), upward)
    dk_ref[0] = key_sum.astype(BF)
    dv_ref[0] = value_sum.astype(BF)


def attention_specs(rows, count):
    return dict(
        qid=pl.BlockSpec((1, rows, 128), lambda s, p: (s, 0, 0)),
        kid=pl.BlockSpec((1, 8, count), lambda s, p: (s, 0, 0)),
        row=pl.BlockSpec((1, rows, PAIR), lambda s, p: (s, 0, p)),
        key=pl.BlockSpec((1, count, PAIR), lambda s, p: (s, 0, p)),
        value=pl.BlockSpec((1, count, PAIR), lambda s, p: (s, 0, PAIRS + p)),
        lse=pl.BlockSpec((1, 1, 2, rows, 128), lambda s, p: (s, p, 0, 0, 0)),
    )


def attend(query_ids, key_ids, queries, key_values):
    streams, rows, _ = queries.shape
    count = key_values.shape[1]
    specs = attention_specs(rows, count)
    macs = streams * 2 * PAIRS * rows * count * HD
    return pl.pallas_call(
        forward_kernel,
        grid=(streams, PAIRS),
        in_specs=[specs["qid"], specs["kid"], specs["row"], specs["key"], specs["value"]],
        out_specs=[specs["row"], specs["lse"]],
        out_shape=[
            jax.ShapeDtypeStruct((streams, rows, HALF), BF),
            jax.ShapeDtypeStruct((streams, PAIRS, 2, rows, 128), F32),
        ],
        compiler_params=pltpu.CompilerParams(vmem_limit_bytes=VMEM_LIMIT if count <= 1024 else VMEM_LARGE),
        cost_estimate=QUICK,
        name="attend",
    )(query_ids, key_ids, queries, key_values, key_values)


def attend_back(query_ids, key_ids, queries, key_values, lse, upward):
    streams, rows, _ = queries.shape
    count = key_values.shape[1]
    specs = attention_specs(rows, count)
    macs = streams * 2 * PAIRS * rows * count * HD
    key_shape = jax.ShapeDtypeStruct((streams, count, HALF), BF)
    return pl.pallas_call(
        backward_kernel,
        grid=(streams, PAIRS),
        in_specs=[
            specs["qid"],
            specs["kid"],
            specs["row"],
            specs["key"],
            specs["value"],
            specs["lse"],
            specs["row"],
        ],
        out_specs=[specs["row"], specs["key"], specs["key"]],
        out_shape=[jax.ShapeDtypeStruct((streams, rows, HALF), BF), key_shape, key_shape],
        compiler_params=pltpu.CompilerParams(vmem_limit_bytes=VMEM_LIMIT if count <= 1024 else VMEM_LARGE),
        cost_estimate=QUICK,
        name="attend_back",
    )(query_ids, key_ids, queries, key_values, key_values, lse, upward)


CHUNK = 384
QUERY_BIAS, VALUE_BIAS, OUT_BIAS, FIRST_GAIN, FIRST_SHIFT, REDUCE_BIAS, SECOND_GAIN, SECOND_SHIFT = range(8)


def norm_rows(value_rows):
    centre = jnp.mean(value_rows, axis=-1, keepdims=True)
    centred = value_rows - centre
    inverse = lax.rsqrt(jnp.mean(centred * centred, axis=-1, keepdims=True) + EPSILON)
    return (centred * inverse, inverse)


def norm_back(upward, normed, inverse):
    mean_up = jnp.mean(upward, axis=-1, keepdims=True)
    mean_cross = jnp.mean(upward * normed, axis=-1, keepdims=True)
    return inverse * (upward - mean_up - normed * mean_cross)


def add_rows(sum_ref, index, values):
    sum_ref[index] += jnp.sum(values.reshape(-1, 8, values.shape[1]), axis=0)


def vector_of(vec_ref, index):
    return vec_ref[index : index + 1, :]


def half_of_ref(place_ref):
    return pl.ds(pl.multiple_of(place_ref[2] * HALF, 128), HALF)


def other_half_of_ref(place_ref):
    return pl.ds(pl.multiple_of((1 - place_ref[2]) * HALF, 128), HALF)


def project(place, mine, other, vectors, weight):
    streams, rows, _ = mine[0].shape
    zs = len(mine)
    chip_rows = 2 * rows
    count = zs * chip_rows
    tile = min(count, 1024)

    def kernel(place_ref, *refs):
        mine_refs, other_refs, (vec_ref, weight_ref) = refs[:zs], refs[zs : 2 * zs], refs[2 * zs : 2 * zs + 2]
        all_ref, pairs_ref, query_ref, rows_ref = refs[2 * zs + 2 :]
        half = half_of_ref(place_ref)
        for j in range(zs):
            here = pl.ds(pl.multiple_of(j * chip_rows + place_ref[2] * rows, rows), rows)
            there = pl.ds(pl.multiple_of(j * chip_rows + (1 - place_ref[2]) * rows, rows), rows)
            for s in range(streams):
                all_ref[s, here, :] = mine_refs[j][s]
                all_ref[s, there, :] = other_refs[j][s]

        @pl.loop(0, streams)
        def _(s):
            for start in range(0, count, tile):
                span = slice(start, start + tile)
                pairs = nn(all_ref[s, span, :], weight_ref[:, HALF:])
                pairs_ref[s, span, :HALF] = pairs[:, :HALF].astype(BF)
                values = pairs[:, HALF:] + vec_ref[VALUE_BIAS : VALUE_BIAS + 1, half]
                pairs_ref[s, span, HALF:] = values.astype(BF)
            tokens = all_ref[s, :chip_rows, :]
            rows_ref[s] = tokens
            queries = nn(tokens, weight_ref[:, :HALF]) + vec_ref[QUERY_BIAS : QUERY_BIAS + 1, half]
            query_ref[s] = (queries * 0.125).astype(BF)

    shape = lambda rows, lanes: jax.ShapeDtypeStruct((streams, rows, lanes), BF)
    return pl.pallas_call(
        kernel,
        in_specs=[pl.BlockSpec(memory_space=pltpu.SMEM)]
        + [pl.BlockSpec(memory_space=pltpu.VMEM)] * (2 * zs + 2),
        out_specs=[pl.BlockSpec(memory_space=pltpu.VMEM)] * 4,
        out_shape=[shape(count, D), shape(count, D), shape(chip_rows, HALF), shape(chip_rows, D)],
        compiler_params=pltpu.CompilerParams(
            vmem_limit_bytes=VMEM_LIMIT if count <= 1024 else VMEM_LARGE
        ),
        cost_estimate=QUICK,
        name="project",
    )(place, *mine, *other, vectors, weight)


def unproject(place, query_back, key_back, value_back, weight):
    streams, count, _ = key_back.shape
    chip_rows = query_back.shape[1]
    rows = chip_rows // 2
    zs = count // chip_rows
    tile = min(count, 1024)

    def kernel(place_ref, query_ref, key_ref, value_ref, weight_ref, mine_ref, other_ref):
        first_core = place_ref[2] == 0

        @pl.loop(0, streams)
        def _(s):
            for start in range(0, count, tile):
                span = slice(start, start + tile)
                back = jnp.concatenate([key_ref[s, span, :], value_ref[s, span, :]], axis=1)
                total = nt(back, weight_ref[:, HALF:])
                for offset in range(0, tile, chip_rows):
                    j = (start + offset) // chip_rows
                    chip = total[offset : offset + chip_rows]
                    if j == 0:
                        chip += nt(query_ref[s], weight_ref[:, :HALF])
                    mine_ref[j, s] = jnp.where(first_core, chip[:rows], chip[rows:]).astype(BF)
                    other_ref[j, s] = jnp.where(first_core, chip[rows:], chip[:rows]).astype(BF)

    shape = jax.ShapeDtypeStruct((zs, streams, rows, D), BF)
    return pl.pallas_call(
        kernel,
        in_specs=[pl.BlockSpec(memory_space=pltpu.SMEM)]
        + [pl.BlockSpec(memory_space=pltpu.VMEM)] * 4,
        out_specs=[pl.BlockSpec(memory_space=pltpu.VMEM)] * 2,
        out_shape=[shape, shape],
        compiler_params=pltpu.CompilerParams(
            vmem_limit_bytes=VMEM_LIMIT if count <= 1024 else VMEM_LARGE
        ),
        cost_estimate=QUICK,
        name="unproject",
    )(place, query_back, key_back, value_back, weight)


def middle_kernel(
    place_ref, mine_ref, other_ref, tok_ref, vec_ref, unit_ref, out_ref, expand_ref, reduce_ref,
    normed_ref, inverse_ref, low_ref, hidden_ref, slope_ref, part_ref, send_ref,
):
    branch = nn(mine_ref[...], out_ref[half_of_ref(place_ref), :])
    branch += nn(other_ref[...], out_ref[other_half_of_ref(place_ref), :])
    branch += vector_of(vec_ref, OUT_BIAS)
    normed, inverse = norm_rows(tok_ref[...].astype(F32) + branch)
    normed_ref[...] = normed
    inverse_ref[...] = jnp.broadcast_to(inverse, inverse_ref.shape)
    first = normed * vector_of(vec_ref, FIRST_GAIN) + vector_of(vec_ref, FIRST_SHIFT)
    low = first.astype(BF)
    low_ref[...] = low
    total = jnp.zeros(part_ref.shape, F32)
    for start in range(0, UNITS, CHUNK):
        span = slice(start, start + CHUNK)
        expanded = nn(low, expand_ref[:, span]) + unit_ref[:, span]
        share = 0.5 * (1.0 + lax.erf(expanded * (0.5**0.5)))
        hidden = (expanded * share).astype(BF)
        hidden_ref[:, span] = hidden
        bell = jnp.exp(-0.5 * expanded * expanded) * 0.3989422804014327
        slope_ref[:, span] = (share + expanded * bell).astype(BF)
        total += nn(hidden, reduce_ref[span, :])
    part_ref[...] = total
    send_ref[...] = total.astype(BF)


def turn_kernel(
    place_ref, part_ref, came_ref, normed_ref, mine_ref, other_ref, slope_ref, vec_ref, reduce_ref, expand_ref,
    act_ref, residual_ref, low_ref, back_ref, next_ref, send_ref, sum_ref, unit_sum_ref,
):
    core = place_ref[2]
    first = normed_ref[...] * vector_of(vec_ref, FIRST_GAIN) + vector_of(vec_ref, FIRST_SHIFT)
    reduced = part_ref[...] + came_ref[...].astype(F32) + vector_of(vec_ref, REDUCE_BIAS)
    normed, inverse = norm_rows(first + reduced)
    gain = vector_of(vec_ref, SECOND_GAIN)
    half = normed.shape[0] // 2
    mine = jnp.where(core == 0, normed[:half], normed[half:])
    act_ref[...] = (mine * gain + vector_of(vec_ref, SECOND_SHIFT)).astype(BF)
    mine, other = mine_ref[...].astype(F32), other_ref[...].astype(F32)
    upward = jnp.concatenate(
        [jnp.where(core == 0, mine, other), jnp.where(core == 0, other, mine)], axis=0
    )
    residual = norm_back(upward * gain, normed, inverse)
    low = residual.astype(BF)
    residual_ref[...] = residual
    low_ref[...] = low
    add_rows(sum_ref, 0, low.astype(F32))
    add_rows(sum_ref, 1, upward * normed)
    add_rows(sum_ref, 2, upward)
    total = jnp.zeros(next_ref.shape, F32)
    for start in range(0, UNITS, CHUNK):
        span = slice(start, start + CHUNK)
        back = (nt(low, reduce_ref[span, :]) * slope_ref[:, span].astype(F32)).astype(BF)
        back_ref[:, span] = back
        unit_sum_ref[:, span] += jnp.sum(back.astype(F32).reshape(-1, 8, CHUNK), axis=0)
        total += nt(back, expand_ref[:, span])
    next_ref[...] = total
    send_ref[...] = total.astype(BF)


def first_back_kernel(
    place_ref, part_ref, came_ref, residual_ref, normed_ref, inverse_ref, vec_ref, out_ref,
    back_ref, low_ref, attended_ref, sum_ref,
):
    upward = part_ref[...] + came_ref[...].astype(F32) + residual_ref[...]
    normed = normed_ref[...]
    add_rows(sum_ref, 1, upward * normed)
    add_rows(sum_ref, 2, upward)
    back = norm_back(upward * vector_of(vec_ref, FIRST_GAIN), normed, inverse_ref[:, :1])
    low = back.astype(BF)
    half = back.shape[0] // 2
    back_ref[...] = jnp.where(place_ref[2] == 0, back[:half], back[half:])
    low_ref[...] = low
    add_rows(sum_ref, 0, low.astype(F32))
    attended_ref[...] = nt(low, out_ref[half_of_ref(place_ref), :]).astype(BF)


def over_rows(body, place, steps, tiled, whole, outs, sums, name):
    def tile_of(ref, step):
        rows = ref.shape[0] // steps
        return ref.at[pl.ds(pl.multiple_of(step * rows, rows), rows)]

    def kernel(place_ref, *refs):
        tiles, refs = refs[: len(tiled)], refs[len(tiled) :]
        kept, refs = refs[: len(whole)], refs[len(whole) :]
        results, totals = refs[: len(outs)], refs[len(outs) :]
        for total in totals:
            total[...] = jnp.zeros_like(total)

        @pl.loop(0, steps)
        def _(step):
            body(
                place_ref,
                *[tile_of(ref, step) for ref in tiles],
                *kept,
                *[tile_of(ref, step) for ref in results],
                *totals,
            )

    return pl.pallas_call(
        kernel,
        in_specs=[pl.BlockSpec(memory_space=pltpu.SMEM)]
        + [pl.BlockSpec(memory_space=pltpu.VMEM)] * (len(tiled) + len(whole)),
        out_specs=[pl.BlockSpec(memory_space=pltpu.VMEM)] * (len(outs) + len(sums)),
        out_shape=[jax.ShapeDtypeStruct(out[:2], out[2]) for out in outs]
        + [jax.ShapeDtypeStruct(shape, F32) for shape in sums],
        compiler_params=pltpu.CompilerParams(vmem_limit_bytes=VMEM_LIMIT),
        cost_estimate=QUICK,
        name=name,
    )(place, *tiled, *whole)


def packed_call(kernel, place, sources, shapes, scratch, name):
    return pl.pallas_call(
        kernel,
        in_specs=[pl.BlockSpec(memory_space=pltpu.SMEM)]
        + [pl.BlockSpec(memory_space=pltpu.VMEM)] * len(sources),
        out_specs=[pl.BlockSpec(memory_space=pltpu.VMEM)] * len(shapes),
        out_shape=[jax.ShapeDtypeStruct(shape, BF) for shape in shapes],
        scratch_shapes=scratch,
        compiler_params=pltpu.CompilerParams(vmem_limit_bytes=VMEM_LIMIT),
        cost_estimate=QUICK,
        name=name,
    )(place, *sources)


def wide_packs_of(place, hidden, reduced_back, first_low, expanded_back, dps, zs):
    chips = dps * zs
    both, wide = D // chips, UNITS // chips
    slots, counts = scatter_slots(dps, zs)
    lanes = 2 * D + UNITS

    def kernel(place_ref, hidden_ref, reduced_ref, low_ref, expanded_ref, *refs):
        outs, (reduce_ref, expand_ref) = refs[: len(counts)], refs[len(counts) :]
        for start in range(0, UNITS, CHUNK):
            span = slice(start, start + CHUNK)
            reduce_ref[span, :] = tn(hidden_ref[:, span], reduced_ref[...]).astype(BF)
        for start in range(0, D, 256):
            span = slice(start, start + 256)
            expand_ref[span, :] = tn(low_ref[:, span], expanded_ref[...]).astype(BF)
        for (k, j), (array, row) in slots.items():
            chip = (place_ref[0] ^ k) * zs + (place_ref[1] ^ j)
            first = pl.multiple_of(chip * wide, 16)
            outs[array][row, :, :D] = reduce_ref[pl.ds(first, both), :]
            outs[array][row, :, D : 2 * D] = reduce_ref[pl.ds(pl.multiple_of(first + both, 16), both), :]
            outs[array][row, :, 2 * D :] = expand_ref[pl.ds(pl.multiple_of(chip * both, 16), both), :]

    return packed_call(
        kernel,
        place,
        [hidden, reduced_back, first_low, expanded_back],
        [(count, both, lanes) for count in counts],
        [pltpu.VMEM((UNITS, D), BF), pltpu.VMEM((D, UNITS), BF)],
        "wide_packs",
    )


def narrow_packs_of(place, tokens, chip_tokens, backs, mine, other, branch_back, sums, dps, zs):
    chips = dps * zs
    both = D // chips
    slots, counts = scatter_slots(dps, zs)
    lanes = 4 * HALF + 128
    query_back, key_back, value_back = backs

    def kernel(
        place_ref, tok_ref, chip_ref, query_ref, key_ref, value_ref, mine_ref, other_ref, branch_ref,
        one_ref, two_ref, unit_ref, *refs,
    ):
        outs, (all_ref, square_ref) = refs[: len(counts)], refs[len(counts) :]
        half = half_of_ref(place_ref)
        for start in range(0, D, 256):
            span = slice(start, start + 256)
            turned = tok_ref[:, span].T
            all_ref[span, :HALF] = tn(chip_ref[:, span], query_ref[...]).astype(BF)
            all_ref[span, HALF : 2 * HALF] = nn(turned, key_ref[...]).astype(BF)
            all_ref[span, 2 * HALF : 3 * HALF] = nn(turned, value_ref[...]).astype(BF)
        branch = branch_ref[:, half]
        all_ref[half, 3 * HALF : 4 * HALF] = tn(mine_ref[...], branch).astype(BF)
        all_ref[other_half_of_ref(place_ref), 3 * HALF : 4 * HALF] = tn(other_ref[...], branch).astype(BF)
        square_ref[...] = jnp.zeros_like(square_ref)
        for row, ref in ((0, query_ref), (1, value_ref)):
            square_ref[row : row + 1, half] = jnp.sum(ref[...].astype(F32), axis=0, keepdims=True)
        for i in range(3):
            square_ref[2 + i : 3 + i, :] = jnp.sum(one_ref[i], axis=0, keepdims=True)
            square_ref[5 + i : 6 + i, :] = jnp.sum(two_ref[i], axis=0, keepdims=True)
        unit = jnp.sum(unit_ref[...], axis=0, keepdims=True)
        for chip in range(chips):
            for h in range(2):
                first = (2 * chip + h) * both
                square_ref[8 + h : 9 + h, chip * both : (chip + 1) * both] = unit[:, first : first + both]
        all_ref[:, 4 * HALF :] = square_ref[...].T.astype(BF)
        for (k, j), (array, row) in slots.items():
            chip = (place_ref[0] ^ k) * zs + (place_ref[1] ^ j)
            outs[array][row] = all_ref[pl.ds(pl.multiple_of(chip * both, 16), both), :]

    return packed_call(
        kernel,
        place,
        [tokens, chip_tokens, query_back, key_back, value_back, mine, other, branch_back, *sums],
        [(count, both, lanes) for count in counts],
        [pltpu.VMEM((D, lanes), BF), pltpu.VMEM((128, D), F32)],
        "narrow_packs",
    )


def column_sum(value_rows):
    return jnp.sum(value_rows.astype(F32), axis=0)


def item_ids(lengths, places):
    items = lengths.shape[1]
    slot = jnp.arange(items, dtype=jnp.int32)
    ends = jnp.sum(jnp.where(slot[:, None] <= slot[None, :], lengths[:, :, None], 0), axis=1)
    return jnp.sum((ends[:, None, :] <= places[None, :, None]).astype(jnp.int32), axis=2)


def body(
    tokens,
    query_weight,
    query_bias,
    key_weight,
    value_weight,
    value_bias,
    out_weight,
    out_bias,
    first_gain,
    attention_norm_shift,
    expand_weight,
    expand_bias,
    reduce_weight,
    reduce_bias,
    second_gain,
    second_shift,
    lengths,
    cotangent,
    *,
    dps,
    seq,
):
    streams, row_count, _ = tokens.shape
    zs = seq // 2
    chips = dps * zs
    block = D // (2 * chips)
    both = 2 * block
    wide = FF // (2 * chips)
    chip_rows = 2 * row_count
    rows = streams * chip_rows
    dp = lax.axis_index("dp")
    z = lax.axis_index("seq") // 2
    core = lax.axis_index("seq") % 2
    place = jnp.stack([dp, z, core]).astype(jnp.int32)
    swap = functools.partial(core_swap, seq=seq)

    def row_major(value):
        return with_layout_constraint(value, Layout(major_to_minor=tuple(range(value.ndim))))

    def in_core_order(mine, other, axis):
        return jnp.where(
            core == 0,
            jnp.concatenate([mine, other], axis=axis),
            jnp.concatenate([other, mine], axis=axis),
        )

    mine, theirs = first_columns(
        place,
        (query_weight, key_weight, value_weight),
        (
            query_bias,
            value_bias,
            out_bias,
            first_gain,
            attention_norm_shift,
            reduce_bias,
            second_gain,
            second_shift,
            expand_bias,
        ),
    )
    early = in_core_order(mine[None], swap(theirs)[None], 0)

    out_weight = out_weight.astype(BF)
    units = expand_weight.astype(BF).reshape(block, chips, 2, wide)

    def columns_for(side):
        unit = lax.dynamic_index_in_dim(units, side, 2, keepdims=False).reshape(block, UNITS)
        return jnp.concatenate([out_weight, unit], axis=1)

    late = in_core_order(columns_for(core)[None], swap(columns_for(1 - core))[None], 0)
    parts = reduce_weight.astype(BF).reshape(2, 2, block, D)
    late = jnp.concatenate([late, parts[:, 0], parts[:, 1]], axis=2)
    other_cotangent = swap(cotangent).reshape(-1, D)
    cotangent = cotangent.reshape(-1, D)
    other_tokens = swap(tokens)
    early = jnp.stack(tied(z_moves(early, seq), late, other_tokens, other_cotangent))
    late = z_moves(tied(late, early), seq)
    early, late = lax.optimization_barrier((gather_dp_first(early, dps), late))
    early = gather_dp_rest(early, gather_dp_halves(early, dps))
    moved = z_moves(tied(tokens, late), seq)
    late = gather_dp_first(jnp.stack(tied(late, early)), dps)

    def gather_plan(parts, direct=False):
        return [
            (
                piece,
                lambda dp, z, row=row, first=first, count=count: (
                    row,
                    Ellipsis,
                    at_lanes(first, count),
                ),
                target,
                lambda dp, z, j=j, k=k: (dp ^ k, z ^ j),
            )
            for piece, row, k, j in dp_pieces(dps, zs, direct)
            for first, count, target in parts
        ]

    qkv_weight, small = local_copies(
        place,
        early,
        [(dps, zs, 2, block, 3 * HALF), (dps, zs, 2, block, 128)],
        gather_plan([(0, 3 * HALF, 0), (3 * HALF, 128, 1)]),
        "place_early",
    )
    qkv_weight = qkv_weight.reshape(D, 3 * HALF)
    small = small.astype(F32).reshape(D, 128)[:, :12].T
    expand_bias = small[8:12].reshape(4, chips, 2, block)
    expand_bias = lax.dynamic_index_in_dim(expand_bias, core, 2, keepdims=False)
    expand_bias = expand_bias.transpose(1, 0, 2).reshape(1, UNITS)

    def half_of(vector):
        return lax.dynamic_slice_in_dim(vector, core * HALF, HALF, 1)

    qkv_weight = tied(qkv_weight, expand_bias)
    halves = gather_dp_halves(tied(late, qkv_weight), dps)
    late = gather_dp_rest(late, halves)
    others = [other_tokens] + [swap(m) for m in moved[1:]]

    all_tokens, key_values, queries, chip_tokens = project(
        place, moved, others, small, qkv_weight
    )
    flat_all = all_tokens.reshape(-1, D)
    spot = jnp.arange(row_count, dtype=jnp.int32)
    steps = jnp.arange(zs, dtype=jnp.int32) ^ z
    starts = (steps[:, None] * 2 + jnp.arange(2, dtype=jnp.int32)) * row_count
    ids = item_ids(lengths, (starts[:, :, None] + spot).reshape(-1))
    key_ids = jnp.broadcast_to(ids[:, None, :], (streams, 8, ids.shape[1]))
    query_ids = jnp.broadcast_to(ids[:, :chip_rows, None], (streams, chip_rows, 128))

    chip_tokens = chip_tokens.reshape(rows, D)
    queries = tied(queries, halves)
    attended, lse = attend(query_ids, key_ids, queries, key_values)
    other_attended = swap(attended).reshape(rows, HALF)
    attended = attended.reshape(rows, HALF)

    out_weight, expand_weight, reduce_weight = local_copies(
        place,
        late,
        [(dps, zs, 2, block, D), (dps, zs, 2, block, UNITS), (dps, zs, 4, block, D)],
        gather_plan([(0, D, 0), (D, UNITS, 1)])
        + [
            (
                piece,
                lambda dp, z, row=row, c=c, h=h: (row, c, slice(None), at_lanes(D + UNITS + h * D, D)),
                2,
                lambda dp, z, j=j, k=k, c=c, h=h: (dp ^ k, z ^ j, 2 * c + h),
            )
            for piece, row, k, j in dp_pieces(dps, zs, False)
            for c in range(2)
            for h in range(2)
        ],
        "place_late",
    )
    out_weight = out_weight.reshape(D, D)
    expand_weight = expand_weight.reshape(D, UNITS)
    reduce_weight = reduce_weight.reshape(UNITS, D)

    normed_one, inverse_one, first_low, hidden, slope, partial, sent = over_rows(
        middle_kernel,
        place,
        streams,
        [attended, other_attended, chip_tokens],
        [small, expand_bias, out_weight, expand_weight, reduce_weight],
        [
            (rows, D, F32),
            (rows, 128, F32),
            (rows, D, BF),
            (rows, UNITS, BF),
            (rows, UNITS, BF),
            (rows, D, F32),
            (rows, D, BF),
        ],
        [],
        "middle",
    )
    activations, residual_two_back, reduced_back, expanded_back, partial, sent, sums_two, unit_sums = over_rows(
        turn_kernel,
        place,
        streams,
        [partial, swap(sent), normed_one, cotangent, other_cotangent, slope],
        [small, reduce_weight, expand_weight],
        [
            (rows // 2, D, BF),
            (rows, D, F32),
            (rows, D, BF),
            (rows, UNITS, BF),
            (rows, D, F32),
            (rows, D, BF),
        ],
        [(3, 8, D), (8, UNITS)],
        "turn",
    )
    came_partial = swap(sent)
    fused = both % 16 == 0

    def scatter_plan(parts, lanes):
        slots, counts = scatter_slots(dps, zs)
        plan = [
            (
                source,
                lambda dp, z, j=j, k=k, index=index: index(dp ^ k, z ^ j),
                array,
                lambda dp, z, row=row, first=first, count=count: (
                    row,
                    slice(None),
                    at_lanes(first, count),
                ),
            )
            for (k, j), (array, row) in slots.items()
            for source, index, first, count in parts
        ]
        return [(count, both, lanes) for count in counts], plan

    if fused:
        wide_packs = wide_packs_of(place, hidden, reduced_back, first_low, expanded_back, dps, zs)
    else:
        wide_packs = local_copies(
            place,
            [
                tn(hidden, reduced_back).astype(BF).reshape(dps, zs, 2, both, D),
                tn(first_low, expanded_back).astype(BF).reshape(dps, zs, both, UNITS),
            ],
            *scatter_plan(
                [
                    (0, lambda d, zz: (d, zz, 0), 0, D),
                    (0, lambda d, zz: (d, zz, 1), D, D),
                    (1, lambda d, zz: (d, zz), 2 * D, UNITS),
                ],
                2 * D + UNITS,
            ),
            "pack_wide",
        )
    wide_came = scatter_dp_first(wide_packs, dps)

    residual_one_back, branch_back, attended_back, sums_one = over_rows(
        first_back_kernel,
        place,
        streams,
        [partial, came_partial, residual_two_back, normed_one, inverse_one],
        [small, out_weight],
        [(rows // 2, D, F32), (rows, D, BF), (rows, HALF, BF)],
        [(3, 8, D)],
        "first_back",
    )
    attended_back = attended_back.reshape(streams, chip_rows, HALF)

    query_back, key_back, value_back = attend_back(
        query_ids, key_ids, queries, key_values, lse, attended_back
    )
    mine_part, other_part = unproject(place, query_back, key_back, value_back, qkv_weight)
    came_part = swap(other_part)
    wide_came = tied(wide_came, other_part)
    wide_onward = scatter_dp_middle(wide_packs, wide_came, dps)
    mine_part, came_part = tied((mine_part, came_part), wide_onward)
    tokens_total = wide_sum([mine_part, came_part])
    tokens_first = tokens_total[zs // 2 :].astype(BF)

    def halved(total, bit, sent):
        return total[:bit] + z_move(sent, bit, seq).astype(F32)

    tokens_total = halved(tokens_total, zs // 2, tokens_first)
    backs = (query_back.reshape(rows, HALF), key_back.reshape(-1, HALF), value_back.reshape(-1, HALF))
    backs = tied(backs, tokens_first)
    if fused:
        narrow_packs = narrow_packs_of(
            place,
            flat_all,
            chip_tokens,
            backs,
            attended,
            other_attended,
            branch_back,
            (sums_one, sums_two, unit_sums),
            dps,
            zs,
        )
        wide_totals = scatter_dp_rest(
            wide_packs, wide_came, wide_onward, dps, lambda came: tied(came, narrow_packs)
        )
    else:
        out_side = half_of(branch_back)
        zeros = jnp.zeros((D,), F32)
        small_grads = jnp.concatenate(
            [
                lax.dynamic_update_slice_in_dim(zeros, column_sum(backs[0]), core * HALF, 0)[None],
                lax.dynamic_update_slice_in_dim(zeros, column_sum(backs[2]), core * HALF, 0)[None],
                jnp.sum(sums_one, axis=1),
                jnp.sum(sums_two, axis=1),
                jnp.sum(unit_sums, axis=0).reshape(chips, 2, both).transpose(1, 0, 2).reshape(2, D),
            ],
            axis=0,
        ).T.astype(BF)
        small_grads = jnp.pad(small_grads, ((0, 0), (0, 128 - small_grads.shape[1])))
        four = (
            tn(chip_tokens, backs[0]).astype(BF),
            tn(flat_all, backs[1]).astype(BF),
            tn(flat_all, backs[2]).astype(BF),
            in_core_order(tn(attended, out_side), tn(other_attended, out_side), 0).astype(BF),
        )
        wide_totals = scatter_dp_rest(wide_packs, wide_came, wide_onward, dps)
        narrow_packs = local_copies(
            place,
            [g.reshape(dps, zs, both, HALF) for g in four] + [small_grads.reshape(dps, zs, both, 128)],
            *scatter_plan(
                [(i, lambda d, zz: (d, zz), i * HALF, HALF) for i in range(4)]
                + [(4, lambda d, zz: (d, zz), 4 * HALF, 128)],
                4 * HALF + 128,
            ),
            "pack_narrow",
        )
    came = tied(scatter_dp_first(narrow_packs, dps), wide_totals)
    narrow_onward = scatter_dp_middle(narrow_packs, came, dps)
    narrow_totals = scatter_dp_rest(narrow_packs, came, narrow_onward, dps)
    wide_grads = scatter_z(tied(wide_totals, tokens_total), seq)
    bit = zs // 4
    while bit:
        tokens_total = halved(tokens_total, bit, tokens_total[bit:].astype(BF))
        bit //= 2
    narrow_totals, tokens_total, wide_grads = lax.optimization_barrier(
        (narrow_totals, tokens_total, wide_grads)
    )
    narrow_grads = scatter_z(narrow_totals, seq)
    tokens_gradient = residual_one_back.reshape(tokens.shape) + tokens_total[0]

    def own_rows(grads):
        split = grads.reshape(2, block, grads.shape[1])
        mine = lax.dynamic_index_in_dim(split, core, 0, keepdims=False)
        return mine, swap(lax.dynamic_index_in_dim(split, 1 - core, 0, keepdims=False))

    mine, other = own_rows(wide_grads[:, 2 * D :])
    expand_grads = in_core_order(
        mine.reshape(block, chips, 1, wide), other.reshape(block, chips, 1, wide), 2
    ).reshape(block, FF)
    reduce_grads = jnp.concatenate([wide_grads[:, :D], wide_grads[:, D : 2 * D]], axis=0)
    mine, other = own_rows(narrow_grads)
    matrices = [
        in_core_order(mine[:, i * HALF : (i + 1) * HALF], other[:, i * HALF : (i + 1) * HALF], 1)
        for i in range(4)
    ]
    own_small = mine[:, 4 * HALF :].T
    both_small = (mine[:, 4 * HALF : 4 * HALF + 2] + other[:, 4 * HALF : 4 * HALF + 2]).T
    expand_bias_grad = narrow_grads[:, 4 * HALF :][:, 8:10].T.reshape(wide)

    return (
        activations.reshape(tokens.shape),
        tokens_gradient,
        matrices[0],
        both_small[0],
        matrices[1],
        matrices[2],
        both_small[1],
        matrices[3],
        own_small[2],
        own_small[3],
        own_small[4],
        expand_grads,
        expand_bias_grad,
        reduce_grads,
        own_small[5],
        own_small[6],
        own_small[7],
    )


def solution(mesh):
    sharded = ("dp", "seq")
    matrix = P(sharded, None)
    vector = P(sharded)
    token = P("dp", "seq", None)
    params = (
        matrix,
        vector,
        matrix,
        matrix,
        vector,
        matrix,
        vector,
        vector,
        vector,
        matrix,
        vector,
        matrix,
        vector,
        vector,
        vector,
    )
    return jax.shard_map(
        functools.partial(body, dps=mesh.shape["dp"], seq=mesh.shape["seq"]),
        mesh=mesh,
        in_specs=(token,) + params + (P("dp", None), token),
        out_specs=(token, token) + params,
        check_vma=False,
    )
```

```python
import functools

import jax
import jax.numpy as jnp
from jax import lax
from jax.experimental.layout import Layout, with_layout_constraint
from jax.experimental import pallas as pl
from jax.experimental.pallas import tpu as pltpu
from jax.sharding import PartitionSpec as P

D = 768
HEADS = 12
HD = 64
FF = 3072
HALF = D // 2
UNITS = FF // 2
PAIR = 2 * HD
PAIRS = HALF // PAIR
NEGATIVE = -1e30
EPSILON = 1e-12
BF = jnp.bfloat16
F32 = jnp.float32
VMEM_LIMIT = 28 * 1024 * 1024
VMEM_LARGE = 56 * 1024 * 1024
QUICK = pl.CostEstimate(flops=0, bytes_accessed=0, transcendentals=0)


def nn(left, right):
    return lax.dot_general(left, right, (((1,), (0,)), ((), ())), preferred_element_type=F32)


def nt(left, right):
    return lax.dot_general(left, right, (((1,), (1,)), ((), ())), preferred_element_type=F32)


def tn(left, right):
    return lax.dot_general(left, right, (((0,), (0,)), ((), ())), preferred_element_type=F32)


def local_copies(place, sources, shapes, plan, name, late=()):
    def kernel(place_ref, *refs):
        ins = refs[: len(sources)]
        outs = refs[len(sources) + len(late) :]
        dp = place_ref[0]
        z = place_ref[1]
        for source, source_index, target, target_index in plan:
            outs[target][target_index(dp, z)] = ins[source][source_index(dp, z)]

    moved = 2 * sum(functools.reduce(lambda a, b: a * b, s) for s in shapes)
    return pl.pallas_call(
        kernel,
        in_specs=[pl.BlockSpec(memory_space=pltpu.SMEM)]
        + [pl.BlockSpec(memory_space=pltpu.VMEM)] * len(sources)
        + [pl.BlockSpec(memory_space=pl.ANY)] * len(late),
        out_specs=[pl.BlockSpec(memory_space=pltpu.VMEM)] * len(shapes),
        out_shape=[jax.ShapeDtypeStruct(shape, BF) for shape in shapes],
        compiler_params=pltpu.CompilerParams(vmem_limit_bytes=VMEM_LIMIT),
        cost_estimate=QUICK,
        name=name,
    )(place, *sources, *late)


def first_columns(place, weights, vectors):
    block = weights[0].shape[0]
    lanes = len(weights) * HALF + 128

    def kernel(place_ref, *refs):
        ins, (mine_ref, theirs_ref, square_ref) = refs[: len(weights) + len(vectors)], refs[-3:]
        core = place_ref[2]
        square_ref[...] = jnp.zeros_like(square_ref)
        row = 0
        for ref in ins[len(weights) :]:
            for part in range(ref.shape[0] // block):
                square_ref[row : row + 1, 0:block] = ref[part * block : (part + 1) * block].reshape(1, block)
                row += 1
        columns = square_ref[...].T[:block].astype(BF)
        for out, side in ((mine_ref, core), (theirs_ref, 1 - core)):
            for i in range(len(weights)):
                picked = ins[i][:, pl.ds(pl.multiple_of(side * HALF, 128), HALF)]
                out[:, i * HALF : (i + 1) * HALF] = picked.astype(BF)
            out[:, len(weights) * HALF :] = columns

    shape = jax.ShapeDtypeStruct((block, lanes), BF)
    return pl.pallas_call(
        kernel,
        in_specs=[pl.BlockSpec(memory_space=pltpu.SMEM)]
        + [pl.BlockSpec(memory_space=pltpu.VMEM)] * (len(weights) + len(vectors)),
        out_specs=[pl.BlockSpec(memory_space=pltpu.VMEM)] * 2,
        out_shape=[shape, shape],
        scratch_shapes=[pltpu.VMEM((128, 128), F32)],
        name="first_columns",
    )(place, *weights, *vectors)


def at_lanes(start, count):
    return pl.ds(start, count)


def core_swap(value, seq):
    return lax.ppermute(value, "seq", [(i, i ^ 1) for i in range(seq)])


def z_move(value, step, seq):
    return lax.ppermute(value, "seq", [(i, i ^ (2 * step)) for i in range(seq)])


def dp_move(value, step, dps):
    return lax.ppermute(value, "dp", [(i, i ^ step) for i in range(dps)])


def tied(value, *others):
    return lax.optimization_barrier((value, others))[0]


def z_moves(value, seq):
    return [value] + [z_move(value, j, seq) for j in range(1, seq // 2)]


def gather_dp_direct(value, dps):
    return [value] + [dp_move(value, k, dps) for k in range(1, dps)]


def gather_dp_first(value, dps):
    return [value] + [dp_move(value, k, dps) for k in range(1, 3 if dps == 4 else dps)]


def gather_dp_halves(blocks, dps):
    if dps != 4:
        return []
    half = blocks[0].shape[0] // 2
    return [blocks[2][:half], blocks[1][half:]]


def gather_dp_rest(blocks, halves):
    return blocks + [dp_move(half, step, 4) for step, half in enumerate(halves, 1)]


def dp_pieces(dps, zs, direct):
    half = zs // 2
    for k in range(dps):
        for j in range(zs):
            if dps == 4 and k == 3 and not direct:
                yield (3, j, k, j) if j < half else (4, j - half, k, j)
            else:
                yield k, j, k, j


def scatter_slots(dps, zs):
    if dps != 4:
        return {(k, j): (k, j) for k in range(dps) for j in range(zs)}, [zs] * dps
    half = zs // 2
    slots = {}
    for j in range(half):
        low, high = j, half + j
        slots[0, low], slots[0, high] = (0, low), (0, high)
        slots[1, low], slots[3, low] = (1, low), (1, half + j)
        slots[2, high], slots[3, high] = (2, j), (2, half + j)
        slots[1, high] = (3, j)
        slots[2, low] = (4, j)
    return slots, [zs, zs, zs, half, half]


def wide_sum(terms):
    return functools.reduce(jnp.add, [t.astype(F32) for t in terms])


def scatter_dp_first(packs, dps):
    if dps != 4:
        return [dp_move(packs[k], k, dps) for k in range(1, dps)]
    return [dp_move(packs[1], 1, dps), dp_move(packs[2], 2, dps)]


def scatter_dp_middle(packs, came, dps):
    if dps != 4:
        return []
    half = packs[3].shape[0]
    return [
        wide_sum([packs[4], came[0][half:]]).astype(BF),
        wide_sum([packs[3], came[1][half:]]).astype(BF),
    ]


def scatter_dp_rest(packs, came, onward, dps, tie=lambda came: came):
    if dps != 4:
        came = tie(came)
        return [wide_sum([packs[0][j]] + [c[j] for c in came]) for j in range(packs[0].shape[0])]
    half = packs[3].shape[0]
    again_two, again_one = tie([dp_move(onward[0], 2, dps), dp_move(onward[1], 1, dps)])
    low = [wide_sum([packs[0][j], came[0][j], again_two[j]]) for j in range(half)]
    return low + [wide_sum([packs[0][half + j], came[1][j], again_one[j]]) for j in range(half)]


def scatter_z(totals, seq, tie=lambda moved: moved):
    moved = tie([z_move(totals[j].astype(BF), j, seq) for j in range(1, seq // 2)])
    return wide_sum([totals[0]] + moved)


def stacked_heads(pair_rows):
    lanes = lax.broadcasted_iota(jnp.int32, pair_rows.shape, 1)
    zero = jnp.zeros_like(pair_rows)
    return jnp.concatenate(
        [jnp.where(lanes < HD, pair_rows, zero), jnp.where(lanes < HD, zero, pair_rows)], axis=0
    )


def unstacked_heads(stacked):
    rows = stacked.shape[0] // 2
    lanes = lax.broadcasted_iota(jnp.int32, (rows, PAIR), 1)
    return jnp.where(lanes < HD, stacked[:rows], stacked[rows:])


def masked_scores(queries, keys, query_ids, key_ids):
    rows = query_ids.shape[0]
    bias = jnp.where(query_ids == key_ids, 0.0, NEGATIVE)
    scores = nt(queries, keys)
    return jnp.concatenate([scores[:rows] + bias, scores[rows:] + bias], axis=0)


def forward_kernel(qid_ref, kid_ref, q_ref, k_ref, v_ref, out_ref, lse_ref):
    rows = q_ref.shape[1] // 2

    @pl.loop(0, 2)
    def _(side):
        span = pl.ds(pl.multiple_of(side * rows, rows), rows)
        queries = stacked_heads(q_ref[0, span, :])
        scores = masked_scores(queries, k_ref[0], qid_ref[0, span, :][:, :1], kid_ref[0][:1, :])
        highest = jnp.max(scores, axis=-1, keepdims=True)
        weights = jnp.exp(scores - highest)
        total = jnp.sum(weights, axis=-1, keepdims=True)
        probs = (weights * (1.0 / total)).astype(BF)
        out_ref[0, span, :] = unstacked_heads(nn(probs, v_ref[0])).astype(BF)
        lse_ref[0, 0, side] = jnp.broadcast_to(highest + jnp.log(total), lse_ref.shape[3:])


def backward_kernel(
    qid_ref, kid_ref, q_ref, k_ref, v_ref, lse_ref, up_ref, dq_ref, dk_ref, dv_ref
):
    rows = q_ref.shape[1] // 2
    key_sum, value_sum = 0.0, 0.0
    for side in range(2):
        span = slice(side * rows, (side + 1) * rows)
        keys = k_ref[0]
        queries = stacked_heads(q_ref[0, span, :])
        upward = stacked_heads(up_ref[0, span, :])
        scores = masked_scores(queries, keys, qid_ref[0, span, :][:, :1], kid_ref[0][:1, :])
        probs = jnp.exp(scores - lse_ref[0, 0, side][:, :1])
        dprobs = nt(upward, v_ref[0])
        correction = jnp.sum(probs * dprobs, axis=-1, keepdims=True)
        dscores = (probs * (dprobs - correction)).astype(BF)
        back = unstacked_heads(nn(dscores, keys)).astype(BF).astype(F32)
        dq_ref[0, span, :] = (back * 0.125).astype(BF)
        key_sum += tn(dscores, queries)
        value_sum += tn(probs.astype(BF), upward)
    dk_ref[0] = key_sum.astype(BF)
    dv_ref[0] = value_sum.astype(BF)


def attention_specs(rows, count):
    return dict(
        qid=pl.BlockSpec((1, rows, 128), lambda s, p: (s, 0, 0)),
        kid=pl.BlockSpec((1, 8, count), lambda s, p: (s, 0, 0)),
        row=pl.BlockSpec((1, rows, PAIR), lambda s, p: (s, 0, p)),
        key=pl.BlockSpec((1, count, PAIR), lambda s, p: (s, 0, p)),
        value=pl.BlockSpec((1, count, PAIR), lambda s, p: (s, 0, PAIRS + p)),
        lse=pl.BlockSpec((1, 1, 2, rows, 128), lambda s, p: (s, p, 0, 0, 0)),
    )


def attend(query_ids, key_ids, queries, key_values):
    streams, rows, _ = queries.shape
    count = key_values.shape[1]
    specs = attention_specs(rows, count)
    macs = streams * 2 * PAIRS * rows * count * HD
    return pl.pallas_call(
        forward_kernel,
        grid=(streams, PAIRS),
        in_specs=[specs["qid"], specs["kid"], specs["row"], specs["key"], specs["value"]],
        out_specs=[specs["row"], specs["lse"]],
        out_shape=[
            jax.ShapeDtypeStruct((streams, rows, HALF), BF),
            jax.ShapeDtypeStruct((streams, PAIRS, 2, rows, 128), F32),
        ],
        compiler_params=pltpu.CompilerParams(vmem_limit_bytes=VMEM_LIMIT if count <= 1024 else VMEM_LARGE),
        cost_estimate=QUICK,
        name="attend",
    )(query_ids, key_ids, queries, key_values, key_values)


def attend_back(query_ids, key_ids, queries, key_values, lse, upward):
    streams, rows, _ = queries.shape
    count = key_values.shape[1]
    specs = attention_specs(rows, count)
    macs = streams * 2 * PAIRS * rows * count * HD
    key_shape = jax.ShapeDtypeStruct((streams, count, HALF), BF)
    return pl.pallas_call(
        backward_kernel,
        grid=(streams, PAIRS),
        in_specs=[
            specs["qid"],
            specs["kid"],
            specs["row"],
            specs["key"],
            specs["value"],
            specs["lse"],
            specs["row"],
        ],
        out_specs=[specs["row"], specs["key"], specs["key"]],
        out_shape=[jax.ShapeDtypeStruct((streams, rows, HALF), BF), key_shape, key_shape],
        compiler_params=pltpu.CompilerParams(vmem_limit_bytes=VMEM_LIMIT if count <= 1024 else VMEM_LARGE),
        cost_estimate=QUICK,
        name="attend_back",
    )(query_ids, key_ids, queries, key_values, key_values, lse, upward)


CHUNK = 768
QUERY_BIAS, VALUE_BIAS, OUT_BIAS, FIRST_GAIN, FIRST_SHIFT, REDUCE_BIAS, SECOND_GAIN, SECOND_SHIFT = range(8)


def norm_rows(value_rows):
    centre = jnp.mean(value_rows, axis=-1, keepdims=True)
    centred = value_rows - centre
    inverse = lax.rsqrt(jnp.mean(centred * centred, axis=-1, keepdims=True) + EPSILON)
    return (centred * inverse, inverse)


def norm_back(upward, normed, inverse):
    mean_up = jnp.mean(upward, axis=-1, keepdims=True)
    mean_cross = jnp.mean(upward * normed, axis=-1, keepdims=True)
    return inverse * (upward - mean_up - normed * mean_cross)


def add_rows(sum_ref, index, values):
    sum_ref[index] += jnp.sum(values.reshape(-1, 8, values.shape[1]), axis=0)


def vector_of(vec_ref, index):
    return vec_ref[index : index + 1, :]


def half_of_ref(place_ref):
    return pl.ds(pl.multiple_of(place_ref[2] * HALF, 128), HALF)


def other_half_of_ref(place_ref):
    return pl.ds(pl.multiple_of((1 - place_ref[2]) * HALF, 128), HALF)


def project(place, mine, other, vectors, weight):
    streams, rows, _ = mine[0].shape
    zs = len(mine)
    chip_rows = 2 * rows
    count = zs * chip_rows
    tile = min(count, 1024)

    def kernel(place_ref, *refs):
        mine_refs, other_refs, (vec_ref, weight_ref) = refs[:zs], refs[zs : 2 * zs], refs[2 * zs : 2 * zs + 2]
        all_ref, pairs_ref, query_ref, rows_ref = refs[2 * zs + 2 :]
        half = half_of_ref(place_ref)
        for j in range(zs):
            here = pl.ds(pl.multiple_of(j * chip_rows + place_ref[2] * rows, rows), rows)
            there = pl.ds(pl.multiple_of(j * chip_rows + (1 - place_ref[2]) * rows, rows), rows)
            for s in range(streams):
                all_ref[s, here, :] = mine_refs[j][s]
                all_ref[s, there, :] = other_refs[j][s]

        @pl.loop(0, streams)
        def _(s):
            for start in range(0, count, tile):
                span = slice(start, start + tile)
                pairs = nn(all_ref[s, span, :], weight_ref[:, HALF:])
                pairs_ref[s, span, :HALF] = pairs[:, :HALF].astype(BF)
                values = pairs[:, HALF:] + vec_ref[VALUE_BIAS : VALUE_BIAS + 1, half]
                pairs_ref[s, span, HALF:] = values.astype(BF)
            tokens = all_ref[s, :chip_rows, :]
            rows_ref[s] = tokens
            queries = nn(tokens, weight_ref[:, :HALF]) + vec_ref[QUERY_BIAS : QUERY_BIAS + 1, half]
            query_ref[s] = (queries * 0.125).astype(BF)

    shape = lambda rows, lanes: jax.ShapeDtypeStruct((streams, rows, lanes), BF)
    return pl.pallas_call(
        kernel,
        in_specs=[pl.BlockSpec(memory_space=pltpu.SMEM)]
        + [pl.BlockSpec(memory_space=pltpu.VMEM)] * (2 * zs + 2),
        out_specs=[pl.BlockSpec(memory_space=pltpu.VMEM)] * 4,
        out_shape=[shape(count, D), shape(count, D), shape(chip_rows, HALF), shape(chip_rows, D)],
        compiler_params=pltpu.CompilerParams(
            vmem_limit_bytes=VMEM_LIMIT if count <= 1024 else VMEM_LARGE
        ),
        cost_estimate=QUICK,
        name="project",
    )(place, *mine, *other, vectors, weight)


def unproject(place, query_back, key_back, value_back, weight):
    streams, count, _ = key_back.shape
    chip_rows = query_back.shape[1]
    rows = chip_rows // 2
    zs = count // chip_rows
    tile = min(count, 1024)

    def kernel(place_ref, query_ref, key_ref, value_ref, weight_ref, mine_ref, other_ref):
        first_core = place_ref[2] == 0

        @pl.loop(0, streams)
        def _(s):
            for start in range(0, count, tile):
                span = slice(start, start + tile)
                back = jnp.concatenate([key_ref[s, span, :], value_ref[s, span, :]], axis=1)
                total = nt(back, weight_ref[:, HALF:])
                for offset in range(0, tile, chip_rows):
                    j = (start + offset) // chip_rows
                    chip = total[offset : offset + chip_rows]
                    if j == 0:
                        chip += nt(query_ref[s], weight_ref[:, :HALF])
                    mine_ref[j, s] = jnp.where(first_core, chip[:rows], chip[rows:]).astype(BF)
                    other_ref[j, s] = jnp.where(first_core, chip[rows:], chip[:rows]).astype(BF)

    shape = jax.ShapeDtypeStruct((zs, streams, rows, D), BF)
    return pl.pallas_call(
        kernel,
        in_specs=[pl.BlockSpec(memory_space=pltpu.SMEM)]
        + [pl.BlockSpec(memory_space=pltpu.VMEM)] * 4,
        out_specs=[pl.BlockSpec(memory_space=pltpu.VMEM)] * 2,
        out_shape=[shape, shape],
        compiler_params=pltpu.CompilerParams(
            vmem_limit_bytes=VMEM_LIMIT if count <= 1024 else VMEM_LARGE
        ),
        cost_estimate=QUICK,
        name="unproject",
    )(place, query_back, key_back, value_back, weight)


def middle_kernel(
    place_ref, mine_ref, other_ref, tok_ref, vec_ref, unit_ref, out_ref, expand_ref, reduce_ref,
    normed_ref, inverse_ref, low_ref, hidden_ref, slope_ref, part_ref, send_ref,
):
    branch = nn(mine_ref[...], out_ref[half_of_ref(place_ref), :])
    branch += nn(other_ref[...], out_ref[other_half_of_ref(place_ref), :])
    branch += vector_of(vec_ref, OUT_BIAS)
    normed, inverse = norm_rows(tok_ref[...].astype(F32) + branch)
    normed_ref[...] = normed
    inverse_ref[...] = jnp.broadcast_to(inverse, inverse_ref.shape)
    first = normed * vector_of(vec_ref, FIRST_GAIN) + vector_of(vec_ref, FIRST_SHIFT)
    low = first.astype(BF)
    low_ref[...] = low
    total = jnp.zeros(part_ref.shape, F32)
    for start in range(0, UNITS, CHUNK):
        span = slice(start, start + CHUNK)
        expanded = nn(low, expand_ref[:, span]) + unit_ref[:, span]
        share = 0.5 * (1.0 + lax.erf(expanded * (0.5**0.5)))
        hidden = (expanded * share).astype(BF)
        hidden_ref[:, span] = hidden
        bell = jnp.exp(-0.5 * expanded * expanded) * 0.3989422804014327
        slope_ref[:, span] = (share + expanded * bell).astype(BF)
        total += nn(hidden, reduce_ref[span, :])
    part_ref[...] = total
    send_ref[...] = total.astype(BF)


def turn_kernel(
    place_ref, part_ref, came_ref, normed_ref, mine_ref, other_ref, slope_ref, vec_ref, reduce_ref, expand_ref,
    act_ref, residual_ref, low_ref, back_ref, next_ref, send_ref, sum_ref, unit_sum_ref,
):
    core = place_ref[2]
    first = normed_ref[...] * vector_of(vec_ref, FIRST_GAIN) + vector_of(vec_ref, FIRST_SHIFT)
    reduced = part_ref[...] + came_ref[...].astype(F32) + vector_of(vec_ref, REDUCE_BIAS)
    normed, inverse = norm_rows(first + reduced)
    gain = vector_of(vec_ref, SECOND_GAIN)
    half = normed.shape[0] // 2
    mine = jnp.where(core == 0, normed[:half], normed[half:])
    act_ref[...] = (mine * gain + vector_of(vec_ref, SECOND_SHIFT)).astype(BF)
    mine, other = mine_ref[...].astype(F32), other_ref[...].astype(F32)
    upward = jnp.concatenate(
        [jnp.where(core == 0, mine, other), jnp.where(core == 0, other, mine)], axis=0
    )
    residual = norm_back(upward * gain, normed, inverse)
    low = residual.astype(BF)
    residual_ref[...] = residual
    low_ref[...] = low
    add_rows(sum_ref, 0, low.astype(F32))
    add_rows(sum_ref, 1, upward * normed)
    add_rows(sum_ref, 2, upward)
    total = jnp.zeros(next_ref.shape, F32)
    for start in range(0, UNITS, CHUNK):
        span = slice(start, start + CHUNK)
        back = (nt(low, reduce_ref[span, :]) * slope_ref[:, span].astype(F32)).astype(BF)
        back_ref[:, span] = back
        unit_sum_ref[:, span] += jnp.sum(back.astype(F32).reshape(-1, 8, CHUNK), axis=0)
        total += nt(back, expand_ref[:, span])
    next_ref[...] = total
    send_ref[...] = total.astype(BF)


def first_back_kernel(
    place_ref, part_ref, came_ref, residual_ref, normed_ref, inverse_ref, vec_ref, out_ref,
    back_ref, low_ref, attended_ref, sum_ref,
):
    upward = part_ref[...] + came_ref[...].astype(F32) + residual_ref[...]
    normed = normed_ref[...]
    add_rows(sum_ref, 1, upward * normed)
    add_rows(sum_ref, 2, upward)
    back = norm_back(upward * vector_of(vec_ref, FIRST_GAIN), normed, inverse_ref[:, :1])
    low = back.astype(BF)
    half = back.shape[0] // 2
    back_ref[...] = jnp.where(place_ref[2] == 0, back[:half], back[half:])
    low_ref[...] = low
    add_rows(sum_ref, 0, low.astype(F32))
    attended_ref[...] = nt(low, out_ref[half_of_ref(place_ref), :]).astype(BF)


def over_rows(body, place, steps, tiled, whole, outs, sums, name):
    def tile_of(ref, step):
        rows = ref.shape[0] // steps
        return ref.at[pl.ds(pl.multiple_of(step * rows, rows), rows)]

    def kernel(place_ref, *refs):
        tiles, refs = refs[: len(tiled)], refs[len(tiled) :]
        kept, refs = refs[: len(whole)], refs[len(whole) :]
        results, totals = refs[: len(outs)], refs[len(outs) :]
        for total in totals:
            total[...] = jnp.zeros_like(total)

        @pl.loop(0, steps)
        def _(step):
            body(
                place_ref,
                *[tile_of(ref, step) for ref in tiles],
                *kept,
                *[tile_of(ref, step) for ref in results],
                *totals,
            )

    return pl.pallas_call(
        kernel,
        in_specs=[pl.BlockSpec(memory_space=pltpu.SMEM)]
        + [pl.BlockSpec(memory_space=pltpu.VMEM)] * (len(tiled) + len(whole)),
        out_specs=[pl.BlockSpec(memory_space=pltpu.VMEM)] * (len(outs) + len(sums)),
        out_shape=[jax.ShapeDtypeStruct(out[:2], out[2]) for out in outs]
        + [jax.ShapeDtypeStruct(shape, F32) for shape in sums],
        compiler_params=pltpu.CompilerParams(vmem_limit_bytes=VMEM_LIMIT),
        cost_estimate=QUICK,
        name=name,
    )(place, *tiled, *whole)


def packed_call(kernel, place, sources, shapes, scratch, name):
    return pl.pallas_call(
        kernel,
        in_specs=[pl.BlockSpec(memory_space=pltpu.SMEM)]
        + [pl.BlockSpec(memory_space=pltpu.VMEM)] * len(sources),
        out_specs=[pl.BlockSpec(memory_space=pltpu.VMEM)] * len(shapes),
        out_shape=[jax.ShapeDtypeStruct(shape, BF) for shape in shapes],
        scratch_shapes=scratch,
        compiler_params=pltpu.CompilerParams(vmem_limit_bytes=VMEM_LIMIT),
        cost_estimate=QUICK,
        name=name,
    )(place, *sources)


def wide_packs_of(place, hidden, reduced_back, first_low, expanded_back, dps, zs):
    chips = dps * zs
    both, wide = D // chips, UNITS // chips
    slots, counts = scatter_slots(dps, zs)
    lanes = 2 * D + UNITS

    def kernel(place_ref, hidden_ref, reduced_ref, low_ref, expanded_ref, *refs):
        outs, (reduce_ref, expand_ref) = refs[: len(counts)], refs[len(counts) :]
        for start in range(0, UNITS, CHUNK):
            span = slice(start, start + CHUNK)
            reduce_ref[span, :] = tn(hidden_ref[:, span], reduced_ref[...]).astype(BF)
        for start in range(0, D, 256):
            span = slice(start, start + 256)
            expand_ref[span, :] = tn(low_ref[:, span], expanded_ref[...]).astype(BF)
        for (k, j), (array, row) in slots.items():
            chip = (place_ref[0] ^ k) * zs + (place_ref[1] ^ j)
            first = pl.multiple_of(chip * wide, 16)
            outs[array][row, :, :D] = reduce_ref[pl.ds(first, both), :]
            outs[array][row, :, D : 2 * D] = reduce_ref[pl.ds(pl.multiple_of(first + both, 16), both), :]
            outs[array][row, :, 2 * D :] = expand_ref[pl.ds(pl.multiple_of(chip * both, 16), both), :]

    return packed_call(
        kernel,
        place,
        [hidden, reduced_back, first_low, expanded_back],
        [(count, both, lanes) for count in counts],
        [pltpu.VMEM((UNITS, D), BF), pltpu.VMEM((D, UNITS), BF)],
        "wide_packs",
    )


def narrow_packs_of(place, tokens, chip_tokens, backs, mine, other, branch_back, sums, dps, zs):
    chips = dps * zs
    both = D // chips
    slots, counts = scatter_slots(dps, zs)
    lanes = 4 * HALF + 128
    query_back, key_back, value_back = backs

    def kernel(
        place_ref, tok_ref, chip_ref, query_ref, key_ref, value_ref, mine_ref, other_ref, branch_ref,
        one_ref, two_ref, unit_ref, *refs,
    ):
        outs, (all_ref, square_ref) = refs[: len(counts)], refs[len(counts) :]
        half = half_of_ref(place_ref)
        for start in range(0, D, 256):
            span = slice(start, start + 256)
            turned = tok_ref[:, span].T
            all_ref[span, :HALF] = tn(chip_ref[:, span], query_ref[...]).astype(BF)
            all_ref[span, HALF : 2 * HALF] = nn(turned, key_ref[...]).astype(BF)
            all_ref[span, 2 * HALF : 3 * HALF] = nn(turned, value_ref[...]).astype(BF)
        branch = branch_ref[:, half]
        all_ref[half, 3 * HALF : 4 * HALF] = tn(mine_ref[...], branch).astype(BF)
        all_ref[other_half_of_ref(place_ref), 3 * HALF : 4 * HALF] = tn(other_ref[...], branch).astype(BF)
        square_ref[...] = jnp.zeros_like(square_ref)
        for row, ref in ((0, query_ref), (1, value_ref)):
            square_ref[row : row + 1, half] = jnp.sum(ref[...].astype(F32), axis=0, keepdims=True)
        for i in range(3):
            square_ref[2 + i : 3 + i, :] = jnp.sum(one_ref[i], axis=0, keepdims=True)
            square_ref[5 + i : 6 + i, :] = jnp.sum(two_ref[i], axis=0, keepdims=True)
        unit = jnp.sum(unit_ref[...], axis=0, keepdims=True)
        for chip in range(chips):
            for h in range(2):
                first = (2 * chip + h) * both
                square_ref[8 + h : 9 + h, chip * both : (chip + 1) * both] = unit[:, first : first + both]
        all_ref[:, 4 * HALF :] = square_ref[...].T.astype(BF)
        for (k, j), (array, row) in slots.items():
            chip = (place_ref[0] ^ k) * zs + (place_ref[1] ^ j)
            outs[array][row] = all_ref[pl.ds(pl.multiple_of(chip * both, 16), both), :]

    return packed_call(
        kernel,
        place,
        [tokens, chip_tokens, query_back, key_back, value_back, mine, other, branch_back, *sums],
        [(count, both, lanes) for count in counts],
        [pltpu.VMEM((D, lanes), BF), pltpu.VMEM((128, D), F32)],
        "narrow_packs",
    )


def column_sum(value_rows):
    return jnp.sum(value_rows.astype(F32), axis=0)


def item_ids(lengths, places):
    items = lengths.shape[1]
    slot = jnp.arange(items, dtype=jnp.int32)
    ends = jnp.sum(jnp.where(slot[:, None] <= slot[None, :], lengths[:, :, None], 0), axis=1)
    return jnp.sum((ends[:, None, :] <= places[None, :, None]).astype(jnp.int32), axis=2)


def body(
    tokens,
    query_weight,
    query_bias,
    key_weight,
    value_weight,
    value_bias,
    out_weight,
    out_bias,
    first_gain,
    attention_norm_shift,
    expand_weight,
    expand_bias,
    reduce_weight,
    reduce_bias,
    second_gain,
    second_shift,
    lengths,
    cotangent,
    *,
    dps,
    seq,
):
    streams, row_count, _ = tokens.shape
    zs = seq // 2
    chips = dps * zs
    block = D // (2 * chips)
    both = 2 * block
    wide = FF // (2 * chips)
    chip_rows = 2 * row_count
    rows = streams * chip_rows
    dp = lax.axis_index("dp")
    z = lax.axis_index("seq") // 2
    core = lax.axis_index("seq") % 2
    place = jnp.stack([dp, z, core]).astype(jnp.int32)
    swap = functools.partial(core_swap, seq=seq)

    def row_major(value):
        return with_layout_constraint(value, Layout(major_to_minor=tuple(range(value.ndim))))

    def in_core_order(mine, other, axis):
        return jnp.where(
            core == 0,
            jnp.concatenate([mine, other], axis=axis),
            jnp.concatenate([other, mine], axis=axis),
        )

    mine, theirs = first_columns(
        place,
        (query_weight, key_weight, value_weight),
        (
            query_bias,
            value_bias,
            out_bias,
            first_gain,
            attention_norm_shift,
            reduce_bias,
            second_gain,
            second_shift,
            expand_bias,
        ),
    )
    early = in_core_order(mine[None], swap(theirs)[None], 0)

    out_weight = out_weight.astype(BF)
    units = expand_weight.astype(BF).reshape(block, chips, 2, wide)

    def columns_for(side):
        unit = lax.dynamic_index_in_dim(units, side, 2, keepdims=False).reshape(block, UNITS)
        return jnp.concatenate([out_weight, unit], axis=1)

    late = in_core_order(columns_for(core)[None], swap(columns_for(1 - core))[None], 0)
    parts = reduce_weight.astype(BF).reshape(2, 2, block, D)
    late = jnp.concatenate([late, parts[:, 0], parts[:, 1]], axis=2)
    other_cotangent = swap(cotangent).reshape(-1, D)
    cotangent = cotangent.reshape(-1, D)
    other_tokens = swap(tokens)
    early = jnp.stack(tied(z_moves(early, seq), late, other_tokens, other_cotangent))
    late = z_moves(tied(late, early), seq)
    early, late = lax.optimization_barrier((gather_dp_first(early, dps), late))
    early = gather_dp_rest(early, gather_dp_halves(early, dps))
    moved = z_moves(tied(tokens, late), seq)
    late = gather_dp_first(jnp.stack(tied(late, early)), dps)

    def gather_plan(parts, direct=False):
        return [
            (
                piece,
                lambda dp, z, row=row, first=first, count=count: (
                    row,
                    Ellipsis,
                    at_lanes(first, count),
                ),
                target,
                lambda dp, z, j=j, k=k: (dp ^ k, z ^ j),
            )
            for piece, row, k, j in dp_pieces(dps, zs, direct)
            for first, count, target in parts
        ]

    qkv_weight, small = local_copies(
        place,
        early,
        [(dps, zs, 2, block, 3 * HALF), (dps, zs, 2, block, 128)],
        gather_plan([(0, 3 * HALF, 0), (3 * HALF, 128, 1)]),
        "place_early",
    )
    qkv_weight = qkv_weight.reshape(D, 3 * HALF)
    small = small.astype(F32).reshape(D, 128)[:, :12].T
    expand_bias = small[8:12].reshape(4, chips, 2, block)
    expand_bias = lax.dynamic_index_in_dim(expand_bias, core, 2, keepdims=False)
    expand_bias = expand_bias.transpose(1, 0, 2).reshape(1, UNITS)

    def half_of(vector):
        return lax.dynamic_slice_in_dim(vector, core * HALF, HALF, 1)

    qkv_weight = tied(qkv_weight, expand_bias)
    halves = gather_dp_halves(tied(late, qkv_weight), dps)
    late = gather_dp_rest(late, halves)
    others = [other_tokens] + [swap(m) for m in moved[1:]]

    all_tokens, key_values, queries, chip_tokens = project(
        place, moved, others, small, qkv_weight
    )
    flat_all = all_tokens.reshape(-1, D)
    spot = jnp.arange(row_count, dtype=jnp.int32)
    steps = jnp.arange(zs, dtype=jnp.int32) ^ z
    starts = (steps[:, None] * 2 + jnp.arange(2, dtype=jnp.int32)) * row_count
    ids = item_ids(lengths, (starts[:, :, None] + spot).reshape(-1))
    key_ids = jnp.broadcast_to(ids[:, None, :], (streams, 8, ids.shape[1]))
    query_ids = jnp.broadcast_to(ids[:, :chip_rows, None], (streams, chip_rows, 128))

    chip_tokens = chip_tokens.reshape(rows, D)
    queries = tied(queries, halves)
    attended, lse = attend(query_ids, key_ids, queries, key_values)
    other_attended = swap(attended).reshape(rows, HALF)
    attended = attended.reshape(rows, HALF)

    out_weight, expand_weight, reduce_weight = local_copies(
        place,
        late,
        [(dps, zs, 2, block, D), (dps, zs, 2, block, UNITS), (dps, zs, 4, block, D)],
        gather_plan([(0, D, 0), (D, UNITS, 1)])
        + [
            (
                piece,
                lambda dp, z, row=row, c=c, h=h: (row, c, slice(None), at_lanes(D + UNITS + h * D, D)),
                2,
                lambda dp, z, j=j, k=k, c=c, h=h: (dp ^ k, z ^ j, 2 * c + h),
            )
            for piece, row, k, j in dp_pieces(dps, zs, False)
            for c in range(2)
            for h in range(2)
        ],
        "place_late",
    )
    out_weight = out_weight.reshape(D, D)
    expand_weight = expand_weight.reshape(D, UNITS)
    reduce_weight = reduce_weight.reshape(UNITS, D)

    normed_one, inverse_one, first_low, hidden, slope, partial, sent = over_rows(
        middle_kernel,
        place,
        streams,
        [attended, other_attended, chip_tokens],
        [small, expand_bias, out_weight, expand_weight, reduce_weight],
        [
            (rows, D, F32),
            (rows, 128, F32),
            (rows, D, BF),
            (rows, UNITS, BF),
            (rows, UNITS, BF),
            (rows, D, F32),
            (rows, D, BF),
        ],
        [],
        "middle",
    )
    activations, residual_two_back, reduced_back, expanded_back, partial, sent, sums_two, unit_sums = over_rows(
        turn_kernel,
        place,
        streams,
        [partial, swap(sent), normed_one, cotangent, other_cotangent, slope],
        [small, reduce_weight, expand_weight],
        [
            (rows // 2, D, BF),
            (rows, D, F32),
            (rows, D, BF),
            (rows, UNITS, BF),
            (rows, D, F32),
            (rows, D, BF),
        ],
        [(3, 8, D), (8, UNITS)],
        "turn",
    )
    came_partial = swap(sent)
    fused = both % 16 == 0

    def scatter_plan(parts, lanes):
        slots, counts = scatter_slots(dps, zs)
        plan = [
            (
                source,
                lambda dp, z, j=j, k=k, index=index: index(dp ^ k, z ^ j),
                array,
                lambda dp, z, row=row, first=first, count=count: (
                    row,
                    slice(None),
                    at_lanes(first, count),
                ),
            )
            for (k, j), (array, row) in slots.items()
            for source, index, first, count in parts
        ]
        return [(count, both, lanes) for count in counts], plan

    if fused:
        wide_packs = wide_packs_of(place, hidden, reduced_back, first_low, expanded_back, dps, zs)
    else:
        wide_packs = local_copies(
            place,
            [
                tn(hidden, reduced_back).astype(BF).reshape(dps, zs, 2, both, D),
                tn(first_low, expanded_back).astype(BF).reshape(dps, zs, both, UNITS),
            ],
            *scatter_plan(
                [
                    (0, lambda d, zz: (d, zz, 0), 0, D),
                    (0, lambda d, zz: (d, zz, 1), D, D),
                    (1, lambda d, zz: (d, zz), 2 * D, UNITS),
                ],
                2 * D + UNITS,
            ),
            "pack_wide",
        )
    wide_came = scatter_dp_first(wide_packs, dps)

    residual_one_back, branch_back, attended_back, sums_one = over_rows(
        first_back_kernel,
        place,
        streams,
        [partial, came_partial, residual_two_back, normed_one, inverse_one],
        [small, out_weight],
        [(rows // 2, D, F32), (rows, D, BF), (rows, HALF, BF)],
        [(3, 8, D)],
        "first_back",
    )
    attended_back = attended_back.reshape(streams, chip_rows, HALF)

    query_back, key_back, value_back = attend_back(
        query_ids, key_ids, queries, key_values, lse, attended_back
    )
    mine_part, other_part = unproject(place, query_back, key_back, value_back, qkv_weight)
    came_part = swap(other_part)
    wide_came = tied(wide_came, other_part)
    wide_onward = scatter_dp_middle(wide_packs, wide_came, dps)
    mine_part, came_part = tied((mine_part, came_part), wide_onward)
    tokens_total = wide_sum([mine_part, came_part])
    tokens_first = tokens_total[zs // 2 :].astype(BF)

    def halved(total, bit, sent):
        return total[:bit] + z_move(sent, bit, seq).astype(F32)

    tokens_total = halved(tokens_total, zs // 2, tokens_first)
    backs = (query_back.reshape(rows, HALF), key_back.reshape(-1, HALF), value_back.reshape(-1, HALF))
    backs = tied(backs, tokens_first)
    if fused:
        narrow_packs = narrow_packs_of(
            place,
            flat_all,
            chip_tokens,
            backs,
            attended,
            other_attended,
            branch_back,
            (sums_one, sums_two, unit_sums),
            dps,
            zs,
        )
        wide_totals = scatter_dp_rest(
            wide_packs, wide_came, wide_onward, dps, lambda came: tied(came, narrow_packs)
        )
    else:
        out_side = half_of(branch_back)
        zeros = jnp.zeros((D,), F32)
        small_grads = jnp.concatenate(
            [
                lax.dynamic_update_slice_in_dim(zeros, column_sum(backs[0]), core * HALF, 0)[None],
                lax.dynamic_update_slice_in_dim(zeros, column_sum(backs[2]), core * HALF, 0)[None],
                jnp.sum(sums_one, axis=1),
                jnp.sum(sums_two, axis=1),
                jnp.sum(unit_sums, axis=0).reshape(chips, 2, both).transpose(1, 0, 2).reshape(2, D),
            ],
            axis=0,
        ).T.astype(BF)
        small_grads = jnp.pad(small_grads, ((0, 0), (0, 128 - small_grads.shape[1])))
        four = (
            tn(chip_tokens, backs[0]).astype(BF),
            tn(flat_all, backs[1]).astype(BF),
            tn(flat_all, backs[2]).astype(BF),
            in_core_order(tn(attended, out_side), tn(other_attended, out_side), 0).astype(BF),
        )
        wide_totals = scatter_dp_rest(wide_packs, wide_came, wide_onward, dps)
        narrow_packs = local_copies(
            place,
            [g.reshape(dps, zs, both, HALF) for g in four] + [small_grads.reshape(dps, zs, both, 128)],
            *scatter_plan(
                [(i, lambda d, zz: (d, zz), i * HALF, HALF) for i in range(4)]
                + [(4, lambda d, zz: (d, zz), 4 * HALF, 128)],
                4 * HALF + 128,
            ),
            "pack_narrow",
        )
    came = tied(scatter_dp_first(narrow_packs, dps), wide_totals)
    narrow_onward = scatter_dp_middle(narrow_packs, came, dps)
    narrow_totals = scatter_dp_rest(narrow_packs, came, narrow_onward, dps)
    wide_grads = scatter_z(tied(wide_totals, tokens_total), seq)
    bit = zs // 4
    while bit:
        tokens_total = halved(tokens_total, bit, tokens_total[bit:].astype(BF))
        bit //= 2
    narrow_totals, tokens_total, wide_grads = lax.optimization_barrier(
        (narrow_totals, tokens_total, wide_grads)
    )
    narrow_grads = scatter_z(narrow_totals, seq)
    tokens_gradient = residual_one_back.reshape(tokens.shape) + tokens_total[0]

    def own_rows(grads):
        split = grads.reshape(2, block, grads.shape[1])
        mine = lax.dynamic_index_in_dim(split, core, 0, keepdims=False)
        return mine, swap(lax.dynamic_index_in_dim(split, 1 - core, 0, keepdims=False))

    mine, other = own_rows(wide_grads[:, 2 * D :])
    expand_grads = in_core_order(
        mine.reshape(block, chips, 1, wide), other.reshape(block, chips, 1, wide), 2
    ).reshape(block, FF)
    reduce_grads = jnp.concatenate([wide_grads[:, :D], wide_grads[:, D : 2 * D]], axis=0)
    mine, other = own_rows(narrow_grads)
    matrices = [
        in_core_order(mine[:, i * HALF : (i + 1) * HALF], other[:, i * HALF : (i + 1) * HALF], 1)
        for i in range(4)
    ]
    own_small = mine[:, 4 * HALF :].T
    both_small = (mine[:, 4 * HALF : 4 * HALF + 2] + other[:, 4 * HALF : 4 * HALF + 2]).T
    expand_bias_grad = narrow_grads[:, 4 * HALF :][:, 8:10].T.reshape(wide)

    return (
        activations.reshape(tokens.shape),
        tokens_gradient,
        matrices[0],
        both_small[0],
        matrices[1],
        matrices[2],
        both_small[1],
        matrices[3],
        own_small[2],
        own_small[3],
        own_small[4],
        expand_grads,
        expand_bias_grad,
        reduce_grads,
        own_small[5],
        own_small[6],
        own_small[7],
    )


def solution(mesh):
    sharded = ("dp", "seq")
    matrix = P(sharded, None)
    vector = P(sharded)
    token = P("dp", "seq", None)
    params = (
        matrix,
        vector,
        matrix,
        matrix,
        vector,
        matrix,
        vector,
        vector,
        vector,
        matrix,
        vector,
        matrix,
        vector,
        vector,
        vector,
    )
    return jax.shard_map(
        functools.partial(body, dps=mesh.shape["dp"], seq=mesh.shape["seq"]),
        mesh=mesh,
        in_specs=(token,) + params + (P("dp", None), token),
        out_specs=(token, token) + params,
        check_vma=False,
    )
```

```python
import functools

import jax
import jax.numpy as jnp
from jax import lax
from jax.experimental.layout import Layout, with_layout_constraint
from jax.experimental import pallas as pl
from jax.experimental.pallas import tpu as pltpu
from jax.sharding import PartitionSpec as P

D = 768
HEADS = 12
HD = 64
FF = 3072
HALF = D // 2
UNITS = FF // 2
PAIR = 2 * HD
PAIRS = HALF // PAIR
NEGATIVE = -1e30
EPSILON = 1e-12
BF = jnp.bfloat16
F32 = jnp.float32
VMEM_LIMIT = 28 * 1024 * 1024
VMEM_LARGE = 56 * 1024 * 1024
QUICK = pl.CostEstimate(flops=0, bytes_accessed=0, transcendentals=0)


def nn(left, right):
    return lax.dot_general(left, right, (((1,), (0,)), ((), ())), preferred_element_type=F32)


def nt(left, right):
    return lax.dot_general(left, right, (((1,), (1,)), ((), ())), preferred_element_type=F32)


def tn(left, right):
    return lax.dot_general(left, right, (((0,), (0,)), ((), ())), preferred_element_type=F32)


def local_copies(place, sources, shapes, plan, name, late=()):
    def kernel(place_ref, *refs):
        ins = refs[: len(sources)]
        outs = refs[len(sources) + len(late) :]
        dp = place_ref[0]
        z = place_ref[1]
        for source, source_index, target, target_index in plan:
            outs[target][target_index(dp, z)] = ins[source][source_index(dp, z)]

    moved = 2 * sum(functools.reduce(lambda a, b: a * b, s) for s in shapes)
    return pl.pallas_call(
        kernel,
        in_specs=[pl.BlockSpec(memory_space=pltpu.SMEM)]
        + [pl.BlockSpec(memory_space=pltpu.VMEM)] * len(sources)
        + [pl.BlockSpec(memory_space=pl.ANY)] * len(late),
        out_specs=[pl.BlockSpec(memory_space=pltpu.VMEM)] * len(shapes),
        out_shape=[jax.ShapeDtypeStruct(shape, BF) for shape in shapes],
        compiler_params=pltpu.CompilerParams(vmem_limit_bytes=VMEM_LIMIT),
        cost_estimate=QUICK,
        name=name,
    )(place, *sources, *late)


def first_columns(place, weights, vectors):
    block = weights[0].shape[0]
    lanes = len(weights) * HALF + 128

    def kernel(place_ref, *refs):
        ins, (mine_ref, theirs_ref, square_ref) = refs[: len(weights) + len(vectors)], refs[-3:]
        core = place_ref[2]
        square_ref[...] = jnp.zeros_like(square_ref)
        row = 0
        for ref in ins[len(weights) :]:
            for part in range(ref.shape[0] // block):
                square_ref[row : row + 1, 0:block] = ref[part * block : (part + 1) * block].reshape(1, block)
                row += 1
        columns = square_ref[...].T[:block].astype(BF)
        for out, side in ((mine_ref, core), (theirs_ref, 1 - core)):
            for i in range(len(weights)):
                picked = ins[i][:, pl.ds(pl.multiple_of(side * HALF, 128), HALF)]
                out[:, i * HALF : (i + 1) * HALF] = picked.astype(BF)
            out[:, len(weights) * HALF :] = columns

    shape = jax.ShapeDtypeStruct((block, lanes), BF)
    return pl.pallas_call(
        kernel,
        in_specs=[pl.BlockSpec(memory_space=pltpu.SMEM)]
        + [pl.BlockSpec(memory_space=pltpu.VMEM)] * (len(weights) + len(vectors)),
        out_specs=[pl.BlockSpec(memory_space=pltpu.VMEM)] * 2,
        out_shape=[shape, shape],
        scratch_shapes=[pltpu.VMEM((128, 128), F32)],
        name="first_columns",
    )(place, *weights, *vectors)


def at_lanes(start, count):
    return pl.ds(start, count)


def core_swap(value, seq):
    return lax.ppermute(value, "seq", [(i, i ^ 1) for i in range(seq)])


def z_move(value, step, seq):
    return lax.ppermute(value, "seq", [(i, i ^ (2 * step)) for i in range(seq)])


def dp_move(value, step, dps):
    return lax.ppermute(value, "dp", [(i, i ^ step) for i in range(dps)])


def tied(value, *others):
    return lax.optimization_barrier((value, others))[0]


def z_moves(value, seq):
    return [value] + [z_move(value, j, seq) for j in range(1, seq // 2)]


def gather_dp_direct(value, dps):
    return [value] + [dp_move(value, k, dps) for k in range(1, dps)]


def gather_dp_first(value, dps):
    return [value] + [dp_move(value, k, dps) for k in range(1, 3 if dps == 4 else dps)]


def gather_dp_halves(blocks, dps):
    if dps != 4:
        return []
    half = blocks[0].shape[0] // 2
    return [blocks[2][:half], blocks[1][half:]]


def gather_dp_rest(blocks, halves):
    return blocks + [dp_move(half, step, 4) for step, half in enumerate(halves, 1)]


def dp_pieces(dps, zs, direct):
    half = zs // 2
    for k in range(dps):
        for j in range(zs):
            if dps == 4 and k == 3 and not direct:
                yield (3, j, k, j) if j < half else (4, j - half, k, j)
            else:
                yield k, j, k, j


def scatter_slots(dps, zs):
    if dps != 4:
        return {(k, j): (k, j) for k in range(dps) for j in range(zs)}, [zs] * dps
    half = zs // 2
    slots = {}
    for j in range(half):
        low, high = j, half + j
        slots[0, low], slots[0, high] = (0, low), (0, high)
        slots[1, low], slots[3, low] = (1, low), (1, half + j)
        slots[2, high], slots[3, high] = (2, j), (2, half + j)
        slots[1, high] = (3, j)
        slots[2, low] = (4, j)
    return slots, [zs, zs, zs, half, half]


def wide_sum(terms):
    return functools.reduce(jnp.add, [t.astype(F32) for t in terms])


def scatter_dp_first(packs, dps):
    if dps != 4:
        return [dp_move(packs[k], k, dps) for k in range(1, dps)]
    return [dp_move(packs[1], 1, dps), dp_move(packs[2], 2, dps)]


def scatter_dp_middle(packs, came, dps):
    if dps != 4:
        return []
    half = packs[3].shape[0]
    return [
        wide_sum([packs[4], came[0][half:]]).astype(BF),
        wide_sum([packs[3], came[1][half:]]).astype(BF),
    ]


def scatter_dp_rest(packs, came, onward, dps, tie=lambda came: came):
    if dps != 4:
        came = tie(came)
        return [wide_sum([packs[0][j]] + [c[j] for c in came]) for j in range(packs[0].shape[0])]
    half = packs[3].shape[0]
    again_two, again_one = tie([dp_move(onward[0], 2, dps), dp_move(onward[1], 1, dps)])
    low = [wide_sum([packs[0][j], came[0][j], again_two[j]]) for j in range(half)]
    return low + [wide_sum([packs[0][half + j], came[1][j], again_one[j]]) for j in range(half)]


def scatter_z(totals, seq, tie=lambda moved: moved):
    moved = tie([z_move(totals[j].astype(BF), j, seq) for j in range(1, seq // 2)])
    return wide_sum([totals[0]] + moved)


def stacked_heads(pair_rows):
    lanes = lax.broadcasted_iota(jnp.int32, pair_rows.shape, 1)
    zero = jnp.zeros_like(pair_rows)
    return jnp.concatenate(
        [jnp.where(lanes < HD, pair_rows, zero), jnp.where(lanes < HD, zero, pair_rows)], axis=0
    )


def unstacked_heads(stacked):
    rows = stacked.shape[0] // 2
    lanes = lax.broadcasted_iota(jnp.int32, (rows, PAIR), 1)
    return jnp.where(lanes < HD, stacked[:rows], stacked[rows:])


def masked_scores(queries, keys, query_ids, key_ids):
    rows = query_ids.shape[0]
    bias = jnp.where(query_ids == key_ids, 0.0, NEGATIVE)
    scores = nt(queries, keys)
    return jnp.concatenate([scores[:rows] + bias, scores[rows:] + bias], axis=0)


def forward_kernel(qid_ref, kid_ref, q_ref, k_ref, v_ref, out_ref, lse_ref):
    rows = q_ref.shape[1] // 2

    @pl.loop(0, 2)
    def _(side):
        span = pl.ds(pl.multiple_of(side * rows, rows), rows)
        queries = stacked_heads(q_ref[0, span, :])
        scores = masked_scores(queries, k_ref[0], qid_ref[0, span, :][:, :1], kid_ref[0][:1, :])
        highest = jnp.max(scores, axis=-1, keepdims=True)
        weights = jnp.exp(scores - highest)
        total = jnp.sum(weights, axis=-1, keepdims=True)
        probs = (weights * (1.0 / total)).astype(BF)
        out_ref[0, span, :] = unstacked_heads(nn(probs, v_ref[0])).astype(BF)
        lse_ref[0, 0, side] = jnp.broadcast_to(highest + jnp.log(total), lse_ref.shape[3:])


def backward_kernel(
    qid_ref, kid_ref, q_ref, k_ref, v_ref, lse_ref, up_ref, dq_ref, dk_ref, dv_ref
):
    rows = q_ref.shape[1] // 2
    key_sum, value_sum = 0.0, 0.0
    for side in range(2):
        span = slice(side * rows, (side + 1) * rows)
        keys = k_ref[0]
        queries = stacked_heads(q_ref[0, span, :])
        upward = stacked_heads(up_ref[0, span, :])
        scores = masked_scores(queries, keys, qid_ref[0, span, :][:, :1], kid_ref[0][:1, :])
        probs = jnp.exp(scores - lse_ref[0, 0, side][:, :1])
        dprobs = nt(upward, v_ref[0])
        correction = jnp.sum(probs * dprobs, axis=-1, keepdims=True)
        dscores = (probs * (dprobs - correction)).astype(BF)
        back = unstacked_heads(nn(dscores, keys)).astype(BF).astype(F32)
        dq_ref[0, span, :] = (back * 0.125).astype(BF)
        key_sum += tn(dscores, queries)
        value_sum += tn(probs.astype(BF), upward)
    dk_ref[0] = key_sum.astype(BF)
    dv_ref[0] = value_sum.astype(BF)


def attention_specs(rows, count):
    return dict(
        qid=pl.BlockSpec((1, rows, 128), lambda s, p: (s, 0, 0)),
        kid=pl.BlockSpec((1, 8, count), lambda s, p: (s, 0, 0)),
        row=pl.BlockSpec((1, rows, PAIR), lambda s, p: (s, 0, p)),
        key=pl.BlockSpec((1, count, PAIR), lambda s, p: (s, 0, p)),
        value=pl.BlockSpec((1, count, PAIR), lambda s, p: (s, 0, PAIRS + p)),
        lse=pl.BlockSpec((1, 1, 2, rows, 128), lambda s, p: (s, p, 0, 0, 0)),
    )


def attend(query_ids, key_ids, queries, key_values):
    streams, rows, _ = queries.shape
    count = key_values.shape[1]
    specs = attention_specs(rows, count)
    macs = streams * 2 * PAIRS * rows * count * HD
    return pl.pallas_call(
        forward_kernel,
        grid=(streams, PAIRS),
        in_specs=[specs["qid"], specs["kid"], specs["row"], specs["key"], specs["value"]],
        out_specs=[specs["row"], specs["lse"]],
        out_shape=[
            jax.ShapeDtypeStruct((streams, rows, HALF), BF),
            jax.ShapeDtypeStruct((streams, PAIRS, 2, rows, 128), F32),
        ],
        compiler_params=pltpu.CompilerParams(vmem_limit_bytes=VMEM_LIMIT if count <= 1024 else VMEM_LARGE),
        cost_estimate=QUICK,
        name="attend",
    )(query_ids, key_ids, queries, key_values, key_values)


def attend_back(query_ids, key_ids, queries, key_values, lse, upward):
    streams, rows, _ = queries.shape
    count = key_values.shape[1]
    specs = attention_specs(rows, count)
    macs = streams * 2 * PAIRS * rows * count * HD
    key_shape = jax.ShapeDtypeStruct((streams, count, HALF), BF)
    return pl.pallas_call(
        backward_kernel,
        grid=(streams, PAIRS),
        in_specs=[
            specs["qid"],
            specs["kid"],
            specs["row"],
            specs["key"],
            specs["value"],
            specs["lse"],
            specs["row"],
        ],
        out_specs=[specs["row"], specs["key"], specs["key"]],
        out_shape=[jax.ShapeDtypeStruct((streams, rows, HALF), BF), key_shape, key_shape],
        compiler_params=pltpu.CompilerParams(vmem_limit_bytes=VMEM_LIMIT if count <= 1024 else VMEM_LARGE),
        cost_estimate=QUICK,
        name="attend_back",
    )(query_ids, key_ids, queries, key_values, key_values, lse, upward)


CHUNK = 1536
QUERY_BIAS, VALUE_BIAS, OUT_BIAS, FIRST_GAIN, FIRST_SHIFT, REDUCE_BIAS, SECOND_GAIN, SECOND_SHIFT = range(8)


def norm_rows(value_rows):
    centre = jnp.mean(value_rows, axis=-1, keepdims=True)
    centred = value_rows - centre
    inverse = lax.rsqrt(jnp.mean(centred * centred, axis=-1, keepdims=True) + EPSILON)
    return (centred * inverse, inverse)


def norm_back(upward, normed, inverse):
    mean_up = jnp.mean(upward, axis=-1, keepdims=True)
    mean_cross = jnp.mean(upward * normed, axis=-1, keepdims=True)
    return inverse * (upward - mean_up - normed * mean_cross)


def add_rows(sum_ref, index, values):
    sum_ref[index] += jnp.sum(values.reshape(-1, 8, values.shape[1]), axis=0)


def vector_of(vec_ref, index):
    return vec_ref[index : index + 1, :]


def half_of_ref(place_ref):
    return pl.ds(pl.multiple_of(place_ref[2] * HALF, 128), HALF)


def other_half_of_ref(place_ref):
    return pl.ds(pl.multiple_of((1 - place_ref[2]) * HALF, 128), HALF)


def project(place, mine, other, vectors, weight):
    streams, rows, _ = mine[0].shape
    zs = len(mine)
    chip_rows = 2 * rows
    count = zs * chip_rows
    tile = min(count, 1024)

    def kernel(place_ref, *refs):
        mine_refs, other_refs, (vec_ref, weight_ref) = refs[:zs], refs[zs : 2 * zs], refs[2 * zs : 2 * zs + 2]
        all_ref, pairs_ref, query_ref, rows_ref = refs[2 * zs + 2 :]
        half = half_of_ref(place_ref)
        for j in range(zs):
            here = pl.ds(pl.multiple_of(j * chip_rows + place_ref[2] * rows, rows), rows)
            there = pl.ds(pl.multiple_of(j * chip_rows + (1 - place_ref[2]) * rows, rows), rows)
            for s in range(streams):
                all_ref[s, here, :] = mine_refs[j][s]
                all_ref[s, there, :] = other_refs[j][s]

        @pl.loop(0, streams)
        def _(s):
            for start in range(0, count, tile):
                span = slice(start, start + tile)
                pairs = nn(all_ref[s, span, :], weight_ref[:, HALF:])
                pairs_ref[s, span, :HALF] = pairs[:, :HALF].astype(BF)
                values = pairs[:, HALF:] + vec_ref[VALUE_BIAS : VALUE_BIAS + 1, half]
                pairs_ref[s, span, HALF:] = values.astype(BF)
            tokens = all_ref[s, :chip_rows, :]
            rows_ref[s] = tokens
            queries = nn(tokens, weight_ref[:, :HALF]) + vec_ref[QUERY_BIAS : QUERY_BIAS + 1, half]
            query_ref[s] = (queries * 0.125).astype(BF)

    shape = lambda rows, lanes: jax.ShapeDtypeStruct((streams, rows, lanes), BF)
    return pl.pallas_call(
        kernel,
        in_specs=[pl.BlockSpec(memory_space=pltpu.SMEM)]
        + [pl.BlockSpec(memory_space=pltpu.VMEM)] * (2 * zs + 2),
        out_specs=[pl.BlockSpec(memory_space=pltpu.VMEM)] * 4,
        out_shape=[shape(count, D), shape(count, D), shape(chip_rows, HALF), shape(chip_rows, D)],
        compiler_params=pltpu.CompilerParams(
            vmem_limit_bytes=VMEM_LIMIT if count <= 1024 else VMEM_LARGE
        ),
        cost_estimate=QUICK,
        name="project",
    )(place, *mine, *other, vectors, weight)


def unproject(place, query_back, key_back, value_back, weight):
    streams, count, _ = key_back.shape
    chip_rows = query_back.shape[1]
    rows = chip_rows // 2
    zs = count // chip_rows
    tile = min(count, 1024)

    def kernel(place_ref, query_ref, key_ref, value_ref, weight_ref, mine_ref, other_ref):
        first_core = place_ref[2] == 0

        @pl.loop(0, streams)
        def _(s):
            for start in range(0, count, tile):
                span = slice(start, start + tile)
                back = jnp.concatenate([key_ref[s, span, :], value_ref[s, span, :]], axis=1)
                total = nt(back, weight_ref[:, HALF:])
                for offset in range(0, tile, chip_rows):
                    j = (start + offset) // chip_rows
                    chip = total[offset : offset + chip_rows]
                    if j == 0:
                        chip += nt(query_ref[s], weight_ref[:, :HALF])
                    mine_ref[j, s] = jnp.where(first_core, chip[:rows], chip[rows:]).astype(BF)
                    other_ref[j, s] = jnp.where(first_core, chip[rows:], chip[:rows]).astype(BF)

    shape = jax.ShapeDtypeStruct((zs, streams, rows, D), BF)
    return pl.pallas_call(
        kernel,
        in_specs=[pl.BlockSpec(memory_space=pltpu.SMEM)]
        + [pl.BlockSpec(memory_space=pltpu.VMEM)] * 4,
        out_specs=[pl.BlockSpec(memory_space=pltpu.VMEM)] * 2,
        out_shape=[shape, shape],
        compiler_params=pltpu.CompilerParams(
            vmem_limit_bytes=VMEM_LIMIT if count <= 1024 else VMEM_LARGE
        ),
        cost_estimate=QUICK,
        name="unproject",
    )(place, query_back, key_back, value_back, weight)


def middle_kernel(
    place_ref, mine_ref, other_ref, tok_ref, vec_ref, unit_ref, out_ref, expand_ref, reduce_ref,
    normed_ref, inverse_ref, low_ref, hidden_ref, slope_ref, part_ref, send_ref,
):
    branch = nn(mine_ref[...], out_ref[half_of_ref(place_ref), :])
    branch += nn(other_ref[...], out_ref[other_half_of_ref(place_ref), :])
    branch += vector_of(vec_ref, OUT_BIAS)
    normed, inverse = norm_rows(tok_ref[...].astype(F32) + branch)
    normed_ref[...] = normed
    inverse_ref[...] = jnp.broadcast_to(inverse, inverse_ref.shape)
    first = normed * vector_of(vec_ref, FIRST_GAIN) + vector_of(vec_ref, FIRST_SHIFT)
    low = first.astype(BF)
    low_ref[...] = low
    total = jnp.zeros(part_ref.shape, F32)
    for start in range(0, UNITS, CHUNK):
        span = slice(start, start + CHUNK)
        expanded = nn(low, expand_ref[:, span]) + unit_ref[:, span]
        share = 0.5 * (1.0 + lax.erf(expanded * (0.5**0.5)))
        hidden = (expanded * share).astype(BF)
        hidden_ref[:, span] = hidden
        bell = jnp.exp(-0.5 * expanded * expanded) * 0.3989422804014327
        slope_ref[:, span] = (share + expanded * bell).astype(BF)
        total += nn(hidden, reduce_ref[span, :])
    part_ref[...] = total
    send_ref[...] = total.astype(BF)


def turn_kernel(
    place_ref, part_ref, came_ref, normed_ref, mine_ref, other_ref, slope_ref, vec_ref, reduce_ref, expand_ref,
    act_ref, residual_ref, low_ref, back_ref, next_ref, send_ref, sum_ref, unit_sum_ref,
):
    core = place_ref[2]
    first = normed_ref[...] * vector_of(vec_ref, FIRST_GAIN) + vector_of(vec_ref, FIRST_SHIFT)
    reduced = part_ref[...] + came_ref[...].astype(F32) + vector_of(vec_ref, REDUCE_BIAS)
    normed, inverse = norm_rows(first + reduced)
    gain = vector_of(vec_ref, SECOND_GAIN)
    half = normed.shape[0] // 2
    mine = jnp.where(core == 0, normed[:half], normed[half:])
    act_ref[...] = (mine * gain + vector_of(vec_ref, SECOND_SHIFT)).astype(BF)
    mine, other = mine_ref[...].astype(F32), other_ref[...].astype(F32)
    upward = jnp.concatenate(
        [jnp.where(core == 0, mine, other), jnp.where(core == 0, other, mine)], axis=0
    )
    residual = norm_back(upward * gain, normed, inverse)
    low = residual.astype(BF)
    residual_ref[...] = residual
    low_ref[...] = low
    add_rows(sum_ref, 0, low.astype(F32))
    add_rows(sum_ref, 1, upward * normed)
    add_rows(sum_ref, 2, upward)
    total = jnp.zeros(next_ref.shape, F32)
    for start in range(0, UNITS, CHUNK):
        span = slice(start, start + CHUNK)
        back = (nt(low, reduce_ref[span, :]) * slope_ref[:, span].astype(F32)).astype(BF)
        back_ref[:, span] = back
        unit_sum_ref[:, span] += jnp.sum(back.astype(F32).reshape(-1, 8, CHUNK), axis=0)
        total += nt(back, expand_ref[:, span])
    next_ref[...] = total
    send_ref[...] = total.astype(BF)


def first_back_kernel(
    place_ref, part_ref, came_ref, residual_ref, normed_ref, inverse_ref, vec_ref, out_ref,
    back_ref, low_ref, attended_ref, sum_ref,
):
    upward = part_ref[...] + came_ref[...].astype(F32) + residual_ref[...]
    normed = normed_ref[...]
    add_rows(sum_ref, 1, upward * normed)
    add_rows(sum_ref, 2, upward)
    back = norm_back(upward * vector_of(vec_ref, FIRST_GAIN), normed, inverse_ref[:, :1])
    low = back.astype(BF)
    half = back.shape[0] // 2
    back_ref[...] = jnp.where(place_ref[2] == 0, back[:half], back[half:])
    low_ref[...] = low
    add_rows(sum_ref, 0, low.astype(F32))
    attended_ref[...] = nt(low, out_ref[half_of_ref(place_ref), :]).astype(BF)


def over_rows(body, place, steps, tiled, whole, outs, sums, name):
    def tile_of(ref, step):
        rows = ref.shape[0] // steps
        return ref.at[pl.ds(pl.multiple_of(step * rows, rows), rows)]

    def kernel(place_ref, *refs):
        tiles, refs = refs[: len(tiled)], refs[len(tiled) :]
        kept, refs = refs[: len(whole)], refs[len(whole) :]
        results, totals = refs[: len(outs)], refs[len(outs) :]
        for total in totals:
            total[...] = jnp.zeros_like(total)

        @pl.loop(0, steps)
        def _(step):
            body(
                place_ref,
                *[tile_of(ref, step) for ref in tiles],
                *kept,
                *[tile_of(ref, step) for ref in results],
                *totals,
            )

    return pl.pallas_call(
        kernel,
        in_specs=[pl.BlockSpec(memory_space=pltpu.SMEM)]
        + [pl.BlockSpec(memory_space=pltpu.VMEM)] * (len(tiled) + len(whole)),
        out_specs=[pl.BlockSpec(memory_space=pltpu.VMEM)] * (len(outs) + len(sums)),
        out_shape=[jax.ShapeDtypeStruct(out[:2], out[2]) for out in outs]
        + [jax.ShapeDtypeStruct(shape, F32) for shape in sums],
        compiler_params=pltpu.CompilerParams(vmem_limit_bytes=VMEM_LIMIT),
        cost_estimate=QUICK,
        name=name,
    )(place, *tiled, *whole)


def packed_call(kernel, place, sources, shapes, scratch, name):
    return pl.pallas_call(
        kernel,
        in_specs=[pl.BlockSpec(memory_space=pltpu.SMEM)]
        + [pl.BlockSpec(memory_space=pltpu.VMEM)] * len(sources),
        out_specs=[pl.BlockSpec(memory_space=pltpu.VMEM)] * len(shapes),
        out_shape=[jax.ShapeDtypeStruct(shape, BF) for shape in shapes],
        scratch_shapes=scratch,
        compiler_params=pltpu.CompilerParams(vmem_limit_bytes=VMEM_LIMIT),
        cost_estimate=QUICK,
        name=name,
    )(place, *sources)


def wide_packs_of(place, hidden, reduced_back, first_low, expanded_back, dps, zs):
    chips = dps * zs
    both, wide = D // chips, UNITS // chips
    slots, counts = scatter_slots(dps, zs)
    lanes = 2 * D + UNITS

    def kernel(place_ref, hidden_ref, reduced_ref, low_ref, expanded_ref, *refs):
        outs, (reduce_ref, expand_ref) = refs[: len(counts)], refs[len(counts) :]
        for start in range(0, UNITS, CHUNK):
            span = slice(start, start + CHUNK)
            reduce_ref[span, :] = tn(hidden_ref[:, span], reduced_ref[...]).astype(BF)
        for start in range(0, D, 256):
            span = slice(start, start + 256)
            expand_ref[span, :] = tn(low_ref[:, span], expanded_ref[...]).astype(BF)
        for (k, j), (array, row) in slots.items():
            chip = (place_ref[0] ^ k) * zs + (place_ref[1] ^ j)
            first = pl.multiple_of(chip * wide, 16)
            outs[array][row, :, :D] = reduce_ref[pl.ds(first, both), :]
            outs[array][row, :, D : 2 * D] = reduce_ref[pl.ds(pl.multiple_of(first + both, 16), both), :]
            outs[array][row, :, 2 * D :] = expand_ref[pl.ds(pl.multiple_of(chip * both, 16), both), :]

    return packed_call(
        kernel,
        place,
        [hidden, reduced_back, first_low, expanded_back],
        [(count, both, lanes) for count in counts],
        [pltpu.VMEM((UNITS, D), BF), pltpu.VMEM((D, UNITS), BF)],
        "wide_packs",
    )


def narrow_packs_of(place, tokens, chip_tokens, backs, mine, other, branch_back, sums, dps, zs):
    chips = dps * zs
    both = D // chips
    slots, counts = scatter_slots(dps, zs)
    lanes = 4 * HALF + 128
    query_back, key_back, value_back = backs

    def kernel(
        place_ref, tok_ref, chip_ref, query_ref, key_ref, value_ref, mine_ref, other_ref, branch_ref,
        one_ref, two_ref, unit_ref, *refs,
    ):
        outs, (all_ref, square_ref) = refs[: len(counts)], refs[len(counts) :]
        half = half_of_ref(place_ref)
        for start in range(0, D, 256):
            span = slice(start, start + 256)
            turned = tok_ref[:, span].T
            all_ref[span, :HALF] = tn(chip_ref[:, span], query_ref[...]).astype(BF)
            all_ref[span, HALF : 2 * HALF] = nn(turned, key_ref[...]).astype(BF)
            all_ref[span, 2 * HALF : 3 * HALF] = nn(turned, value_ref[...]).astype(BF)
        branch = branch_ref[:, half]
        all_ref[half, 3 * HALF : 4 * HALF] = tn(mine_ref[...], branch).astype(BF)
        all_ref[other_half_of_ref(place_ref), 3 * HALF : 4 * HALF] = tn(other_ref[...], branch).astype(BF)
        square_ref[...] = jnp.zeros_like(square_ref)
        for row, ref in ((0, query_ref), (1, value_ref)):
            square_ref[row : row + 1, half] = jnp.sum(ref[...].astype(F32), axis=0, keepdims=True)
        for i in range(3):
            square_ref[2 + i : 3 + i, :] = jnp.sum(one_ref[i], axis=0, keepdims=True)
            square_ref[5 + i : 6 + i, :] = jnp.sum(two_ref[i], axis=0, keepdims=True)
        unit = jnp.sum(unit_ref[...], axis=0, keepdims=True)
        for chip in range(chips):
            for h in range(2):
                first = (2 * chip + h) * both
                square_ref[8 + h : 9 + h, chip * both : (chip + 1) * both] = unit[:, first : first + both]
        all_ref[:, 4 * HALF :] = square_ref[...].T.astype(BF)
        for (k, j), (array, row) in slots.items():
            chip = (place_ref[0] ^ k) * zs + (place_ref[1] ^ j)
            outs[array][row] = all_ref[pl.ds(pl.multiple_of(chip * both, 16), both), :]

    return packed_call(
        kernel,
        place,
        [tokens, chip_tokens, query_back, key_back, value_back, mine, other, branch_back, *sums],
        [(count, both, lanes) for count in counts],
        [pltpu.VMEM((D, lanes), BF), pltpu.VMEM((128, D), F32)],
        "narrow_packs",
    )


def column_sum(value_rows):
    return jnp.sum(value_rows.astype(F32), axis=0)


def item_ids(lengths, places):
    items = lengths.shape[1]
    slot = jnp.arange(items, dtype=jnp.int32)
    ends = jnp.sum(jnp.where(slot[:, None] <= slot[None, :], lengths[:, :, None], 0), axis=1)
    return jnp.sum((ends[:, None, :] <= places[None, :, None]).astype(jnp.int32), axis=2)


def body(
    tokens,
    query_weight,
    query_bias,
    key_weight,
    value_weight,
    value_bias,
    out_weight,
    out_bias,
    first_gain,
    attention_norm_shift,
    expand_weight,
    expand_bias,
    reduce_weight,
    reduce_bias,
    second_gain,
    second_shift,
    lengths,
    cotangent,
    *,
    dps,
    seq,
):
    streams, row_count, _ = tokens.shape
    zs = seq // 2
    chips = dps * zs
    block = D // (2 * chips)
    both = 2 * block
    wide = FF // (2 * chips)
    chip_rows = 2 * row_count
    rows = streams * chip_rows
    dp = lax.axis_index("dp")
    z = lax.axis_index("seq") // 2
    core = lax.axis_index("seq") % 2
    place = jnp.stack([dp, z, core]).astype(jnp.int32)
    swap = functools.partial(core_swap, seq=seq)

    def row_major(value):
        return with_layout_constraint(value, Layout(major_to_minor=tuple(range(value.ndim))))

    def in_core_order(mine, other, axis):
        return jnp.where(
            core == 0,
            jnp.concatenate([mine, other], axis=axis),
            jnp.concatenate([other, mine], axis=axis),
        )

    mine, theirs = first_columns(
        place,
        (query_weight, key_weight, value_weight),
        (
            query_bias,
            value_bias,
            out_bias,
            first_gain,
            attention_norm_shift,
            reduce_bias,
            second_gain,
            second_shift,
            expand_bias,
        ),
    )
    early = in_core_order(mine[None], swap(theirs)[None], 0)

    out_weight = out_weight.astype(BF)
    units = expand_weight.astype(BF).reshape(block, chips, 2, wide)

    def columns_for(side):
        unit = lax.dynamic_index_in_dim(units, side, 2, keepdims=False).reshape(block, UNITS)
        return jnp.concatenate([out_weight, unit], axis=1)

    late = in_core_order(columns_for(core)[None], swap(columns_for(1 - core))[None], 0)
    parts = reduce_weight.astype(BF).reshape(2, 2, block, D)
    late = jnp.concatenate([late, parts[:, 0], parts[:, 1]], axis=2)
    other_cotangent = swap(cotangent).reshape(-1, D)
    cotangent = cotangent.reshape(-1, D)
    other_tokens = swap(tokens)
    early = jnp.stack(tied(z_moves(early, seq), late, other_tokens, other_cotangent))
    late = z_moves(tied(late, early), seq)
    early, late = lax.optimization_barrier((gather_dp_first(early, dps), late))
    early = gather_dp_rest(early, gather_dp_halves(early, dps))
    moved = z_moves(tied(tokens, late), seq)
    late = gather_dp_first(jnp.stack(tied(late, early)), dps)

    def gather_plan(parts, direct=False):
        return [
            (
                piece,
                lambda dp, z, row=row, first=first, count=count: (
                    row,
                    Ellipsis,
                    at_lanes(first, count),
                ),
                target,
                lambda dp, z, j=j, k=k: (dp ^ k, z ^ j),
            )
            for piece, row, k, j in dp_pieces(dps, zs, direct)
            for first, count, target in parts
        ]

    qkv_weight, small = local_copies(
        place,
        early,
        [(dps, zs, 2, block, 3 * HALF), (dps, zs, 2, block, 128)],
        gather_plan([(0, 3 * HALF, 0), (3 * HALF, 128, 1)]),
        "place_early",
    )
    qkv_weight = qkv_weight.reshape(D, 3 * HALF)
    small = small.astype(F32).reshape(D, 128)[:, :12].T
    expand_bias = small[8:12].reshape(4, chips, 2, block)
    expand_bias = lax.dynamic_index_in_dim(expand_bias, core, 2, keepdims=False)
    expand_bias = expand_bias.transpose(1, 0, 2).reshape(1, UNITS)

    def half_of(vector):
        return lax.dynamic_slice_in_dim(vector, core * HALF, HALF, 1)

    qkv_weight = tied(qkv_weight, expand_bias)
    halves = gather_dp_halves(tied(late, qkv_weight), dps)
    late = gather_dp_rest(late, halves)
    others = [other_tokens] + [swap(m) for m in moved[1:]]

    all_tokens, key_values, queries, chip_tokens = project(
        place, moved, others, small, qkv_weight
    )
    flat_all = all_tokens.reshape(-1, D)
    spot = jnp.arange(row_count, dtype=jnp.int32)
    steps = jnp.arange(zs, dtype=jnp.int32) ^ z
    starts = (steps[:, None] * 2 + jnp.arange(2, dtype=jnp.int32)) * row_count
    ids = item_ids(lengths, (starts[:, :, None] + spot).reshape(-1))
    key_ids = jnp.broadcast_to(ids[:, None, :], (streams, 8, ids.shape[1]))
    query_ids = jnp.broadcast_to(ids[:, :chip_rows, None], (streams, chip_rows, 128))

    chip_tokens = chip_tokens.reshape(rows, D)
    queries = tied(queries, halves)
    attended, lse = attend(query_ids, key_ids, queries, key_values)
    other_attended = swap(attended).reshape(rows, HALF)
    attended = attended.reshape(rows, HALF)

    out_weight, expand_weight, reduce_weight = local_copies(
        place,
        late,
        [(dps, zs, 2, block, D), (dps, zs, 2, block, UNITS), (dps, zs, 4, block, D)],
        gather_plan([(0, D, 0), (D, UNITS, 1)])
        + [
            (
                piece,
                lambda dp, z, row=row, c=c, h=h: (row, c, slice(None), at_lanes(D + UNITS + h * D, D)),
                2,
                lambda dp, z, j=j, k=k, c=c, h=h: (dp ^ k, z ^ j, 2 * c + h),
            )
            for piece, row, k, j in dp_pieces(dps, zs, False)
            for c in range(2)
            for h in range(2)
        ],
        "place_late",
    )
    out_weight = out_weight.reshape(D, D)
    expand_weight = expand_weight.reshape(D, UNITS)
    reduce_weight = reduce_weight.reshape(UNITS, D)

    normed_one, inverse_one, first_low, hidden, slope, partial, sent = over_rows(
        middle_kernel,
        place,
        streams,
        [attended, other_attended, chip_tokens],
        [small, expand_bias, out_weight, expand_weight, reduce_weight],
        [
            (rows, D, F32),
            (rows, 128, F32),
            (rows, D, BF),
            (rows, UNITS, BF),
            (rows, UNITS, BF),
            (rows, D, F32),
            (rows, D, BF),
        ],
        [],
        "middle",
    )
    activations, residual_two_back, reduced_back, expanded_back, partial, sent, sums_two, unit_sums = over_rows(
        turn_kernel,
        place,
        streams,
        [partial, swap(sent), normed_one, cotangent, other_cotangent, slope],
        [small, reduce_weight, expand_weight],
        [
            (rows // 2, D, BF),
            (rows, D, F32),
            (rows, D, BF),
            (rows, UNITS, BF),
            (rows, D, F32),
            (rows, D, BF),
        ],
        [(3, 8, D), (8, UNITS)],
        "turn",
    )
    came_partial = swap(sent)
    fused = both % 16 == 0

    def scatter_plan(parts, lanes):
        slots, counts = scatter_slots(dps, zs)
        plan = [
            (
                source,
                lambda dp, z, j=j, k=k, index=index: index(dp ^ k, z ^ j),
                array,
                lambda dp, z, row=row, first=first, count=count: (
                    row,
                    slice(None),
                    at_lanes(first, count),
                ),
            )
            for (k, j), (array, row) in slots.items()
            for source, index, first, count in parts
        ]
        return [(count, both, lanes) for count in counts], plan

    if fused:
        wide_packs = wide_packs_of(place, hidden, reduced_back, first_low, expanded_back, dps, zs)
    else:
        wide_packs = local_copies(
            place,
            [
                tn(hidden, reduced_back).astype(BF).reshape(dps, zs, 2, both, D),
                tn(first_low, expanded_back).astype(BF).reshape(dps, zs, both, UNITS),
            ],
            *scatter_plan(
                [
                    (0, lambda d, zz: (d, zz, 0), 0, D),
                    (0, lambda d, zz: (d, zz, 1), D, D),
                    (1, lambda d, zz: (d, zz), 2 * D, UNITS),
                ],
                2 * D + UNITS,
            ),
            "pack_wide",
        )
    wide_came = scatter_dp_first(wide_packs, dps)

    residual_one_back, branch_back, attended_back, sums_one = over_rows(
        first_back_kernel,
        place,
        streams,
        [partial, came_partial, residual_two_back, normed_one, inverse_one],
        [small, out_weight],
        [(rows // 2, D, F32), (rows, D, BF), (rows, HALF, BF)],
        [(3, 8, D)],
        "first_back",
    )
    attended_back = attended_back.reshape(streams, chip_rows, HALF)

    query_back, key_back, value_back = attend_back(
        query_ids, key_ids, queries, key_values, lse, attended_back
    )
    mine_part, other_part = unproject(place, query_back, key_back, value_back, qkv_weight)
    came_part = swap(other_part)
    wide_came = tied(wide_came, other_part)
    wide_onward = scatter_dp_middle(wide_packs, wide_came, dps)
    mine_part, came_part = tied((mine_part, came_part), wide_onward)
    tokens_total = wide_sum([mine_part, came_part])
    tokens_first = tokens_total[zs // 2 :].astype(BF)

    def halved(total, bit, sent):
        return total[:bit] + z_move(sent, bit, seq).astype(F32)

    tokens_total = halved(tokens_total, zs // 2, tokens_first)
    backs = (query_back.reshape(rows, HALF), key_back.reshape(-1, HALF), value_back.reshape(-1, HALF))
    backs = tied(backs, tokens_first)
    if fused:
        narrow_packs = narrow_packs_of(
            place,
            flat_all,
            chip_tokens,
            backs,
            attended,
            other_attended,
            branch_back,
            (sums_one, sums_two, unit_sums),
            dps,
            zs,
        )
        wide_totals = scatter_dp_rest(
            wide_packs, wide_came, wide_onward, dps, lambda came: tied(came, narrow_packs)
        )
    else:
        out_side = half_of(branch_back)
        zeros = jnp.zeros((D,), F32)
        small_grads = jnp.concatenate(
            [
                lax.dynamic_update_slice_in_dim(zeros, column_sum(backs[0]), core * HALF, 0)[None],
                lax.dynamic_update_slice_in_dim(zeros, column_sum(backs[2]), core * HALF, 0)[None],
                jnp.sum(sums_one, axis=1),
                jnp.sum(sums_two, axis=1),
                jnp.sum(unit_sums, axis=0).reshape(chips, 2, both).transpose(1, 0, 2).reshape(2, D),
            ],
            axis=0,
        ).T.astype(BF)
        small_grads = jnp.pad(small_grads, ((0, 0), (0, 128 - small_grads.shape[1])))
        four = (
            tn(chip_tokens, backs[0]).astype(BF),
            tn(flat_all, backs[1]).astype(BF),
            tn(flat_all, backs[2]).astype(BF),
            in_core_order(tn(attended, out_side), tn(other_attended, out_side), 0).astype(BF),
        )
        wide_totals = scatter_dp_rest(wide_packs, wide_came, wide_onward, dps)
        narrow_packs = local_copies(
            place,
            [g.reshape(dps, zs, both, HALF) for g in four] + [small_grads.reshape(dps, zs, both, 128)],
            *scatter_plan(
                [(i, lambda d, zz: (d, zz), i * HALF, HALF) for i in range(4)]
                + [(4, lambda d, zz: (d, zz), 4 * HALF, 128)],
                4 * HALF + 128,
            ),
            "pack_narrow",
        )
    came = tied(scatter_dp_first(narrow_packs, dps), wide_totals)
    narrow_onward = scatter_dp_middle(narrow_packs, came, dps)
    narrow_totals = scatter_dp_rest(narrow_packs, came, narrow_onward, dps)
    wide_grads = scatter_z(tied(wide_totals, tokens_total), seq)
    bit = zs // 4
    while bit:
        tokens_total = halved(tokens_total, bit, tokens_total[bit:].astype(BF))
        bit //= 2
    narrow_totals, tokens_total, wide_grads = lax.optimization_barrier(
        (narrow_totals, tokens_total, wide_grads)
    )
    narrow_grads = scatter_z(narrow_totals, seq)
    tokens_gradient = residual_one_back.reshape(tokens.shape) + tokens_total[0]

    def own_rows(grads):
        split = grads.reshape(2, block, grads.shape[1])
        mine = lax.dynamic_index_in_dim(split, core, 0, keepdims=False)
        return mine, swap(lax.dynamic_index_in_dim(split, 1 - core, 0, keepdims=False))

    mine, other = own_rows(wide_grads[:, 2 * D :])
    expand_grads = in_core_order(
        mine.reshape(block, chips, 1, wide), other.reshape(block, chips, 1, wide), 2
    ).reshape(block, FF)
    reduce_grads = jnp.concatenate([wide_grads[:, :D], wide_grads[:, D : 2 * D]], axis=0)
    mine, other = own_rows(narrow_grads)
    matrices = [
        in_core_order(mine[:, i * HALF : (i + 1) * HALF], other[:, i * HALF : (i + 1) * HALF], 1)
        for i in range(4)
    ]
    own_small = mine[:, 4 * HALF :].T
    both_small = (mine[:, 4 * HALF : 4 * HALF + 2] + other[:, 4 * HALF : 4 * HALF + 2]).T
    expand_bias_grad = narrow_grads[:, 4 * HALF :][:, 8:10].T.reshape(wide)

    return (
        activations.reshape(tokens.shape),
        tokens_gradient,
        matrices[0],
        both_small[0],
        matrices[1],
        matrices[2],
        both_small[1],
        matrices[3],
        own_small[2],
        own_small[3],
        own_small[4],
        expand_grads,
        expand_bias_grad,
        reduce_grads,
        own_small[5],
        own_small[6],
        own_small[7],
    )


def solution(mesh):
    sharded = ("dp", "seq")
    matrix = P(sharded, None)
    vector = P(sharded)
    token = P("dp", "seq", None)
    params = (
        matrix,
        vector,
        matrix,
        matrix,
        vector,
        matrix,
        vector,
        vector,
        vector,
        matrix,
        vector,
        matrix,
        vector,
        vector,
        vector,
    )
    return jax.shard_map(
        functools.partial(body, dps=mesh.shape["dp"], seq=mesh.shape["seq"]),
        mesh=mesh,
        in_specs=(token,) + params + (P("dp", None), token),
        out_specs=(token, token) + params,
        check_vma=False,
    )
```
